32 devices in a mesh: mod: 2 (over y), dp: 16 (over z, x, core).
Axes of the slice: x: 2, y: 2, z: 4, core: 2. Of those that a mesh axis runs over, the one named last changes fastest.
Arguments:
- patch_tokens: bfloat16 [2, 32, 256, 768], P('mod', 'dp'), may hold values from -6 to 6
- grid_coords: int32 [32, 2, 256], P('dp'), may hold values from 0 to 15, as said below
- has_radar: int32 [32], P('dp'), may hold values 0 or 1
- enc_gains: float32 [2, 2, 768], P('mod'), may hold values from 0.1 to 1.9
- enc_project: bfloat16 [2, 768, 2304], P('mod'), may hold values from -0.21875 to 0.21875
- enc_mixer: bfloat16 [2, 768, 768], P('mod'), may hold values from -0.625 to 0.625
- enc_expand: bfloat16 [2, 768, 3072], P('mod'), may hold values from -0.21875 to 0.21875
- enc_reduce: bfloat16 [2, 3072, 768], P('mod'), may hold values from -0.109375 to 0.109375
- cross_norms: float32 [2, 768], replicated, may hold values from 0.1 to 1.9
- cross_gain: float32 [768], replicated, may hold values from 0.1 to 1.9
- cross_query: bfloat16 [768, 768], P(None, 'mod'), may hold values from -0.21875 to 0.21875
- cross_keyval: bfloat16 [2, 768, 768], P(None, None, 'mod'), may hold values from -0.21875 to 0.21875
- cross_mixer: bfloat16 [768, 768], P('mod'), may hold values from -0.625 to 0.625
- cross_expand: bfloat16 [768, 3072], P(None, 'mod'), may hold values from -0.21875 to 0.21875
- cross_reduce: bfloat16 [3072, 768], P('mod'), may hold values from -0.109375 to 0.109375
- enc_cotangent: bfloat16 [2, 32, 256, 768], P('mod', 'dp'), may hold values from -8 to 8
- joined_cotangent: bfloat16 [32, 256, 768], P('dp'), may hold values from -8 to 8
Outputs:
- encoded: bfloat16 [2, 32, 256, 768], P('mod', 'dp')
- joined_tokens: bfloat16 [32, 256, 768], P('dp')
- contrast_loss: float32 [], replicated
- patch_grad: float32 [2, 32, 256, 768], P('mod', 'dp')
- enc_gains_grad: float32 [2, 2, 768], P('mod', None, 'dp')
- enc_project_grad: float32 [2, 768, 2304], P('mod', 'dp')
- enc_mixer_grad: float32 [2, 768, 768], P('mod', 'dp')
- enc_expand_grad: float32 [2, 768, 3072], P('mod', 'dp')
- enc_reduce_grad: float32 [2, 3072, 768], P('mod', None, 'dp')
- cross_norms_grad: float32 [2, 768], P('mod', 'dp')
- cross_gain_grad: float32 [768], P('dp')
- cross_query_grad: float32 [768, 768], P('dp', 'mod')
- cross_keyval_grad: float32 [2, 768, 768], P(None, 'dp', 'mod')
- cross_mixer_grad: float32 [768, 768], P('mod', 'dp')
- cross_expand_grad: float32 [768, 3072], P('dp', 'mod')
- cross_reduce_grad: float32 [3072, 768], P('mod', 'dp')
The draws below stay inside these ranges and needn't reach their ends.
Inputs may be any that keep to these rules, and one draw needn't show every extreme that they name: For each image, grid_coords[i, 0, j] and grid_coords[i, 1, j] are the grid row and column of patch j; each of the 16 x 16 cells appears exactly once per image.
All inputs are finite; a program needn't handle non-finite values. No bound on the sum of `has_radar` on one device may be relied on, other than what follows from the above.
Results may differ from the reference program's by a relative error of at most 0.025.
Values may be sent and summed in bfloat16 or wider, within the bound.
A program may use at most 192 MiB of HBM per device.

```python
import jax
import jax.numpy as jnp
from jax import lax

HEADS = 12
HEAD_DIM = 64
D = 768
FF = 3072
GRID = 16
P_SIZE = 256
ITEMS_DEV = 2
ITEMS_TOT = 32
N_DP = 16


def draw_grid_coords(key, part):
    key = jax.random.fold_in(key, 7)
    item_keys = jax.random.split(key, ITEMS_TOT)
    shuffled = jax.vmap(lambda member: jax.random.permutation(member, P_SIZE))(item_keys)
    return jnp.stack([shuffled // GRID, shuffled % GRID], axis=1).astype(jnp.int32)


def with_ends(values, key, smallest, top_value):
    extent = values.shape
    place = [jax.random.randint(jax.random.fold_in(key, axis), (), 0, extent[axis]) for axis in range(len(extent))]
    values = values.at[tuple(place)].set(smallest)
    longest = extent.index(max(extent))
    place[longest] = (place[longest] + 1) % extent[longest]
    return values.at[tuple(place)].set(top_value)


def spiked(entries, own_key, source, target, parts, factor):
    def block_of(axis_at):
        return (jnp.arange(entries.shape[axis_at]) // (entries.shape[axis_at] // parts)).reshape((-1,) + (1,) * (entries.ndim - 1 - axis_at))

    first = jax.random.permutation(own_key, parts)[block_of(target)]
    other_side = (block_of(target) + parts // 2) % parts
    return jnp.where((block_of(source) == first) | (block_of(source) == other_side), factor * entries, entries)


def steps_of(key, extent, cuts, smallest, high):
    loudness, own = 1.0, jax.random.fold_in(key, 6)
    for dim, parts in cuts:
        draws = jnp.exp(jax.random.uniform(jax.random.fold_in(own, dim), (parts,), jnp.float32, smallest / len(cuts), high / len(cuts)))
        loudness = loudness * jnp.repeat(draws, extent[dim] // parts).reshape([-1 if axis == dim else 1 for axis in range(len(extent))])
    return loudness


def bell_draw(own_key, extent, spread, reach, cuts=(), dtype=jnp.bfloat16):
    values = spread * jax.random.normal(own_key, extent, jnp.float32)
    if cuts:
        values = values * steps_of(own_key, extent, cuts, -0.22, 0.18)
    return jnp.clip(values, -reach, reach).astype(dtype)


def noise_with(rng, extent, deviation, reach, cuts, heavy, kind=jnp.bfloat16):
    result = deviation * jax.random.normal(rng, extent, jnp.float32)
    if cuts:
        result = result * steps_of(rng, extent, cuts, -0.22, 0.18)
    return jnp.clip(spiked(result, jax.random.fold_in(rng, 3), *heavy), -reach, reach).astype(kind)


def setup_inputs(seed: int = 0) -> dict:
    arg_keys = jax.random.split(jax.random.key(seed), 18)
    return {
        "patch_tokens": bell_draw(arg_keys[0], (2, ITEMS_TOT, P_SIZE, D), 1.0, 6.0, ((0, 2), (1, 16))),
        "grid_coords": draw_grid_coords(jax.random.fold_in(arg_keys[17], 71), 0),
        "has_radar": with_ends((jax.random.randint(arg_keys[2], (ITEMS_TOT,), 0, 4) < 3).astype(jnp.int32), jax.random.fold_in(arg_keys[2], 1), 0, 1),
        "enc_gains": jnp.clip(1.0 + 0.18 * jax.random.normal(arg_keys[3], (2, 2, D), jnp.float32), 0.1, 1.9),
        "enc_project": bell_draw(arg_keys[4], (2, D, 3 * D), D ** -0.5, 0.21875, ((0, 2),)),
        "enc_mixer": bell_draw(arg_keys[5], (2, D, D), (D // 8) ** -0.5, 0.625, ((0, 2),)),
        "enc_expand": bell_draw(arg_keys[6], (2, D, FF), D ** -0.5, 0.21875, ((0, 2),)),
        "enc_reduce": bell_draw(arg_keys[7], (2, FF, D), FF ** -0.5, 0.109375, ((0, 2),)),
        "cross_norms": jnp.clip(1.0 + 0.18 * jax.random.normal(arg_keys[8], (2, D), jnp.float32), 0.1, 1.9),
        "cross_gain": jnp.clip(1.0 + 0.18 * jax.random.normal(arg_keys[9], (D,), jnp.float32), 0.1, 1.9),
        "cross_query": bell_draw(arg_keys[10], (D, D), D ** -0.5, 0.21875, ((1, 2),)),
        "cross_keyval": bell_draw(arg_keys[11], (2, D, D), D ** -0.5, 0.21875, ((2, 2),)),
        "cross_mixer": bell_draw(arg_keys[12], (D, D), (D // 8) ** -0.5, 0.625, ((0, 2),)),
        "cross_expand": bell_draw(arg_keys[13], (D, FF), D ** -0.5, 0.21875, ((1, 2),)),
        "cross_reduce": bell_draw(arg_keys[14], (FF, D), FF ** -0.5, 0.109375, ((0, 2),)),
        "enc_cotangent": noise_with(arg_keys[15], (2, ITEMS_TOT, P_SIZE, D), 1.0, 8.0, ((0, 2), (1, 16)), (1, 3, 16, 2.0)),
        "joined_cotangent": noise_with(arg_keys[16], (ITEMS_TOT, P_SIZE, D), 1.0, 8.0, ((0, 16),), (0, 2, 16, 2.0)),
    }


@jax.custom_vjp
def low(v):
    return lax.optimization_barrier(v.astype(jnp.bfloat16)).astype(jnp.float32)

@jax.custom_vjp
def low_back(v):
    return v

def low_keep(v):
    return (low(v), None)

def low_pass(kept, grad):
    return (grad,)

def back_keep(v):
    return (v, None)

def back_low(kept, grad):
    return (low(grad),)
low.defvjp(low_keep, low_pass)
low_back.defvjp(back_keep, back_low)
logit_scale = 50.0
highest_precision = lax.Precision.HIGHEST

def product(left_side, right_side):
    return jnp.matmul(left_side, right_side, precision=highest_precision)

def layer_norm(values, gain):
    centre = values - lax.optimization_barrier(jnp.mean(values, axis=-1, keepdims=True))
    return centre * lax.rsqrt(lax.optimization_barrier(jnp.mean(centre * centre, axis=-1, keepdims=True)) + 1e-06) * gain

def distances(grid_coords):
    grid_rows = grid_coords[:, 0, :].astype(jnp.float32)
    grid_columns = grid_coords[:, 1, :].astype(jnp.float32)
    across = grid_rows[:, :, None] - grid_rows[:, None, :]
    upward = grid_columns[:, :, None] - grid_columns[:, None, :]
    return jnp.sqrt(across * across + upward * upward)

def head_slopes(first_head, head_total):
    return jnp.exp2(-8.0 * (first_head + jnp.arange(head_total) + 1).astype(jnp.float32) / HEADS)

def attend(query_rows, key_rows, value_rows, bias):
    item_count = query_rows.shape[0]
    head_count = bias.shape[1]
    head_shape = (item_count, P_SIZE, head_count, HEAD_DIM)
    scores = jnp.einsum('nqhd,nkhd->nhqk', query_rows.reshape(head_shape), key_rows.reshape(head_shape), precision=highest_precision)
    scores = low_back(scores * HEAD_DIM ** (-0.5) + bias)
    probabilities = low(jax.nn.softmax(scores, axis=-1))
    mixed_heads = jnp.einsum('nhqk,nkhd->nqhd', probabilities, value_rows.reshape(head_shape), precision=highest_precision)
    return low(low_back(mixed_heads.reshape(item_count, P_SIZE, head_count * HEAD_DIM)))

def encode(tokens, gain_pair, project_weight, mixer_weight, expand_weight, reduce_weight, bias):
    normed = low(layer_norm(tokens, gain_pair[0]))
    project = low(low_back(product(normed, project_weight)))
    mixed_heads = attend(project[..., :D], project[..., D:2 * D], project[..., 2 * D:], bias)
    residual = tokens + low_back(product(mixed_heads, mixer_weight))
    normed_two = low(layer_norm(residual, gain_pair[1]))
    hidden = low(jax.nn.gelu(low_back(product(normed_two, expand_weight))))
    return low(residual + low_back(product(hidden, reduce_weight)))

def joining(optical, radar_tokens, norm_gains, mlp_gain, query_weight, keyval_weight, mixer_weight, expand_weight, reduce_weight, bias):
    query_in = low(layer_norm(radar_tokens, norm_gains[1]))
    keyval_in = low(layer_norm(optical, norm_gains[0]))
    query_rows = low(low_back(product(query_in, query_weight)))
    key_rows = low(low_back(product(keyval_in, keyval_weight[0])))
    value_rows = low(low_back(product(keyval_in, keyval_weight[1])))
    mixed_heads = attend(query_rows, key_rows, value_rows, bias)
    residual = radar_tokens + low_back(product(mixed_heads, mixer_weight))
    normed = low(layer_norm(residual, mlp_gain))
    hidden = low(jax.nn.gelu(low_back(product(normed, expand_weight))))
    return residual + low_back(product(hidden, reduce_weight))

def contrast(pooled, present):
    unit_rows = pooled * lax.rsqrt(lax.optimization_barrier(jnp.mean(pooled * pooled, axis=-1, keepdims=True)) + 1e-06)
    logits = product(unit_rows[0], unit_rows[1].T) * (logit_scale / D)
    absent = 10000.0 * (1.0 - present)
    row_total = jax.nn.logsumexp(logits - absent[None, :], axis=1)
    column_total = jax.nn.logsumexp(logits - absent[:, None], axis=0)
    return jnp.sum(present * (row_total + column_total - 2.0 * jnp.diagonal(logits))) / (2.0 * ITEMS_TOT)

def layer_group(params, tokens, distance, present):
    enc_gains, enc_project, enc_mixer, enc_expand, enc_reduce, cross_norms, cross_gain, cross_query, cross_keyval, cross_mixer, cross_expand, cross_reduce = params
    bias = -head_slopes(0, HEADS)[None, :, None, None] * distance[:, None]
    optical = encode(tokens[0], enc_gains[0], enc_project[0], enc_mixer[0], enc_expand[0], enc_reduce[0], bias)
    radar_tokens = encode(tokens[1], enc_gains[1], enc_project[1], enc_mixer[1], enc_expand[1], enc_reduce[1], bias)
    joined_tokens = present[:, None, None] * joining(optical, radar_tokens, cross_norms, cross_gain, cross_query, cross_keyval, cross_mixer, cross_expand, cross_reduce, bias)
    encoded = jnp.stack([optical, radar_tokens])
    return (encoded, joined_tokens, lax.optimization_barrier(jnp.mean(encoded, axis=2)))

def reference(patch_tokens, grid_coords, has_radar, enc_gains, enc_project, enc_mixer, enc_expand, enc_reduce, cross_norms, cross_gain, cross_query, cross_keyval, cross_mixer, cross_expand, cross_reduce, enc_cotangent, joined_cotangent):
    present = has_radar.astype(jnp.float32)
    distance = distances(grid_coords).reshape(N_DP, ITEMS_DEV, P_SIZE, P_SIZE)
    present_groups = present.reshape(N_DP, ITEMS_DEV)
    params = tuple((weight.astype(jnp.float32) for weight in (enc_gains, enc_project, enc_mixer, enc_expand, enc_reduce, cross_norms, cross_gain, cross_query, cross_keyval, cross_mixer, cross_expand, cross_reduce)))
    checked = jax.checkpoint(layer_group)

    def forward(tokens, weights):
        groups = jnp.transpose(tokens.reshape(2, N_DP, ITEMS_DEV, P_SIZE, D), (1, 0, 2, 3, 4))
        encoded, joined_tokens, pooled = lax.map(lambda member: checked(weights, member[0], member[1], member[2]), (groups, distance, present_groups))
        encoded = jnp.transpose(encoded, (1, 0, 2, 3, 4)).reshape(2, ITEMS_TOT, P_SIZE, D)
        pooled = jnp.transpose(pooled, (1, 0, 2, 3)).reshape(2, ITEMS_TOT, D)
        return (encoded, joined_tokens.reshape(ITEMS_TOT, P_SIZE, D), contrast(pooled, present))
    outputs, pullback = jax.vjp(forward, patch_tokens.astype(jnp.float32), params)
    encoded, joined_tokens, loss_value = outputs
    token_grad, grads = pullback((enc_cotangent.astype(jnp.float32), joined_cotangent.astype(jnp.float32), jnp.ones_like(loss_value)))
    return (encoded.astype(jnp.bfloat16), joined_tokens.astype(jnp.bfloat16), loss_value, token_grad, grads[0], grads[1], grads[2], grads[3], grads[4], grads[5], grads[6], grads[7], grads[8], grads[9], grads[10], grads[11])
```

```python
import jax
import jax.numpy as jnp
from jax import lax
from jax.sharding import PartitionSpec as P

HEADS = 12
HEAD_DIM = 64
LOGIT_SCALE = 50.0
F32 = jnp.float32
BF16 = jnp.bfloat16


def norm_forward(values, gain):
    centre = values - jnp.mean(values, axis=-1, keepdims=True)
    inverse = lax.rsqrt(jnp.mean(centre * centre, axis=-1, keepdims=True) + 1e-06)
    unit_rows = centre * inverse
    return (unit_rows * gain, unit_rows, inverse)


def norm_backward(grad_out, unit_rows, inverse, gain):
    weighted = grad_out * gain
    return inverse * (
        weighted
        - jnp.mean(weighted, axis=-1, keepdims=True)
        - unit_rows * jnp.mean(weighted * unit_rows, axis=-1, keepdims=True)
    )


def matmul(left_side, right_side):
    return jnp.einsum("npd,de->npe", left_side, right_side, preferred_element_type=F32)


def matmul_back(left_side, right_side):
    return jnp.einsum("npe,de->npd", left_side, right_side, preferred_element_type=F32)


def gelu_grad(pre_act, upstream):
    return jax.vjp(jax.nn.gelu, pre_act)[1](upstream)[0]


def slopes_for(first_head, head_total):
    return jnp.exp2(-8.0 * (first_head + jnp.arange(head_total) + 1).astype(F32) / HEADS)


def split_heads(values, head_count):
    return values.reshape(values.shape[0], values.shape[1], head_count, HEAD_DIM)


def attend_forward(query_rows, key_rows, value_rows, bias):
    head_count = bias.shape[1]
    scores = (
        jnp.einsum(
            "nqhd,nkhd->nhqk",
            split_heads(query_rows, head_count),
            split_heads(key_rows, head_count),
            preferred_element_type=F32,
        )
        * HEAD_DIM ** (-0.5)
        + bias
    )
    highest = jnp.max(scores, axis=-1, keepdims=True)
    shifted = jnp.exp(scores - highest)
    denominator = jnp.sum(shifted, axis=-1, keepdims=True)
    probabilities = (shifted / denominator).astype(BF16)
    mixed_heads = jnp.einsum(
        "nhqk,nkhd->nqhd", probabilities, split_heads(value_rows, head_count), preferred_element_type=F32
    )
    return (mixed_heads.reshape(query_rows.shape).astype(BF16), probabilities)


def attend_backward(query_rows, key_rows, value_rows, probabilities, grad_mixed):
    head_count = probabilities.shape[1]
    query_heads = split_heads(query_rows, head_count)
    key_heads = split_heads(key_rows, head_count)
    value_heads = split_heads(value_rows, head_count)
    grad_heads = split_heads(grad_mixed, head_count)
    scale_factor = HEAD_DIM ** (-0.5)
    grad_probs = jnp.einsum("nqhd,nkhd->nhqk", grad_heads, value_heads, preferred_element_type=F32)
    grad_values = jnp.einsum("nhqk,nqhd->nkhd", probabilities, grad_heads, preferred_element_type=F32)
    wide = probabilities.astype(F32)
    inner_sum = jnp.sum(grad_probs * wide, axis=-1, keepdims=True)
    grad_scores = (wide * (grad_probs - inner_sum)).astype(BF16)
    grad_queries = jnp.einsum("nhqk,nkhd->nqhd", grad_scores, key_heads, preferred_element_type=F32)
    grad_keys = jnp.einsum("nhqk,nqhd->nkhd", grad_scores, query_heads, preferred_element_type=F32)
    row_shape = query_rows.shape
    return (
        (grad_queries * scale_factor).reshape(row_shape).astype(BF16),
        (grad_keys * scale_factor).reshape(row_shape).astype(BF16),
        grad_values.reshape(row_shape).astype(BF16),
    )


def contrast(pooled, present):
    total = pooled.shape[1]
    inverse = lax.rsqrt(jnp.mean(pooled * pooled, axis=-1, keepdims=True) + 1e-06)
    unit = pooled * inverse
    scale = LOGIT_SCALE / pooled.shape[2]
    logits = jnp.dot(unit[0], unit[1].T, precision=lax.Precision.HIGHEST) * scale
    absent = 10000.0 * (1.0 - present)
    by_row = logits - absent[None, :]
    by_column = logits - absent[:, None]
    row_total = jax.nn.logsumexp(by_row, axis=1, keepdims=True)
    column_total = jax.nn.logsumexp(by_column, axis=0, keepdims=True)
    same = jnp.eye(total, dtype=F32)
    diagonal = jnp.sum(logits * same, axis=1)
    loss = jnp.sum(present * (row_total[:, 0] + column_total[0] - 2.0 * diagonal)) / (2.0 * total)
    grad_logits = (
        present[:, None] * jnp.exp(by_row - row_total)
        + present[None, :] * jnp.exp(by_column - column_total)
        - 2.0 * same * present[:, None]
    ) * (scale / (2.0 * total))
    grad_unit = jnp.stack(
        [
            jnp.dot(grad_logits, unit[1], precision=lax.Precision.HIGHEST),
            jnp.dot(grad_logits.T, unit[0], precision=lax.Precision.HIGHEST),
        ]
    )
    return loss, inverse * (grad_unit - unit * jnp.mean(grad_unit * unit, axis=-1, keepdims=True))


def flipped(array, axis, bit):
    return lax.ppermute(array, axis, [(i, i ^ (1 << bit)) for i in range(lax.axis_size(axis))])


def other_half(weight, quarter):
    rows = weight.shape[0] // 4
    mine = flipped(lax.dynamic_slice_in_dim(weight, quarter * rows, rows, 0), "mod", 0)
    beside = flipped(mine, "dp", 1)
    odd = quarter >= 2
    pair = jnp.stack([jnp.where(odd, beside, mine), jnp.where(odd, mine, beside)])
    swapped = flipped(pair, "dp", 0)
    odd = quarter % 2 == 1
    whole = jnp.stack([jnp.where(odd, swapped, pair), jnp.where(odd, pair, swapped)], axis=1)
    return whole.reshape(weight.shape)


def block_order(width, count):
    bits = count.bit_length() - 1
    block = width // count
    rows = jnp.arange(width)
    place = rows // block
    partner = jnp.zeros_like(place)
    for bit in range(bits):
        partner = partner | (((place >> (bits - 1 - bit)) & 1) << bit)
    source = (lax.axis_index("dp") ^ partner) * block + rows % block
    return (source[:, None] == jnp.arange(width)[None, :]).astype(BF16)


def ordered(order, values):
    flat = values.reshape(-1, values.shape[-1])
    return jnp.einsum("jd,rd->jr", order, flat, preferred_element_type=F32).astype(BF16)


def summed(left_rows, grad_rows):
    count = lax.axis_size("dp")
    flat = grad_rows.reshape(-1, grad_rows.shape[-1])
    half = left_rows.shape[0] // 2
    send = jnp.dot(left_rows[half:], flat, preferred_element_type=F32).astype(BF16)
    keep = jnp.dot(left_rows[:half], flat, preferred_element_type=F32).astype(BF16)
    bits = count.bit_length() - 1
    for bit in range(bits):
        got = flipped(send, "dp", bit)
        if bit == bits - 1:
            return keep.astype(F32) + got.astype(F32)
        half = half // 2
        send = (keep[half:].astype(F32) + got[half:].astype(F32)).astype(BF16)
        keep = (keep[:half].astype(F32) + got[:half].astype(F32)).astype(BF16)


def summed_blocks(blocks):
    bits = lax.axis_size("dp").bit_length() - 1
    for bit in range(bits):
        half = blocks.shape[0] // 2
        blocks = blocks[:half] + flipped(blocks[half:], "dp", bit)
    return blocks[0]


def shards(
    patch_tokens,
    grid_coords,
    has_radar,
    enc_gains,
    enc_project,
    enc_mixer,
    enc_expand,
    enc_reduce,
    cross_norms,
    cross_gain,
    cross_query,
    cross_keyval,
    cross_mixer,
    cross_expand,
    cross_reduce,
    enc_cotangent,
    joined_cotangent,
):
    item_count, patches, model_width = patch_tokens.shape[1:]
    half_index = lax.axis_index("mod")
    dp_index = lax.axis_index("dp")
    dp_size = lax.axis_size("dp")
    is_radar = half_index == 1
    quarter = dp_index & 3
    quarter = (quarter >> 1) * 2 + (quarter & 1)
    local_heads = cross_query.shape[1] // HEAD_DIM

    qkv_own = jnp.concatenate([cross_query, cross_keyval[0], cross_keyval[1]], axis=1)
    qkv_other = other_half(qkv_own, quarter)
    mixer_other = other_half(cross_mixer, quarter)
    expand_other = other_half(cross_expand, quarter)
    reduce_other = other_half(cross_reduce, quarter)
    order = block_order(model_width, dp_size)

    grid_rows = grid_coords[:, 0, :].astype(F32)
    grid_columns = grid_coords[:, 1, :].astype(F32)
    across = grid_rows[:, :, None] - grid_rows[:, None, :]
    upward = grid_columns[:, :, None] - grid_columns[:, None, :]
    distance = jnp.sqrt(across * across + upward * upward)

    def bias_of(first, count):
        return -slopes_for(first, count)[None, :, None, None] * distance[:, None]

    tokens = patch_tokens[0].astype(F32)
    gain_pair = enc_gains[0]
    normed, unit_one, inverse_one = norm_forward(tokens, gain_pair[0])
    normed = normed.astype(BF16)
    project = matmul(normed, enc_project[0]).astype(BF16)
    query_rows = project[..., :model_width]
    key_rows = project[..., model_width : 2 * model_width]
    value_rows = project[..., 2 * model_width :]
    mixed_heads, probs = attend_forward(query_rows, key_rows, value_rows, bias_of(0, HEADS))
    residual = tokens + matmul(mixed_heads, enc_mixer[0])
    normed_two, unit_two, inverse_two = norm_forward(residual, gain_pair[1])
    normed_two = normed_two.astype(BF16)
    expanded = matmul(normed_two, enc_expand[0])
    hidden = jax.nn.gelu(expanded).astype(BF16)
    encoded = (residual + matmul(hidden, enc_reduce[0])).astype(BF16)
    partner = flipped(encoded, "mod", 0)

    present_row = jnp.broadcast_to(has_radar.astype(F32)[:, None], (item_count, 128))
    pooled_own = jnp.concatenate([jnp.mean(encoded.astype(F32), axis=1), present_row], axis=1)
    gathered = lax.all_gather(pooled_own, ("mod", "dp"), axis=0, tiled=True)
    total_items = gathered.shape[0] // 2
    gathered = gathered.reshape(2, total_items, model_width + 128)
    loss_value, pool_grad = contrast(gathered[:, :, :model_width], gathered[0, :, model_width])
    own_pool_grad = lax.dynamic_slice(
        pool_grad, (half_index, dp_index * item_count, 0), (1, item_count, model_width)
    )[0]

    radar_tokens = jnp.where(is_radar, encoded, partner).astype(F32)
    optical = jnp.where(is_radar, partner, encoded).astype(F32)
    query_in, unit_query, inverse_query = norm_forward(radar_tokens, cross_norms[1])
    keyval_in, unit_keyval, inverse_keyval = norm_forward(optical, cross_norms[0])
    query_in = query_in.astype(BF16)
    keyval_in = keyval_in.astype(BF16)
    width = local_heads * HEAD_DIM
    parts = []
    for qkv, mixer, first in (
        (qkv_own, cross_mixer, half_index * local_heads),
        (qkv_other, mixer_other, (1 - half_index) * local_heads),
    ):
        queries = matmul(query_in, qkv[:, :width]).astype(BF16)
        keyvals = matmul(keyval_in, qkv[:, width:]).astype(BF16)
        keys, values = keyvals[..., :width], keyvals[..., width:]
        mixed, cross_probs = attend_forward(queries, keys, values, bias_of(first, local_heads))
        parts.append((qkv, mixer, queries, keys, values, mixed, cross_probs))
    cross_resid = radar_tokens + matmul(parts[0][5], cross_mixer) + matmul(parts[1][5], mixer_other)
    cross_normed, unit_cross, inverse_cross = norm_forward(cross_resid, cross_gain)
    cross_normed = cross_normed.astype(BF16)
    wide_own = matmul(cross_normed, cross_expand)
    wide_other = matmul(cross_normed, expand_other)
    hidden_own = jax.nn.gelu(wide_own).astype(BF16)
    hidden_other = jax.nn.gelu(wide_other).astype(BF16)
    present = has_radar.astype(F32)[:, None, None]

    def own_image(values):
        return lax.dynamic_slice_in_dim(values, half_index, 1, 0)

    joined_mine = own_image(present) * (
        own_image(cross_resid)
        + matmul(own_image(hidden_own), cross_reduce)
        + matmul(own_image(hidden_other), reduce_other)
    )
    joined_mine = joined_mine.astype(BF16)
    joined_theirs = flipped(joined_mine, "mod", 0)
    joined_tokens = jnp.concatenate(
        [jnp.where(is_radar, joined_theirs, joined_mine), jnp.where(is_radar, joined_mine, joined_theirs)]
    )

    grad_joined = present * joined_cotangent.astype(F32)
    grad_branch = grad_joined.astype(BF16)
    creduce_sum = summed(ordered(order, grad_branch), hidden_own)
    gexp_own = gelu_grad(wide_own, matmul_back(grad_branch, cross_reduce)).astype(BF16)
    gexp_other = gelu_grad(wide_other, matmul_back(grad_branch, reduce_other)).astype(BF16)
    cexpand_sum = summed(ordered(order, cross_normed), gexp_own)
    grad_cnormed = matmul_back(gexp_own, cross_expand) + matmul_back(gexp_other, expand_other)
    gain_grad = jnp.sum(own_image(grad_cnormed * unit_cross), axis=(0, 1))
    grad_cresid = grad_joined + norm_backward(grad_cnormed, unit_cross, inverse_cross, cross_gain)
    grad_attention = grad_cresid.astype(BF16)
    cmixer_sum = summed(ordered(order, grad_attention), parts[0][5])
    grad_q, grad_kv = [], []
    for qkv, mixer, queries, keys, values, mixed, cross_probs in parts:
        grad_cmixed = matmul_back(grad_attention, mixer).astype(BF16)
        gq, gk, gv = attend_backward(queries, keys, values, cross_probs, grad_cmixed)
        grad_q.append(gq)
        grad_kv.append(jnp.concatenate([gk, gv], axis=-1))
    query_sum = summed(ordered(order, query_in), grad_q[0])
    keyval_sum = summed(ordered(order, keyval_in), grad_kv[0])
    grad_query_in = matmul_back(grad_q[0], qkv_own[:, :width]) + matmul_back(grad_q[1], qkv_other[:, :width])
    grad_keyval_in = matmul_back(grad_kv[0], qkv_own[:, width:]) + matmul_back(grad_kv[1], qkv_other[:, width:])
    own_norm_in = jnp.where(is_radar, grad_query_in, grad_keyval_in)
    own_unit = jnp.where(is_radar, unit_query, unit_keyval)
    own_inverse = jnp.where(is_radar, inverse_query, inverse_keyval)
    own_gain = jnp.where(is_radar, cross_norms[1], cross_norms[0])
    norms_grad = jnp.sum(own_norm_in * own_unit, axis=(0, 1))
    grad_own_norm = norm_backward(own_norm_in, own_unit, own_inverse, own_gain)
    grad_out = (
        enc_cotangent[0].astype(F32)
        + own_pool_grad[:, None, :] / patches
        + grad_own_norm
        + jnp.where(is_radar, grad_cresid, 0.0)
    )

    grad_narrow = grad_out.astype(BF16)
    reduce_sum = summed(ordered(order, grad_narrow), hidden)
    grad_hidden = matmul_back(grad_narrow, enc_reduce[0])
    grad_expanded = gelu_grad(expanded, grad_hidden).astype(BF16)
    expand_sum = summed(ordered(order, normed_two), grad_expanded)
    grad_normed_two = matmul_back(grad_expanded, enc_expand[0])
    gain_two = jnp.sum(grad_normed_two * unit_two, axis=(0, 1))
    grad_resid = grad_out + norm_backward(grad_normed_two, unit_two, inverse_two, gain_pair[1])
    grad_mixer_out = grad_resid.astype(BF16)
    mixer_sum = summed(ordered(order, mixed_heads), grad_mixer_out)
    grad_mixed = matmul_back(grad_mixer_out, enc_mixer[0]).astype(BF16)
    grad_project = jnp.concatenate(
        attend_backward(query_rows, key_rows, value_rows, probs, grad_mixed), axis=-1
    )
    project_sum = summed(ordered(order, normed), grad_project)
    grad_normed = matmul_back(grad_project, enc_project[0])
    gain_one = jnp.sum(grad_normed * unit_one, axis=(0, 1))
    patch_grad = grad_resid + norm_backward(grad_normed, unit_one, inverse_one, gain_pair[0])

    vectors = jnp.stack([gain_one, gain_two, norms_grad, gain_grad])
    placed = jnp.dot(vectors, order.astype(F32).T, precision=lax.Precision.HIGHEST)
    block = model_width // dp_size
    vector_sum = summed_blocks(jnp.moveaxis(placed.reshape(4, dp_size, block), 1, 0))
    gain_sum = vector_sum[3] + flipped(vector_sum[3], "mod", 0)
    return (
        encoded[None],
        joined_tokens,
        loss_value,
        patch_grad[None],
        vector_sum[None, :2],
        project_sum[None],
        mixer_sum[None],
        expand_sum[None],
        reduce_sum.T[None],
        vector_sum[2:3],
        gain_sum,
        query_sum,
        jnp.stack([keyval_sum[:, :width], keyval_sum[:, width:]]),
        cmixer_sum.T,
        cexpand_sum,
        creduce_sum.T,
    )


def solution(mesh):
    placed = (
        P("mod", "dp", None, None),
        P("dp", None, None),
        P("dp"),
        P("mod", None, None),
        P("mod", None, None),
        P("mod", None, None),
        P("mod", None, None),
        P("mod", None, None),
        P(),
        P(),
        P(None, "mod"),
        P(None, None, "mod"),
        P("mod", None),
        P(None, "mod"),
        P("mod", None),
        P("mod", "dp", None, None),
        P("dp", None, None),
    )
    return jax.shard_map(
        shards,
        mesh=mesh,
        in_specs=placed,
        out_specs=(
            P("mod", "dp", None, None),
            P("dp", None, None),
            P(),
            P("mod", "dp", None, None),
            P("mod", None, "dp"),
            P("mod", "dp", None),
            P("mod", "dp", None),
            P("mod", "dp", None),
            P("mod", None, "dp"),
            P("mod", "dp"),
            P("dp"),
            P("dp", "mod"),
            P(None, "dp", "mod"),
            P("mod", "dp"),
            P("dp", "mod"),
            P("mod", "dp"),
        ),
        check_vma=False,
    )
```

```python
import functools

import jax
import jax.numpy as jnp
from jax import lax
from jax.experimental import pallas as pl
from jax.experimental.pallas import tpu as pltpu
from jax.sharding import PartitionSpec as P

HEADS = 12
HEAD_DIM = 64
LOGIT_SCALE = 50.0
F32 = jnp.float32
BF16 = jnp.bfloat16
PAIR = 2 * HEAD_DIM
LAST = (((1,), (1,)), ((), ()))
FIRST = (((0,), (0,)), ((), ()))
VMEM = pl.BlockSpec(memory_space=pltpu.VMEM)
SMEM = pl.BlockSpec(memory_space=pltpu.SMEM)
ANY = pl.BlockSpec(memory_space=pl.ANY)


def dot(left, right):
    return jnp.dot(left, right, preferred_element_type=F32)


def dot_last(left, right):
    return lax.dot_general(left, right, LAST, preferred_element_type=F32)


def dot_first(left, right):
    return lax.dot_general(left, right, FIRST, preferred_element_type=F32)


def norm_rows(values):
    centre = values - jnp.mean(values, axis=-1, keepdims=True)
    inverse = lax.rsqrt(jnp.mean(centre * centre, axis=-1, keepdims=True) + 1e-06)
    return centre * inverse, inverse


def norm_back(grad_out, unit, inverse, gain):
    weighted = grad_out * gain
    return inverse * (
        weighted
        - jnp.mean(weighted, axis=-1, keepdims=True)
        - unit * jnp.mean(weighted * unit, axis=-1, keepdims=True)
    )


def column_sum(values):
    return jnp.sum(values, axis=0, keepdims=True)


def gelu_pair(values):
    root = 0.7978845608028654
    square = values * values
    tanh = jnp.tanh(values * (root + (root * 0.044715) * square))
    half = 0.5 + 0.5 * tanh
    slope = half + (0.5 * values) * (1.0 - tanh * tanh) * (root + (3.0 * root * 0.044715) * square)
    return values * half, slope


def stacked(pair, low):
    zero = jnp.zeros_like(pair)
    return jnp.concatenate([jnp.where(low, pair, zero), jnp.where(low, zero, pair)], axis=0)


def side_by_side(values):
    rows = values.shape[0] // 2
    return jnp.concatenate([values[:rows], values[rows:]], axis=1)


def lanes(first, index):
    return pl.ds(pl.multiple_of(first + index * PAIR, PAIR), PAIR)


def attend(q_ref, k_ref, v_ref, starts, dist_ref, slope_ref, probs_ref, mixed_ref):
    patches = dist_ref.shape[0]
    low = lax.broadcasted_iota(jnp.int32, (patches, PAIR), 1) < HEAD_DIM
    scale = jnp.asarray(HEAD_DIM**-0.5, BF16)

    def one(index, carry):
        queries = stacked(q_ref[:, lanes(starts[0], index)] * scale, low)
        keys = k_ref[:, lanes(starts[1], index)]
        values = stacked(v_ref[:, lanes(starts[2], index)], low)
        scores = dot_last(queries, keys)
        distance = dist_ref[...]
        halves = []
        for side in range(2):
            part = scores[side * patches : (side + 1) * patches] - slope_ref[2 * index + side] * distance
            part = jnp.exp(part - jnp.max(part, axis=-1, keepdims=True))
            part = part * (1.0 / jnp.sum(part, axis=-1, keepdims=True))
            halves.append(part.astype(BF16))
        probs = jnp.concatenate(halves, axis=1)
        probs_ref[index] = probs
        mixed_ref[:, lanes(0, index)] = dot(probs, values).astype(BF16)
        return carry

    lax.fori_loop(0, HEADS // 2, one, 0)


def attend_back(q_ref, k_ref, v_ref, starts, probs_ref, grad_ref, out_refs, out_starts):
    patches = q_ref.shape[0]
    low = lax.broadcasted_iota(jnp.int32, (patches, PAIR), 1) < HEAD_DIM
    scale = jnp.asarray(HEAD_DIM**-0.5, BF16)

    def one(index, carry):
        queries = stacked(q_ref[:, lanes(starts[0], index)] * scale, low)
        keys = stacked(k_ref[:, lanes(starts[1], index)] * scale, low)
        values = v_ref[:, lanes(starts[2], index)]
        grads = stacked(grad_ref[:, lanes(0, index)], low)
        both = probs_ref[index]
        probs = jnp.concatenate([both[:, :patches], both[:, patches:]], axis=0)
        grad_probs = dot_last(grads, values)
        wide = probs.astype(F32)
        inner = jnp.sum(grad_probs * wide, axis=-1, keepdims=True)
        grad_scores = (wide * (grad_probs - inner)).astype(BF16)
        out_refs[0][:, lanes(out_starts[0], index)] = dot(side_by_side(grad_scores), keys).astype(BF16)
        out_refs[1][:, lanes(out_starts[1], index)] = dot_first(grad_scores, queries).astype(BF16)
        out_refs[2][:, lanes(out_starts[2], index)] = dot_first(probs, grads).astype(BF16)
        return carry

    lax.fori_loop(0, HEADS // 2, one, 0)


def begin(copies):
    for copy in copies:
        copy.start()


def finish(copies):
    for copy in copies:
        copy.wait()


def encode_kernel(
    tokens_ref, dist_ref, slope_ref, gain_ref, project_hbm, mixer_hbm, expand_hbm, reduce_hbm,
    encoded_ref, pooled_ref, normed_ref, rows_ref, probs_ref, mixed_ref, resid_ref, normed_two_ref,
    hidden_ref, slope_out_ref,
    project_ref, mixer_ref, expand_ref, reduce_ref, sems,
):
    copies = [
        pltpu.make_async_copy(source, target, sems.at[i])
        for i, (source, target) in enumerate(
            (
                (project_hbm, project_ref),
                (mixer_hbm, mixer_ref),
                (expand_hbm, expand_ref),
                (reduce_hbm, reduce_ref),
            )
        )
    ]
    begin(copies)
    width = tokens_ref.shape[1]
    tokens = tokens_ref[...].astype(F32)
    unit, _ = norm_rows(tokens)
    normed_ref[...] = (unit * gain_ref[0:1, :]).astype(BF16)
    copies[0].wait()
    for part in range(3):
        cut = slice(part * width, (part + 1) * width)
        rows_ref[:, cut] = dot(normed_ref[...], project_ref[:, cut]).astype(BF16)
    attend(rows_ref, rows_ref, rows_ref, (0, width, 2 * width), dist_ref, slope_ref, probs_ref, mixed_ref)
    copies[1].wait()
    resid = tokens_ref[...].astype(F32) + dot(mixed_ref[...], mixer_ref[...])
    resid_ref[...] = resid
    unit, _ = norm_rows(resid)
    normed_two_ref[...] = (unit * gain_ref[1:2, :]).astype(BF16)
    copies[2].wait()
    for part in range(expand_ref.shape[1] // width):
        cut = slice(part * width, (part + 1) * width)
        value, slope = gelu_pair(dot(normed_two_ref[...], expand_ref[:, cut]))
        hidden_ref[:, cut] = value.astype(BF16)
        slope_out_ref[:, cut] = slope.astype(BF16)
    copies[3].wait()
    encoded = (resid_ref[...] + dot(hidden_ref[...], reduce_ref[...])).astype(BF16)
    encoded_ref[...] = encoded
    pooled_ref[...] = jnp.mean(encoded.astype(F32), axis=0, keepdims=True)


def limits():
    return pltpu.CompilerParams(vmem_limit_bytes=60 * 1024 * 1024)


def shape(dims, dtype):
    return jax.ShapeDtypeStruct(dims, dtype)


def cost(macs, size):
    return pl.CostEstimate(flops=2 * macs, bytes_accessed=size, transcendentals=0)


def encode(tokens, dist, slopes, gains, project, mixer, expand, reduce):
    patches, width = tokens.shape
    wide = expand.shape[1]
    weights = (project, mixer, expand, reduce)
    return pl.pallas_call(
        encode_kernel,
        out_shape=(
            shape((patches, width), BF16),
            shape((1, width), F32),
            shape((patches, width), BF16),
            shape((patches, 3 * width), BF16),
            shape((HEADS // 2, patches, 2 * patches), BF16),
            shape((patches, width), BF16),
            shape((patches, width), F32),
            shape((patches, width), BF16),
            shape((patches, wide), BF16),
            shape((patches, wide), BF16),
        ),
        in_specs=[VMEM, VMEM, SMEM, VMEM] + [ANY] * 4,
        out_specs=(VMEM,) * 10,
        scratch_shapes=[pltpu.VMEM(w.shape, BF16) for w in weights] + [pltpu.SemaphoreType.DMA((4,))],
        compiler_params=limits(),
        cost_estimate=cost(patches * sum(w.size for w in weights), 24 * 2**20),
        name="encode",
    )(tokens, dist, slopes, gains, *weights)


def encode_back_kernel(
    cotangent_ref, part_ref, pool_ref, gain_ref, tokens_ref, resid_ref, slope_ref, rows_ref, probs_ref,
    project_hbm, mixer_hbm, expand_hbm, reduce_hbm,
    patch_ref, branch_ref, gexp_ref, gattn_ref, grows_ref, gains_ref,
    project_ref, mixer_ref, expand_ref, reduce_ref, gmix_ref, sems,
):
    copies = [
        pltpu.make_async_copy(source, target, sems.at[i])
        for i, (source, target) in enumerate(
            (
                (reduce_hbm, reduce_ref),
                (expand_hbm, expand_ref),
                (mixer_hbm, mixer_ref),
                (project_hbm, project_ref),
            )
        )
    ]
    begin(copies)
    patches, width = tokens_ref.shape
    grad = cotangent_ref[...].astype(F32) + pool_ref[...] * (1.0 / patches) + part_ref[...]
    patch_ref[...] = grad
    branch_ref[...] = grad.astype(BF16)
    copies[0].wait()
    for part in range(expand_ref.shape[1] // width):
        cut = slice(part * width, (part + 1) * width)
        upstream = dot_last(branch_ref[...], reduce_ref[cut, :])
        gexp_ref[:, cut] = (upstream * slope_ref[:, cut].astype(F32)).astype(BF16)
    copies[1].wait()
    grad_normed = dot_last(gexp_ref[...], expand_ref[...])
    unit, inverse = norm_rows(resid_ref[...])
    gains_ref[1:2, :] = column_sum(grad_normed * unit)
    grad = patch_ref[...] + norm_back(grad_normed, unit, inverse, gain_ref[1:2, :])
    patch_ref[...] = grad
    gattn_ref[...] = grad.astype(BF16)
    copies[2].wait()
    gmix_ref[...] = dot_last(gattn_ref[...], mixer_ref[...]).astype(BF16)
    starts = (0, width, 2 * width)
    attend_back(rows_ref, rows_ref, rows_ref, starts, probs_ref, gmix_ref, (grows_ref,) * 3, starts)
    copies[3].wait()
    grad_normed = dot_last(grows_ref[...], project_ref[...])
    unit, inverse = norm_rows(tokens_ref[...].astype(F32))
    gains_ref[0:1, :] = column_sum(grad_normed * unit)
    patch_ref[...] = patch_ref[...] + norm_back(grad_normed, unit, inverse, gain_ref[0:1, :])


def encode_back(cotangent, part, pool, gains, tokens, resid, slope, rows, probs, project, mixer, expand, reduce):
    patches, width = tokens.shape
    wide = expand.shape[1]
    weights = (project, mixer, expand, reduce)
    return pl.pallas_call(
        encode_back_kernel,
        out_shape=(
            shape((patches, width), F32),
            shape((patches, width), BF16),
            shape((patches, wide), BF16),
            shape((patches, width), BF16),
            shape((patches, 3 * width), BF16),
            shape((2, width), F32),
        ),
        in_specs=[VMEM] * 9 + [ANY] * 4,
        out_specs=(VMEM,) * 6,
        scratch_shapes=[pltpu.VMEM(w.shape, BF16) for w in weights]
        + [pltpu.VMEM((patches, width), BF16), pltpu.SemaphoreType.DMA((4,))],
        compiler_params=limits(),
        cost_estimate=cost(patches * sum(w.size for w in weights), 24 * 2**20),
        name="encode_back",
    )(cotangent, part, pool, gains, tokens, resid, slope, rows, probs, *weights)


def pack_kernel(query, keyval, mixer, expand, reduce, first, second, third, sems):
    quarter = quarter_of(lax.axis_index("dp"))
    rows, half = query.shape[0] // 4, query.shape[1]
    mixer_rows = mixer.shape[0] // 4
    wide_rows = reduce.shape[0] // 4
    width = mixer.shape[1]
    own = pl.ds(quarter * rows, rows)
    plan = [
        (query.at[own], first.at[0:rows, 0:half]),
        (keyval.at[0, own], first.at[0:rows, half:width]),
        (keyval.at[1, pl.ds(quarter * rows, rows // 2)], first.at[rows : rows + rows // 2, 0:half]),
        (keyval.at[1, pl.ds(quarter * rows + rows // 2, rows // 2)], first.at[rows : rows + rows // 2, half:width]),
        (mixer.at[pl.ds(quarter * mixer_rows, mixer_rows)], first.at[rows + rows // 2 : rows + rows // 2 + mixer_rows]),
        (expand.at[own, 0:width], second.at[0:rows]),
        (expand.at[own, width : 2 * width], second.at[rows : 2 * rows]),
        (reduce.at[pl.ds(quarter * wide_rows, wide_rows)], third),
    ]
    copies = [pltpu.make_async_copy(a, b, sems.at[i]) for i, (a, b) in enumerate(plan)]
    begin(copies)
    finish(copies)


def quarter_of(index):
    return lax.rem(index, 4)


def pack(query, keyval, mixer, expand, reduce):
    width = mixer.shape[1]
    rows = query.shape[0] // 4
    return pl.pallas_call(
        pack_kernel,
        out_shape=(shape((2 * rows, width), BF16),) * 3,
        in_specs=[ANY] * 5,
        out_specs=(VMEM,) * 3,
        scratch_shapes=[pltpu.SemaphoreType.DMA((8,))],
        compiler_params=limits(),
        cost_estimate=cost(0, 4 * 2**20),
        name="pack",
    )(query, keyval, mixer, expand, reduce)


def unpack_plan(pieces, quarter, query, keyval, mixer, expand, reduce):
    first, second, third = pieces
    rows, width = first.shape[0] // 2, first.shape[1]
    half = width // 2
    mixer_rows = rows // 2
    own = pl.ds(quarter * rows, rows)
    wide_rows = 2 * rows
    wide = 2 * width
    return (
        [
            (first.at[0:rows, 0:half], query.at[own, half:width]),
            (first.at[0:rows, half:width], keyval.at[own, half:width]),
            (first.at[rows : rows + rows // 2, 0:half],
             keyval.at[pl.ds(quarter * rows, rows // 2), width + half : 2 * width]),
            (first.at[rows : rows + rows // 2, half:width],
             keyval.at[pl.ds(quarter * rows + rows // 2, rows // 2), width + half : 2 * width]),
            (first.at[rows + rows // 2 : 2 * rows], mixer.at[pl.ds(half + quarter * mixer_rows, mixer_rows)]),
        ],
        [
            (second.at[0:rows], expand.at[own, wide : wide + width]),
            (second.at[rows : 2 * rows], expand.at[own, wide + width : 2 * wide]),
        ],
        [(third, reduce.at[pl.ds(wide + quarter * wide_rows, wide_rows)])],
    )


def joining_kernel(
    image, own_ref, other_ref, dist_ref, slope_ref, norms_ref, gain_ref, present_ref, cotangent_ref,
    query_hbm, keyval_hbm, mixer_hbm, expand_hbm, reduce_hbm, *rest,
):
    pieces, rest = rest[:12], rest[12:]
    (
        joined_ref, part_ref, query_in_ref, keyval_in_ref, normed_ref, mixed_own_ref, hidden_own_ref, branch_ref,
        gexp_own_ref, gattn_ref, gq_own_ref, gkv_own_ref, gains_ref,
        query_ref, keyval_ref, mixer_ref, expand_ref, reduce_ref,
        q_ref, kv_ref, probs_ref, mixed_ref, hidden_ref, resid_ref, gexp_ref, gmix_ref, gq_ref, gkv_ref, gin_ref, sems,
    ) = rest
    patches, width = own_ref.shape
    half = width // 2
    wide = 2 * width
    mod = lax.axis_index("mod")
    is_radar = mod == 1
    quarter = quarter_of(lax.axis_index("dp"))
    plans = (
        [
            (query_hbm, query_ref.at[:, 0:half]),
            (keyval_hbm.at[0], keyval_ref.at[:, 0:half]),
            (keyval_hbm.at[1], keyval_ref.at[:, width : width + half]),
            (mixer_hbm, mixer_ref.at[0:half]),
        ],
        [(expand_hbm, expand_ref.at[:, 0:wide])],
        [(reduce_hbm, reduce_ref.at[0:wide])],
    )
    where = (quarter, quarter ^ 2, quarter ^ 1, quarter ^ 3)
    for source in range(4):
        more = unpack_plan(
            pieces[3 * source : 3 * source + 3], where[source], query_ref, keyval_ref, mixer_ref, expand_ref, reduce_ref
        )
        for plan, extra in zip(plans, more):
            plan.extend(extra)
    groups, place = [], 0
    for plan in plans:
        groups.append([pltpu.make_async_copy(a, b, sems.at[place + i]) for i, (a, b) in enumerate(plan)])
        place += len(plan)
    for group in groups:
        begin(group)

    radar = jnp.where(is_radar, own_ref[...], other_ref[...]).astype(F32)
    optical = jnp.where(is_radar, other_ref[...], own_ref[...]).astype(F32)
    unit, _ = norm_rows(radar)
    query_in_ref[...] = (unit * norms_ref[1:2, :]).astype(BF16)
    unit, _ = norm_rows(optical)
    keyval_in_ref[...] = (unit * norms_ref[0:1, :]).astype(BF16)
    finish(groups[0])
    q_ref[...] = dot(query_in_ref[...], query_ref[...]).astype(BF16)
    for part in range(2):
        cut = slice(part * width, (part + 1) * width)
        kv_ref[:, cut] = dot(keyval_in_ref[...], keyval_ref[:, cut]).astype(BF16)
    starts = (0, 0, width)
    attend(q_ref, kv_ref, kv_ref, starts, dist_ref, slope_ref, probs_ref, mixed_ref)
    mixed_own_ref[...] = mixed_ref[:, 0:half]
    radar = jnp.where(is_radar, own_ref[...], other_ref[...]).astype(F32)
    resid = radar + dot(mixed_ref[...], mixer_ref[...])
    resid_ref[...] = resid
    unit, _ = norm_rows(resid)
    normed_ref[...] = (unit * gain_ref[...]).astype(BF16)
    present = present_ref[image].astype(F32)
    grad_joined = present * cotangent_ref[...].astype(F32)
    branch_ref[...] = grad_joined.astype(BF16)
    finish(groups[1])
    finish(groups[2])
    for part in range(expand_ref.shape[1] // width):
        cut = slice(part * width, (part + 1) * width)
        value, slope = gelu_pair(dot(normed_ref[...], expand_ref[:, cut]))
        hidden_ref[:, cut] = value.astype(BF16)
        upstream = dot_last(branch_ref[...], reduce_ref[cut, :])
        gexp_ref[:, cut] = (upstream * slope).astype(BF16)
    hidden_own_ref[...] = hidden_ref[:, 0:wide]
    gexp_own_ref[...] = gexp_ref[:, 0:wide]

    @pl.when(mod == image)
    def _():
        joined_ref[...] = (present * (resid_ref[...] + dot(hidden_ref[...], reduce_ref[...]))).astype(BF16)

    @pl.when(mod != image)
    def _():
        joined_ref[...] = jnp.zeros_like(joined_ref)

    grad_normed = dot_last(gexp_ref[...], expand_ref[...])
    unit, inverse = norm_rows(resid_ref[...])
    gains_ref[1:2, :] = column_sum(grad_normed * unit)
    grad_joined = present * cotangent_ref[...].astype(F32)
    grad = grad_joined + norm_back(grad_normed, unit, inverse, gain_ref[...])
    part_ref[...] = grad
    gattn_ref[...] = grad.astype(BF16)
    gmix_ref[...] = dot_last(gattn_ref[...], mixer_ref[...]).astype(BF16)
    attend_back(q_ref, kv_ref, kv_ref, starts, probs_ref, gmix_ref, (gq_ref, gkv_ref, gkv_ref), (0, 0, width))
    gq_own_ref[...] = gq_ref[:, 0:half]
    gkv_own_ref[:, 0:half] = gkv_ref[:, 0:half]
    gkv_own_ref[:, half:width] = gkv_ref[:, width : width + half]

    @pl.when(is_radar)
    def _():
        gin_ref[...] = dot_last(gq_ref[...], query_ref[...])

    @pl.when(mod == 0)
    def _():
        gin_ref[...] = dot_last(gkv_ref[...], keyval_ref[...])

    gain = jnp.where(is_radar, norms_ref[1:2, :], norms_ref[0:1, :])
    unit, inverse = norm_rows(own_ref[...].astype(F32))
    grad_in = gin_ref[...]
    gains_ref[0:1, :] = column_sum(grad_in * unit)
    part_ref[...] = jnp.where(is_radar, part_ref[...], 0.0) + norm_back(grad_in, unit, inverse, gain)


def joining(image, own, other, dist, slopes, norms, gain, present, cotangent, weights, pieces):
    patches, width = own.shape
    half, wide = width // 2, 2 * width
    copies = 6 + 4 * 8
    return pl.pallas_call(
        functools.partial(joining_kernel, image),
        out_shape=(
            shape((patches, width), BF16),
            shape((patches, width), F32),
            shape((patches, width), BF16),
            shape((patches, width), BF16),
            shape((patches, width), BF16),
            shape((patches, half), BF16),
            shape((patches, wide), BF16),
            shape((patches, width), BF16),
            shape((patches, wide), BF16),
            shape((patches, width), BF16),
            shape((patches, half), BF16),
            shape((patches, width), BF16),
            shape((2, width), F32),
        ),
        in_specs=[VMEM, VMEM, VMEM, SMEM, VMEM, VMEM, SMEM, VMEM] + [ANY] * (5 + 12),
        out_specs=(VMEM,) * 13,
        scratch_shapes=[
            pltpu.VMEM((width, width), BF16),
            pltpu.VMEM((width, 2 * width), BF16),
            pltpu.VMEM((width, width), BF16),
            pltpu.VMEM((width, 2 * wide), BF16),
            pltpu.VMEM((2 * wide, width), BF16),
            pltpu.VMEM((patches, width), BF16),
            pltpu.VMEM((patches, 2 * width), BF16),
            pltpu.VMEM((HEADS // 2, patches, 2 * patches), BF16),
            pltpu.VMEM((patches, width), BF16),
            pltpu.VMEM((patches, 2 * wide), BF16),
            pltpu.VMEM((patches, width), F32),
            pltpu.VMEM((patches, 2 * wide), BF16),
            pltpu.VMEM((patches, width), BF16),
            pltpu.VMEM((patches, width), BF16),
            pltpu.VMEM((patches, 2 * width), BF16),
            pltpu.VMEM((patches, width), F32),
            pltpu.SemaphoreType.DMA((copies,)),
        ],
        compiler_params=limits(),
        cost_estimate=cost(patches * 9 * width * width * 3, 24 * 2**20),
        name="joining",
    )(own, other, dist, slopes, norms, gain, present, cotangent, *weights, *pieces)


def ring_bits(index, count):
    return [lax.rem(index // (1 << bit), 2) for bit in range(count)]


def side_of(buffer, left, bit, index):
    return buffer.at[tuple(index if other == bit else slice(None) for other in left)]


def sum_kernel(plan, results, orders, sizes, *refs):
    n_in, n_out, slots = sizes
    inputs, vector_ref = refs[:n_in], refs[n_in]
    outs, vector_out = refs[n_in + 1 : n_in + 1 + n_out], refs[n_in + 1 + n_out]
    scratch = refs[n_in + 2 + n_out :]
    bits = len(orders[0])
    held, got = scratch[:bits], scratch[bits : 2 * bits]
    vector_held, vector_got = scratch[2 * bits : 3 * bits - 1], scratch[3 * bits - 1 : 4 * bits - 1]
    send_sems, recv_sems = scratch[4 * bits - 1 :]
    me = lax.axis_index("dp")
    mine = ring_bits(me, bits)
    partners = [me + (1 - 2 * mine[bit]) * (1 << bit) for bit in range(bits)]
    barrier = pltpu.get_barrier_semaphore()
    for partner in partners:
        pl.semaphore_signal(barrier, inc=1, device_id={"dp": partner}, device_id_type=pl.DeviceIdType.MESH)
    pl.semaphore_wait(barrier, bits)
    every = list(range(bits))[::-1]
    total = len(plan)
    block = outs[0].shape[0]
    copies = {}

    def left_at(chunk, stage):
        done = orders[chunk][:stage]
        return [bit for bit in every if bit not in done]

    def source(chunk, stage):
        if chunk == total:
            return vector_ref if stage == 0 else vector_held[stage - 1]
        return held[stage].at[chunk % slots]

    def target(chunk, stage):
        return vector_got[stage] if chunk == total else got[stage].at[chunk]

    def send(chunk, stage):
        bit = orders[chunk][stage]
        copy = pltpu.make_async_remote_copy(
            src_ref=side_of(source(chunk, stage), left_at(chunk, stage), bit, 1 - mine[bit]),
            dst_ref=target(chunk, stage),
            send_sem=send_sems.at[stage, chunk],
            recv_sem=recv_sems.at[stage, chunk],
            device_id={"dp": partners[bit]},
            device_id_type=pl.DeviceIdType.MESH,
        )
        copy.start()
        copies[chunk, stage] = copy

    def free(chunk, stage):
        if chunk >= 0:
            copies[chunk, stage].wait_send()

    def make(chunk):
        free(chunk - slots, 0)
        for lefts, rights, cut, place in plan[chunk]:
            product = None
            for one, other in zip(lefts, rights):
                term = dot_first(inputs[one][...], inputs[other][:, cut[0] : cut[1]])
                product = term if product is None else product + term
            product = product.astype(BF16)
            for index in range(1 << bits):
                where = tuple((index >> bit) & 1 for bit in every)
                held[0][(chunk % slots, *where, slice(None), slice(place, place + cut[1] - cut[0]))] = product[
                    index * block : (index + 1) * block
                ]

    def take(chunk, stage):
        bit = orders[chunk][stage]
        copies[chunk, stage].wait_recv()
        kept = side_of(source(chunk, stage), left_at(chunk, stage), bit, mine[bit])
        if chunk == total:
            value = kept[...] + target(chunk, stage)[...]
            (vector_out if stage == bits - 1 else vector_held[stage])[...] = value
        elif stage == bits - 1:
            out, place = results[chunk]
            width = got[stage].shape[-1]
            outs[out][:, place : place + width] = kept[...].astype(F32) + target(chunk, stage)[...].astype(F32)
        else:
            free(chunk - slots, stage + 1)
            held[stage + 1][chunk % slots] = kept[...] + target(chunk, stage)[...]

    for step in range(total + 1 + bits):
        if step < total:
            make(step)
        if step <= total:
            send(step, 0)
        for stage in range(bits):
            chunk = step - 1 - stage
            if 0 <= chunk <= total:
                take(chunk, stage)
                if stage < bits - 1:
                    send(chunk, stage + 1)
    for stage in range(bits):
        for chunk in range(max(0, total - slots), total):
            free(chunk, stage)
        free(total, stage)


def summed_products(inputs, plan, results, widths, vector, count):
    bits = count.bit_length() - 1
    rows = inputs[0].shape[1]
    block, total, slots = rows // count, len(plan), 3
    orders = [tuple(range(bits))] * (total + 1)
    two = (2,) * bits
    return pl.pallas_call(
        functools.partial(sum_kernel, plan, results, orders, (len(inputs), len(widths), slots)),
        out_shape=tuple(shape((block, width), F32) for width in widths) + (shape(vector.shape[bits:], F32),),
        in_specs=[VMEM] * (len(inputs) + 1),
        out_specs=(VMEM,) * (len(widths) + 1),
        scratch_shapes=[pltpu.VMEM((slots, *two[stage:], block, rows), BF16) for stage in range(bits)]
        + [pltpu.VMEM((total, *two[stage + 1 :], block, rows), BF16) for stage in range(bits)]
        + [pltpu.VMEM(vector.shape[stage:], F32) for stage in range(1, bits)]
        + [pltpu.VMEM(vector.shape[stage:], F32) for stage in range(1, bits + 1)]
        + [pltpu.SemaphoreType.DMA((bits, total + 1))] * 2,
        compiler_params=pltpu.CompilerParams(
            collective_id=0, has_side_effects=True, vmem_limit_bytes=62 * 1024 * 1024
        ),
        cost_estimate=cost(total * rows * rows * 512, 48 * 2**20),
        name="sum_products",
    )(*inputs, vector)


def contrast(pooled, present):
    total = pooled.shape[1]
    inverse = lax.rsqrt(jnp.mean(pooled * pooled, axis=-1, keepdims=True) + 1e-06)
    unit = pooled * inverse
    scale = LOGIT_SCALE / pooled.shape[2]
    logits = jnp.dot(unit[0], unit[1].T, precision=lax.Precision.HIGHEST) * scale
    absent = 10000.0 * (1.0 - present)
    by_row = logits - absent[None, :]
    by_column = logits - absent[:, None]
    row_total = jax.nn.logsumexp(by_row, axis=1, keepdims=True)
    column_total = jax.nn.logsumexp(by_column, axis=0, keepdims=True)
    same = jnp.eye(total, dtype=F32)
    diagonal = jnp.sum(logits * same, axis=1)
    loss = jnp.sum(present * (row_total[:, 0] + column_total[0] - 2.0 * diagonal)) / (2.0 * total)
    grad_logits = (
        present[:, None] * jnp.exp(by_row - row_total)
        + present[None, :] * jnp.exp(by_column - column_total)
        - 2.0 * same * present[:, None]
    ) * (scale / (2.0 * total))
    grad_unit = jnp.stack(
        [
            jnp.dot(grad_logits, unit[1], precision=lax.Precision.HIGHEST),
            jnp.dot(grad_logits.T, unit[0], precision=lax.Precision.HIGHEST),
        ]
    )
    return loss, inverse * (grad_unit - unit * jnp.mean(grad_unit * unit, axis=-1, keepdims=True))


def flipped(array, axis, bit):
    return lax.ppermute(array, axis, [(i, i ^ (1 << bit)) for i in range(lax.axis_size(axis))])


def block_order(width, count):
    bits = count.bit_length() - 1
    block = width // count
    rows = jnp.arange(width)
    place = rows // block
    partner = jnp.zeros_like(place)
    for bit in range(bits):
        partner = partner | (((place >> (bits - 1 - bit)) & 1) << bit)
    source = (lax.axis_index("dp") ^ partner) * block + rows % block
    return (source[:, None] == jnp.arange(width)[None, :]).astype(BF16)


def ordered(order, values):
    flat = jnp.concatenate(values, axis=0)
    return jnp.einsum("jd,rd->jr", order, flat, preferred_element_type=F32).astype(BF16)


def summed(left_rows, grad_rows):
    count = lax.axis_size("dp")
    flat = jnp.concatenate(grad_rows, axis=0)
    half = left_rows.shape[0] // 2
    send = jnp.dot(left_rows[half:], flat, preferred_element_type=F32).astype(BF16)
    keep = jnp.dot(left_rows[:half], flat, preferred_element_type=F32).astype(BF16)
    bits = count.bit_length() - 1
    for bit in range(bits):
        got = flipped(send, "dp", bit)
        if bit == bits - 1:
            return keep.astype(F32) + got.astype(F32)
        half = half // 2
        send = (keep[half:].astype(F32) + got[half:].astype(F32)).astype(BF16)
        keep = (keep[:half].astype(F32) + got[:half].astype(F32)).astype(BF16)


def summed_blocks(blocks):
    bits = lax.axis_size("dp").bit_length() - 1
    for bit in range(bits):
        half = blocks.shape[0] // 2
        blocks = blocks[:half] + flipped(blocks[half:], "dp", bit)
    return blocks[0]


def all_summed(products, blocks):
    count = blocks.shape[0]
    rows = products[0][0][0].shape[1]
    if count != 16 or (rows // count) % 16:
        order = block_order(rows, count)
        sums = [summed(ordered(order, lefts), rights) for lefts, rights in products]
        wanted = jnp.dot(order[:: rows // count, :: rows // count].astype(F32), blocks.reshape(count, -1),
                         precision=lax.Precision.HIGHEST)
        return (*sums, summed_blocks(wanted.reshape(blocks.shape)))
    inputs, plan, results, widths, fill = [], [], [], [], 0
    for lefts, rights in products:
        first = len(inputs)
        inputs.extend([*lefts, *rights])
        left = tuple(range(first, first + len(lefts)))
        right = tuple(range(first + len(lefts), len(inputs)))
        width = rights[0].shape[1]
        if width < rows:
            if not fill:
                plan.append([])
                results.append((len(widths), 0))
                widths.append(rows)
            plan[-1].append((left, right, (0, width), fill))
            fill = (fill + width) % rows
            continue
        for start in range(0, width, rows):
            plan.append([(left, right, (start, start + rows), 0)])
            results.append((len(widths), start))
        widths.append(width)
    vector = jnp.pad(blocks, ((0, 0), (0, 8 - blocks.shape[1]), (0, 128 - blocks.shape[2])))
    vector = vector.reshape((2,) * (count.bit_length() - 1) + vector.shape[1:])
    *sums, vector_sum = summed_products(inputs, plan, results, widths, vector, count)
    both = sums.pop(2)
    sums[2:2] = [both[:, : rows // 2], both[:, rows // 2 :]]
    return (*sums, vector_sum[: blocks.shape[1], : blocks.shape[2]])


def shards(
    patch_tokens,
    grid_coords,
    has_radar,
    enc_gains,
    enc_project,
    enc_mixer,
    enc_expand,
    enc_reduce,
    cross_norms,
    cross_gain,
    cross_query,
    cross_keyval,
    cross_mixer,
    cross_expand,
    cross_reduce,
    enc_cotangent,
    joined_cotangent,
):
    item_count, patches, model_width = patch_tokens.shape[1:]
    images = range(item_count)
    half_index = lax.axis_index("mod")
    dp_index = lax.axis_index("dp")
    dp_size = lax.axis_size("dp")
    is_radar = half_index == 1
    weights = (enc_project[0], enc_mixer[0], enc_expand[0], enc_reduce[0])
    cross_weights = (cross_query, cross_keyval, cross_mixer, cross_expand, cross_reduce)

    pieces = []
    for packed in pack(*cross_weights):
        mine = flipped(packed, "mod", 0)
        beside = flipped(mine, "dp", 1)
        pieces.append((mine, beside, flipped(mine, "dp", 0), flipped(beside, "dp", 0)))
    pieces = [pieces[group][source] for source in range(4) for group in range(3)]

    grid = grid_coords.astype(F32)
    across = grid[:, 0, :, None] - grid[:, 0, None, :]
    upward = grid[:, 1, :, None] - grid[:, 1, None, :]
    distance = jnp.sqrt(across * across + upward * upward)
    heads = jnp.arange(HEADS)
    slopes = jnp.exp2(-8.0 * (heads + 1).astype(F32) / HEADS)
    cross_heads = (heads + half_index * (HEADS // 2)) % HEADS
    cross_slopes = jnp.exp2(-8.0 * (cross_heads + 1).astype(F32) / HEADS)

    forward = [encode(patch_tokens[0, n], distance[n], slopes, enc_gains[0], *weights) for n in images]
    partners = [flipped(forward[n][0], "mod", 0) for n in images]

    pooled_own = jnp.concatenate([forward[n][1] for n in images], axis=0)
    pooled_pair = jnp.stack([pooled_own, flipped(pooled_own, "mod", 0)], axis=1)
    present_row = jnp.broadcast_to(has_radar.astype(F32)[:, None, None], (item_count, 1, model_width))
    gathered = lax.all_gather(jnp.concatenate([pooled_pair, present_row], axis=1), "dp", axis=0, tiled=True)
    first, second = gathered[:, 0], gathered[:, 1]
    pooled = jnp.stack([jnp.where(is_radar, second, first), jnp.where(is_radar, first, second)])
    loss_value, pool_grad = contrast(pooled, gathered[:, 2, 0])
    own_pool_grad = lax.dynamic_slice(
        pool_grad, (half_index, dp_index * item_count, 0), (1, item_count, model_width)
    )[0]

    joined = [
        joining(
            n, forward[n][0], partners[n], distance[n], cross_slopes, cross_norms, cross_gain[None], has_radar,
            joined_cotangent[n], cross_weights, pieces,
        )
        for n in images
    ]
    joined_mine = jnp.where(is_radar, joined[1][0], joined[0][0])
    joined_theirs = flipped(joined_mine, "mod", 0)
    joined_tokens = jnp.stack(
        [jnp.where(is_radar, joined_theirs, joined_mine), jnp.where(is_radar, joined_mine, joined_theirs)]
    )
    def each(results, place):
        return [results[n][place] for n in images]

    backward = [
        encode_back(
            enc_cotangent[0, n], joined[n][1], own_pool_grad[n : n + 1], enc_gains[0], patch_tokens[0, n],
            forward[n][6], forward[n][9], forward[n][3], forward[n][4], *weights,
        )
        for n in images
    ]
    own_gain = jnp.where(is_radar, joined[1][12][1], joined[0][12][1])
    own_gain = own_gain + flipped(own_gain[None], "mod", 0)[0]
    gains = backward[0][5] + backward[1][5]
    vectors = jnp.stack([gains[0], gains[1], joined[0][12][0] + joined[1][12][0], own_gain])
    block = model_width // dp_size
    blocks = jnp.moveaxis(vectors.reshape(4, dp_size, block), 1, 0)
    products = (
        (each(joined, 7), each(joined, 6)),
        (each(joined, 4), each(joined, 8)),
        (each(joined, 2), each(joined, 10)),
        (each(joined, 9), each(joined, 5)),
        (each(joined, 3), each(joined, 11)),
        (each(backward, 1), each(forward, 8)),
        (each(forward, 7), each(backward, 2)),
        (each(forward, 5), each(backward, 3)),
        (each(forward, 2), each(backward, 4)),
    )
    (creduce_sum, cexpand_sum, query_sum, cmixer_sum, keyval_sum, reduce_sum, expand_sum, mixer_sum, project_sum,
     vector_sum) = all_summed(products, blocks)
    width = model_width // 2
    return (
        jnp.stack(each(forward, 0))[None],
        joined_tokens,
        loss_value,
        jnp.stack(each(backward, 0))[None],
        vector_sum[None, :2],
        project_sum[None],
        mixer_sum[None],
        expand_sum[None],
        reduce_sum.T[None],
        vector_sum[2:3],
        vector_sum[3],
        query_sum,
        jnp.stack([keyval_sum[:, :width], keyval_sum[:, width:]]),
        cmixer_sum.T,
        cexpand_sum,
        creduce_sum.T,
    )


def solution(mesh):
    placed = (
        P("mod", "dp", None, None),
        P("dp", None, None),
        P("dp"),
        P("mod", None, None),
        P("mod", None, None),
        P("mod", None, None),
        P("mod", None, None),
        P("mod", None, None),
        P(),
        P(),
        P(None, "mod"),
        P(None, None, "mod"),
        P("mod", None),
        P(None, "mod"),
        P("mod", None),
        P("mod", "dp", None, None),
        P("dp", None, None),
    )
    return jax.shard_map(
        shards,
        mesh=mesh,
        in_specs=placed,
        out_specs=(
            P("mod", "dp", None, None),
            P("dp", None, None),
            P(),
            P("mod", "dp", None, None),
            P("mod", None, "dp"),
            P("mod", "dp", None),
            P("mod", "dp", None),
            P("mod", "dp", None),
            P("mod", None, "dp"),
            P("mod", "dp"),
            P("dp"),
            P("dp", "mod"),
            P(None, "dp", "mod"),
            P("mod", "dp"),
            P("dp", "mod"),
            P("mod", "dp"),
        ),
        check_vma=False,
    )
```

```python
import functools

import jax
import jax.numpy as jnp
from jax import lax
from jax.experimental import pallas as pl
from jax.experimental.pallas import tpu as pltpu
from jax.sharding import PartitionSpec as P

HEADS = 12
HEAD_DIM = 64
LOGIT_SCALE = 50.0
F32 = jnp.float32
BF16 = jnp.bfloat16
PAIR = 2 * HEAD_DIM
LAST = (((1,), (1,)), ((), ()))
FIRST = (((0,), (0,)), ((), ()))
VMEM = pl.BlockSpec(memory_space=pltpu.VMEM)
SMEM = pl.BlockSpec(memory_space=pltpu.SMEM)
ANY = pl.BlockSpec(memory_space=pl.ANY)


def dot(left, right):
    return jnp.dot(left, right, preferred_element_type=F32)


def dot_last(left, right):
    return lax.dot_general(left, right, LAST, preferred_element_type=F32)


def dot_first(left, right):
    return lax.dot_general(left, right, FIRST, preferred_element_type=F32)


def norm_rows(values):
    centre = values - jnp.mean(values, axis=-1, keepdims=True)
    inverse = lax.rsqrt(jnp.mean(centre * centre, axis=-1, keepdims=True) + 1e-06)
    return centre * inverse, inverse


def norm_back(grad_out, unit, inverse, gain):
    weighted = grad_out * gain
    return inverse * (
        weighted
        - jnp.mean(weighted, axis=-1, keepdims=True)
        - unit * jnp.mean(weighted * unit, axis=-1, keepdims=True)
    )


def column_sum(values):
    return jnp.sum(values, axis=0, keepdims=True)


def gelu_pair(values):
    root = 0.7978845608028654
    square = values * values
    tanh = jnp.tanh(values * (root + (root * 0.044715) * square))
    half = 0.5 + 0.5 * tanh
    slope = half + (0.5 * values) * (1.0 - tanh * tanh) * (root + (3.0 * root * 0.044715) * square)
    return values * half, slope


def stacked(pair, low):
    zero = jnp.zeros_like(pair)
    return jnp.concatenate([jnp.where(low, pair, zero), jnp.where(low, zero, pair)], axis=0)


def side_by_side(values):
    rows = values.shape[0] // 2
    return jnp.concatenate([values[:rows], values[rows:]], axis=1)


def lanes(first, index):
    return pl.ds(pl.multiple_of(first + index * PAIR, PAIR), PAIR)


def attend(q_ref, k_ref, v_ref, starts, dist_ref, slope_ref, probs_ref, mixed_ref):
    patches = dist_ref.shape[0]
    low = lax.broadcasted_iota(jnp.int32, (patches, PAIR), 1) < HEAD_DIM
    scale = jnp.asarray(HEAD_DIM**-0.5, BF16)

    def one(index, carry):
        queries = stacked(q_ref[:, lanes(starts[0], index)] * scale, low)
        keys = k_ref[:, lanes(starts[1], index)]
        values = stacked(v_ref[:, lanes(starts[2], index)], low)
        scores = dot_last(queries, keys)
        distance = dist_ref[...]
        halves = []
        for side in range(2):
            part = scores[side * patches : (side + 1) * patches] - slope_ref[2 * index + side] * distance
            part = jnp.exp(part - jnp.max(part, axis=-1, keepdims=True))
            part = part * (1.0 / jnp.sum(part, axis=-1, keepdims=True))
            halves.append(part.astype(BF16))
        probs = jnp.concatenate(halves, axis=1)
        probs_ref[index] = probs
        mixed_ref[:, lanes(0, index)] = dot(probs, values).astype(BF16)
        return carry

    lax.fori_loop(0, HEADS // 2, one, 0)


def attend_back(q_ref, k_ref, v_ref, starts, probs_ref, grad_ref, out_refs, out_starts):
    patches = q_ref.shape[0]
    low = lax.broadcasted_iota(jnp.int32, (patches, PAIR), 1) < HEAD_DIM
    scale = jnp.asarray(HEAD_DIM**-0.5, BF16)

    def one(index, carry):
        queries = stacked(q_ref[:, lanes(starts[0], index)] * scale, low)
        keys = stacked(k_ref[:, lanes(starts[1], index)] * scale, low)
        values = v_ref[:, lanes(starts[2], index)]
        grads = stacked(grad_ref[:, lanes(0, index)], low)
        both = probs_ref[index]
        probs = jnp.concatenate([both[:, :patches], both[:, patches:]], axis=0)
        grad_probs = dot_last(grads, values)
        wide = probs.astype(F32)
        inner = jnp.sum(grad_probs * wide, axis=-1, keepdims=True)
        grad_scores = (wide * (grad_probs - inner)).astype(BF16)
        out_refs[0][:, lanes(out_starts[0], index)] = dot(side_by_side(grad_scores), keys).astype(BF16)
        out_refs[1][:, lanes(out_starts[1], index)] = dot_first(grad_scores, queries).astype(BF16)
        out_refs[2][:, lanes(out_starts[2], index)] = dot_first(probs, grads).astype(BF16)
        return carry

    lax.fori_loop(0, HEADS // 2, one, 0)


def begin(copies):
    for copy in copies:
        copy.start()


def finish(copies):
    for copy in copies:
        copy.wait()


def limits():
    return pltpu.CompilerParams(vmem_limit_bytes=60 * 1024 * 1024)


def shape(dims, dtype):
    return jax.ShapeDtypeStruct(dims, dtype)


def cost(macs, size):
    return pl.CostEstimate(flops=2 * macs, bytes_accessed=size, transcendentals=0)


def encode_back_kernel(
    cotangent_ref, part_ref, pool_ref, gain_ref, tokens_ref, resid_ref, slope_ref, rows_ref, probs_ref,
    project_hbm, mixer_hbm, expand_hbm, reduce_hbm,
    patch_ref, branch_ref, gexp_ref, gattn_ref, grows_ref, gains_ref,
    project_ref, mixer_ref, expand_ref, reduce_ref, gmix_ref, sems,
):
    copies = [
        pltpu.make_async_copy(source, target, sems.at[i])
        for i, (source, target) in enumerate(
            (
                (reduce_hbm, reduce_ref),
                (expand_hbm, expand_ref),
                (mixer_hbm, mixer_ref),
                (project_hbm, project_ref),
            )
        )
    ]
    begin(copies)
    patches, width = tokens_ref.shape
    grad = cotangent_ref[...].astype(F32) + pool_ref[...] * (1.0 / patches) + part_ref[...]
    patch_ref[...] = grad
    branch_ref[...] = grad.astype(BF16)
    copies[0].wait()
    for part in range(expand_ref.shape[1] // width):
        cut = slice(part * width, (part + 1) * width)
        upstream = dot_last(branch_ref[...], reduce_ref[cut, :])
        gexp_ref[:, cut] = (upstream * slope_ref[:, cut].astype(F32)).astype(BF16)
    copies[1].wait()
    grad_normed = dot_last(gexp_ref[...], expand_ref[...])
    unit, inverse = norm_rows(resid_ref[...])
    gains_ref[1:2, :] = column_sum(grad_normed * unit)
    grad = patch_ref[...] + norm_back(grad_normed, unit, inverse, gain_ref[1:2, :])
    patch_ref[...] = grad
    gattn_ref[...] = grad.astype(BF16)
    copies[2].wait()
    gmix_ref[...] = dot_last(gattn_ref[...], mixer_ref[...]).astype(BF16)
    starts = (0, width, 2 * width)
    attend_back(rows_ref, rows_ref, rows_ref, starts, probs_ref, gmix_ref, (grows_ref,) * 3, starts)
    copies[3].wait()
    grad_normed = dot_last(grows_ref[...], project_ref[...])
    unit, inverse = norm_rows(tokens_ref[...].astype(F32))
    gains_ref[0:1, :] = column_sum(grad_normed * unit)
    patch_ref[...] = patch_ref[...] + norm_back(grad_normed, unit, inverse, gain_ref[0:1, :])


def encode_back(cotangent, part, pool, gains, tokens, resid, slope, rows, probs, project, mixer, expand, reduce):
    patches, width = tokens.shape
    wide = expand.shape[1]
    weights = (project, mixer, expand, reduce)
    return pl.pallas_call(
        encode_back_kernel,
        out_shape=(
            shape((patches, width), F32),
            shape((patches, width), BF16),
            shape((patches, wide), BF16),
            shape((patches, width), BF16),
            shape((patches, 3 * width), BF16),
            shape((2, width), F32),
        ),
        in_specs=[VMEM] * 9 + [ANY] * 4,
        out_specs=(VMEM,) * 6,
        scratch_shapes=[pltpu.VMEM(w.shape, BF16) for w in weights]
        + [pltpu.VMEM((patches, width), BF16), pltpu.SemaphoreType.DMA((4,))],
        compiler_params=limits(),
        cost_estimate=cost(patches * sum(w.size for w in weights), 24 * 2**20),
        name="encode_back",
    )(cotangent, part, pool, gains, tokens, resid, slope, rows, probs, *weights)


def ring_bits(index, count):
    return [lax.rem(index // (1 << bit), 2) for bit in range(count)]


def side_of(buffer, left, bit, index):
    return buffer.at[tuple(index if other == bit else slice(None) for other in left)]


class Outputs:
    def __init__(self, sems):
        self.sems, self.used, self.open = sems, 0, {}

    def emit(self, key, source, target):
        copy = pltpu.make_async_copy(source, target, self.sems.at[self.used])
        self.used += 1
        copy.start()
        self.open.setdefault(key, []).append(copy)

    def ready(self, *keys):
        for key in keys:
            for copy in self.open.pop(key, []):
                copy.wait()

    def finish(self):
        self.ready(*list(self.open))


def remote(source, target, send_sem, recv_sem, device):
    return pltpu.make_async_remote_copy(
        src_ref=source,
        dst_ref=target,
        send_sem=send_sem,
        recv_sem=recv_sem,
        device_id=device,
        device_id_type=pl.DeviceIdType.MESH,
    )


class Weights:
    def __init__(self, refs, me, mod, sems):
        self.refs, self.sems, self.mod = refs, sems, mod
        low = ring_bits(me, 3)
        self.flip = [1 - 2 * bit for bit in low]
        self.partner = [{"dp": me + flip * (1 << bit)} for bit, flip in enumerate(self.flip)]
        self.eighth = lax.rem(me, 8)
        self.copies = {}

    def view(self, weight, eighth, own=False):
        query, mixer, expand, reduce = self.refs
        width = mixer.shape[0]
        half, wide = width // 2, 2 * width

        def rows(first, size):
            return pl.ds(pl.multiple_of(first + eighth * size, 16), size)

        if weight == 0:
            return query.at[:, rows(0, width // 8), slice(0, half) if own else slice(half, width)]
        if weight == 1:
            return mixer.at[rows(0 if own else half, half // 8)]
        if weight == 2:
            return expand.at[rows(0, width // 8), slice(0, wide) if own else slice(wide, 2 * wide)]
        return reduce.at[rows(0 if own else wide, wide // 8)]

    def send(self, weight, place, eighth, device, own=False):
        send_sems, recv_sems = self.sems
        copy = remote(
            self.view(weight, eighth, own), self.view(weight, eighth),
            send_sems.at[weight, place], recv_sems.at[weight, place], device,
        )
        copy.start()
        self.copies[weight, place] = copy

    def eighths(self, weight):
        first, second = (2, 1) if weight == 2 else (1, 2)
        at_first = self.eighth + self.flip[first] * (1 << first)
        at_second = self.eighth + self.flip[second] * (1 << second)
        both = at_first + self.flip[second] * (1 << second)
        return first, second, (self.eighth, at_first, at_second, both)

    def advance(self, weight, event):
        first, second, pieces = self.eighths(weight)
        if event == 0:
            self.send(weight, 0, pieces[0], {"mod": 1 - self.mod}, own=True)
        elif event == 1:
            self.copies[weight, 0].wait_recv()
            self.send(weight, 1, pieces[0], self.partner[first])
            self.send(weight, 2, pieces[0], self.partner[second])
            self.send(weight, 4, pieces[0], self.partner[0])
        elif event == 2:
            self.copies[weight, 1].wait_recv()
            self.send(weight, 3, pieces[1], self.partner[second])
            self.send(weight, 5, pieces[1], self.partner[0])
        elif event == 3:
            self.copies[weight, 2].wait_recv()
            self.send(weight, 6, pieces[2], self.partner[0])
            self.copies[weight, 3].wait_recv()
            self.send(weight, 7, pieces[3], self.partner[0])
        else:
            for place in range(4, 8):
                self.copies[weight, place].wait_recv()

    def finish(self):
        for copy in self.copies.values():
            copy.wait_send()


class Gather:
    def __init__(self, ref, me, mod, bits, sems):
        self.ref, self.sems, self.copies, self.done = ref, sems, [], False
        self.me, self.mod, self.flip = me, mod, [1 - 2 * bit for bit in ring_bits(me, bits)]

    def advance(self):
        stage = len(self.copies)
        if self.done:
            return
        if stage:
            self.copies[-1].wait_recv()
        if stage > len(self.flip):
            self.done = True
            return
        if stage == 0:
            view, device = self.ref.at[self.me, self.mod], {"mod": 1 - self.mod}
        else:
            size = 1 << (stage - 1)
            view = self.ref.at[pl.ds(self.me // size * size, size)]
            device = {"dp": self.me + self.flip[stage - 1] * size}
        copy = remote(view, view, self.sems[0].at[stage], self.sems[1].at[stage], device)
        copy.start()
        self.copies.append(copy)

    def finish(self):
        for copy in self.copies:
            copy.wait_send()


def contrast_into(gathered_ref, pooled_ref, grad_ref, loss_ref, pool_ref, me, mod, items):
    count = gathered_ref.shape[0]
    width = pooled_ref.shape[2]
    total = items * count
    for half in range(2):
        for n in range(items):
            for part in range(width // 128):
                pooled_ref[half, n * count : (n + 1) * count, part * 128 : (part + 1) * 128] = gathered_ref[
                    :, half, n * (width // 128) + part, :
                ]
    flags = [gathered_ref[:, 0, items * (width // 128) + n, :][:, 0:1] for n in range(items)]
    present = jnp.concatenate(flags, axis=0)
    same = lax.broadcasted_iota(jnp.int32, (total, total), 0) == lax.broadcasted_iota(jnp.int32, (total, total), 1)
    same = jnp.where(same, 1.0, 0.0)
    present_row = column_sum(present * same)
    scale = LOGIT_SCALE / width
    units, inverses = [], []
    for half in range(2):
        pooled = pooled_ref[half]
        inverses.append(lax.rsqrt(jnp.mean(pooled * pooled, axis=-1, keepdims=True) + 1e-06))
        units.append(pooled * inverses[-1])
    exact = lax.Precision.HIGHEST
    logits = lax.dot_general(units[0], units[1], LAST, precision=exact, preferred_element_type=F32) * scale
    by_row = logits - 10000.0 * (1.0 - present_row)
    by_column = logits - 10000.0 * (1.0 - present)
    row_top = jnp.max(by_row, axis=1, keepdims=True)
    column_top = jnp.max(by_column, axis=0, keepdims=True)
    by_row = jnp.exp(by_row - row_top)
    by_column = jnp.exp(by_column - column_top)
    row_sum = jnp.sum(by_row, axis=1, keepdims=True)
    column_total = column_sum(by_column)
    row_part = present * (row_top + jnp.log(row_sum) - 2.0 * jnp.sum(logits * same, axis=1, keepdims=True))
    column_part = present_row * (column_top + jnp.log(column_total))
    loss = (jnp.sum(row_part) + jnp.sum(column_part)) / (2.0 * total)
    loss_ref[...] = jnp.full(loss_ref.shape, loss, F32)
    grad_logits = (
        present * by_row / row_sum + present_row * by_column / column_total - 2.0 * same * present
    ) * (scale / (2.0 * total))

    def own(half, grad_unit):
        unit = units[half]
        grad_ref[...] = inverses[half] * (grad_unit - unit * jnp.mean(grad_unit * unit, axis=-1, keepdims=True))

    @pl.when(mod == 0)
    def _():
        own(0, jnp.dot(grad_logits, units[1], precision=exact, preferred_element_type=F32))

    @pl.when(mod == 1)
    def _():
        own(1, lax.dot_general(grad_logits, units[0], FIRST, precision=exact, preferred_element_type=F32))

    for n in range(items):
        pool_ref[n : n + 1, :] = grad_ref[pl.ds(n * count + me, 1), :]


def forward_kernel(
    tokens_ref, dist_ref, slope_ref, cross_slope_ref, gain_ref, norms_ref, cross_gain_ref, present_ref, cotangent_ref,
    project_hbm, mixer_hbm, expand_hbm, reduce_hbm,
    query_hbm, keyval_hbm, cmixer_hbm, cexpand_hbm, creduce_hbm,
    encoded_out, joined_out, normed_out, rows_out, probs_out, mixed_out, resid_out, normed_two_out, hidden_out, slope_out,
    part_out, query_in_out, keyval_in_out, cnormed_out, cmixed_out, chidden_out, branch_out, cgexp_out, cgattn_out,
    gq_out, gkv_out,
    gains_ref, loss_ref, pool_ref,
    project_ref, mixer_ref, expand_ref, reduce_ref,
    cquery_ref, cmixer_ref, cexpand_ref, creduce_ref,
    encoded_ref, partner_ref, normed_ref, rows_ref, probs_ref, mixed_ref, resid_ref, normed_two_ref, hidden_ref,
    slope_keep_ref,
    q_ref, kv_ref, cprobs_ref, cmixed_ref, cresid_ref, chidden_ref, cgexp_ref, query_in_ref, keyval_in_ref, cnormed_ref,
    branch_ref, cgattn_ref, gq_ref, gkv_ref, gmix_ref, gin_ref, part_ref, joined_ref,
    gathered_ref, pooled_ref, grad_ref,
    load_sems, out_sems, weight_sends, weight_recvs, gather_sends, gather_recvs, swap_sends, swap_recvs,
):
    items, patches, width = tokens_ref.shape
    half, wide = width // 2, 2 * width
    count = gathered_ref.shape[0]
    bits = count.bit_length() - 1
    me, mod = lax.axis_index("dp"), lax.axis_index("mod")
    is_radar = mod == 1
    across = {"mod": 1 - mod}
    loads = [
        pltpu.make_async_copy(source, target, load_sems.at[i])
        for i, (source, target) in enumerate(
            (
                (project_hbm, project_ref),
                (query_hbm, cquery_ref.at[0, :, 0:half]),
                (keyval_hbm, cquery_ref.at[1:3, :, 0:half]),
                (cmixer_hbm, cmixer_ref.at[0:half]),
                (cexpand_hbm, cexpand_ref.at[:, 0:wide]),
                (creduce_hbm, creduce_ref.at[0:wide]),
                (mixer_hbm, mixer_ref),
                (expand_hbm, expand_ref),
                (reduce_hbm, reduce_ref),
            )
        )
    ]
    begin(loads)
    weights = Weights((cquery_ref, cmixer_ref, cexpand_ref, creduce_ref), me, mod, (weight_sends, weight_recvs))
    gather = Gather(gathered_ref, me, mod, bits, (gather_sends, gather_recvs))
    outputs = Outputs(out_sems)
    swaps = {}

    def swap(key, source, target):
        place = len(swaps)
        swaps[key] = remote(source, target, swap_sends.at[place], swap_recvs.at[place], across)
        swaps[key].start()

    barrier = pltpu.get_barrier_semaphore()
    others = [across] + [{"dp": me + flip * (1 << bit)} for bit, flip in enumerate(gather.flip)]
    for device in others:
        pl.semaphore_signal(barrier, inc=1, device_id=device, device_id_type=pl.DeviceIdType.MESH)
    pl.semaphore_wait(barrier, len(others))

    def pump(*events):
        for event in events:
            weights.advance(*event)

    def encode_image(n, pumps):
        def put(key, source, target):
            outputs.emit(key, source, target.at[n])

        tokens = tokens_ref[n].astype(F32)
        unit, _ = norm_rows(tokens)
        outputs.ready("normed", "rows")
        normed_ref[...] = (unit * gain_ref[0:1, :]).astype(BF16)
        put("normed", normed_ref, normed_out)
        if n == 0:
            loads[0].wait()
        for part in range(3):
            cut = slice(part * width, (part + 1) * width)
            rows_ref[:, cut] = dot(normed_ref[...], project_ref[:, cut]).astype(BF16)
        put("rows", rows_ref, rows_out)
        if n == 0:
            finish(loads[1:6])
        pump(*pumps[0])
        outputs.ready("probs", "mixed")
        attend(
            rows_ref, rows_ref, rows_ref, (0, width, 2 * width), dist_ref.at[n], slope_ref, probs_ref, mixed_ref
        )
        put("probs", probs_ref, probs_out)
        put("mixed", mixed_ref, mixed_out)
        pump(*pumps[1])
        if n == 0:
            loads[6].wait()
        outputs.ready("resid", "normed_two")
        resid = tokens_ref[n].astype(F32) + dot(mixed_ref[...], mixer_ref[...])
        resid_ref[...] = resid
        unit, _ = norm_rows(resid)
        normed_two_ref[...] = (unit * gain_ref[1:2, :]).astype(BF16)
        put("resid", resid_ref, resid_out)
        put("normed_two", normed_two_ref, normed_two_out)
        if n == 0:
            finish(loads[7:9])
        outputs.ready("hidden", "slope")
        for part in range(expand_ref.shape[1] // width):
            cut = slice(part * width, (part + 1) * width)
            value, slope = gelu_pair(dot(normed_two_ref[...], expand_ref[:, cut]))
            hidden_ref[:, cut] = value.astype(BF16)
            slope_keep_ref[:, cut] = slope.astype(BF16)
        put("hidden", hidden_ref, hidden_out)
        put("slope", slope_keep_ref, slope_out)
        pump(*pumps[2])
        encoded = (resid_ref[...] + dot(hidden_ref[...], reduce_ref[...])).astype(BF16)
        encoded_ref[n] = encoded
        put(("encoded", n), encoded_ref.at[n], encoded_out)
        swap(n, encoded_ref.at[n], partner_ref.at[n])
        pooled = jnp.mean(encoded.astype(F32), axis=0, keepdims=True)
        if n == 0:
            gathered_ref[me, mod] = jnp.zeros(gathered_ref.shape[2:], F32)
        for part in range(width // 128):
            place = n * (width // 128) + part
            gathered_ref[me, mod, place : place + 1, :] = pooled[:, part * 128 : (part + 1) * 128]
        place = items * (width // 128) + n
        gathered_ref[me, mod, place : place + 1, :] = jnp.full((1, 128), present_ref[n], jnp.int32).astype(F32)
        pump(*pumps[3])

    encode_image(0, (((0, 0), (1, 0), (2, 0), (3, 0)), ((0, 1), (1, 1)), ((0, 2), (1, 2)), ()))
    encode_image(1, (((2, 1),), ((3, 1), (0, 3), (1, 3)), ((2, 2),), ((3, 2),)))
    gather.advance()

    def join_image(n, pumps):
        def put(key, source, target):
            outputs.emit(key, source, target.at[n])

        swaps[n].wait_recv()
        own, other = encoded_ref[n], partner_ref[n]
        unit, _ = norm_rows(jnp.where(is_radar, own, other).astype(F32))
        outputs.ready("query_in", "keyval_in")
        query_in_ref[...] = (unit * norms_ref[1:2, :]).astype(BF16)
        unit, _ = norm_rows(jnp.where(is_radar, other, own).astype(F32))
        keyval_in_ref[...] = (unit * norms_ref[0:1, :]).astype(BF16)
        put("query_in", query_in_ref, query_in_out)
        put("keyval_in", keyval_in_ref, keyval_in_out)
        pump(*pumps[0])
        q_ref[...] = dot(query_in_ref[...], cquery_ref[0]).astype(BF16)
        for part in range(2):
            kv_ref[:, part * width : (part + 1) * width] = dot(keyval_in_ref[...], cquery_ref[1 + part]).astype(BF16)
        gather.advance()
        starts = (0, 0, width)
        outputs.ready("cmixed")
        attend(q_ref, kv_ref, kv_ref, starts, dist_ref.at[n], cross_slope_ref, cprobs_ref, cmixed_ref)
        put("cmixed", cmixed_ref.at[:, 0:half], cmixed_out)
        gather.advance()
        radar = jnp.where(is_radar, encoded_ref[n], partner_ref[n]).astype(F32)
        resid = radar + dot(cmixed_ref[...], cmixer_ref[...])
        cresid_ref[...] = resid
        unit, _ = norm_rows(resid)
        outputs.ready("cnormed", "branch")
        cnormed_ref[...] = (unit * cross_gain_ref[...]).astype(BF16)
        put("cnormed", cnormed_ref, cnormed_out)
        present = present_ref[n].astype(F32)
        branch_ref[...] = (present * cotangent_ref[n].astype(F32)).astype(BF16)
        put("branch", branch_ref, branch_out)
        pump(*pumps[1])
        outputs.ready("chidden", "cgexp")
        for part in range(cexpand_ref.shape[1] // width):
            cut = slice(part * width, (part + 1) * width)
            value, slope = gelu_pair(dot(cnormed_ref[...], cexpand_ref[:, cut]))
            chidden_ref[:, cut] = value.astype(BF16)
            upstream = dot_last(branch_ref[...], creduce_ref[cut, :])
            cgexp_ref[:, cut] = (upstream * slope).astype(BF16)
        put("chidden", chidden_ref.at[:, 0:wide], chidden_out)
        put("cgexp", cgexp_ref.at[:, 0:wide], cgexp_out)

        @pl.when(mod == n)
        def _():
            joined_ref[...] = (present * (cresid_ref[...] + dot(chidden_ref[...], creduce_ref[...]))).astype(BF16)

        if n == items - 1:
            swap("joined", joined_ref, joined_out.at[mod])
            outputs.emit("joined", joined_ref, joined_out.at[mod])
        gather.advance()
        grad_normed = dot_last(cgexp_ref[...], cexpand_ref[...])
        unit, inverse = norm_rows(cresid_ref[...])
        own_gain = jnp.where(mod == n, 1.0, 0.0) * column_sum(grad_normed * unit)
        gains_ref[1:2, :] = own_gain if n == 0 else gains_ref[1:2, :] + own_gain
        grad = present * cotangent_ref[n].astype(F32) + norm_back(grad_normed, unit, inverse, cross_gain_ref[...])
        outputs.ready("part", "cgattn")
        part_ref[...] = grad
        cgattn_ref[...] = grad.astype(BF16)
        put("cgattn", cgattn_ref, cgattn_out)
        gmix_ref[...] = dot_last(cgattn_ref[...], cmixer_ref[...]).astype(BF16)
        gather.advance()
        outputs.ready("gq", "gkv")
        attend_back(q_ref, kv_ref, kv_ref, starts, cprobs_ref, gmix_ref, (gq_ref, gkv_ref, gkv_ref), (0, 0, width))
        put("gq", gq_ref.at[:, 0:half], gq_out)
        outputs.emit("gkv", gkv_ref.at[:, 0:half], gkv_out.at[n, :, 0:half])
        outputs.emit("gkv", gkv_ref.at[:, width : width + half], gkv_out.at[n, :, half:width])
        gather.advance()

        @pl.when(is_radar)
        def _():
            gin_ref[...] = dot_last(gq_ref[...], cquery_ref[0])

        @pl.when(mod == 0)
        def _():
            gin_ref[...] = dot_last(gkv_ref[:, 0:width], cquery_ref[1]) + dot_last(gkv_ref[:, width:], cquery_ref[2])

        gain = jnp.where(is_radar, norms_ref[1:2, :], norms_ref[0:1, :])
        unit, inverse = norm_rows(encoded_ref[n].astype(F32))
        grad_in = gin_ref[...]
        sums = column_sum(grad_in * unit)
        gains_ref[0:1, :] = sums if n == 0 else gains_ref[0:1, :] + sums
        part_ref[...] = jnp.where(is_radar, part_ref[...], 0.0) + norm_back(grad_in, unit, inverse, gain)
        put("part", part_ref, part_out)

    join_image(0, (((0, 4), (1, 4)), ((2, 3), (3, 3), (2, 4), (3, 4))))
    join_image(1, ((), ()))
    while not gather.done:
        gather.advance()
    contrast_into(gathered_ref, pooled_ref, grad_ref, loss_ref, pool_ref, me, mod, items)
    swaps["joined"].wait_recv()
    for copy in swaps.values():
        copy.wait_send()
    weights.finish()
    gather.finish()
    outputs.finish()


def forward(tokens, dist, slopes, cross_slopes, gains, norms, cross_gain, present, cotangent, weights, cross, count):
    items, patches, width = tokens.shape
    half, wide, full = width // 2, 2 * width, 4 * width
    bits = count.bit_length() - 1
    pairs = HEADS // 2

    def out(*dims, dtype=BF16):
        return shape((items, patches, *dims), dtype)

    outs = (
        out(width), out(width), out(width), out(3 * width), shape((items, pairs, patches, 2 * patches), BF16), out(width),
        out(width, dtype=F32), out(width), out(full), out(full),
        out(width, dtype=F32), out(width), out(width), out(width), out(half), out(wide), out(width), out(wide), out(width),
        out(half), out(width),
    )
    row = (patches, width)
    narrow = [row, (patches, 3 * width), (pairs, patches, 2 * patches), row]
    scratch = [pltpu.VMEM(w.shape, BF16) for w in weights]
    scratch += [pltpu.VMEM(d, BF16) for d in ((3, width, width), (width, width), (width, full), (full, width))]
    scratch += [pltpu.VMEM((items, *row), BF16)] * 2
    scratch += [pltpu.VMEM(d, BF16) for d in narrow]
    scratch += [pltpu.VMEM(row, F32), pltpu.VMEM(row, BF16), pltpu.VMEM((patches, full), BF16), pltpu.VMEM((patches, full), BF16)]
    scratch += [pltpu.VMEM(d, BF16) for d in (row, (patches, wide), (pairs, patches, 2 * patches), row)]
    scratch += [pltpu.VMEM(row, F32), pltpu.VMEM((patches, full), BF16), pltpu.VMEM((patches, full), BF16)]
    scratch += [pltpu.VMEM(row, BF16)] * 5
    scratch += [pltpu.VMEM(row, BF16), pltpu.VMEM((patches, wide), BF16), pltpu.VMEM(row, BF16)]
    scratch += [pltpu.VMEM(row, F32), pltpu.VMEM(row, F32), pltpu.VMEM(row, BF16)]
    scratch += [
        pltpu.VMEM((count, 2, 16, 128), F32),
        pltpu.VMEM((2, items * count, width), F32),
        pltpu.VMEM((items * count, width), F32),
    ]
    dma = pltpu.SemaphoreType.DMA
    scratch += [dma((9,)), dma((2 * 24 + 4,)), dma((4, 8)), dma((4, 8)), dma((bits + 1,)), dma((bits + 1,)), dma((3,)), dma((3,))]
    return pl.pallas_call(
        forward_kernel,
        out_shape=outs + (shape((2, width), F32), shape((8, 128), F32), shape((items, width), F32)),
        in_specs=[VMEM, VMEM, SMEM, SMEM, VMEM, VMEM, VMEM, SMEM, VMEM] + [ANY] * 9,
        out_specs=(ANY,) * len(outs) + (VMEM,) * 3,
        scratch_shapes=scratch,
        compiler_params=pltpu.CompilerParams(
            collective_id=1, has_side_effects=True, vmem_limit_bytes=62 * 1024 * 1024
        ),
        cost_estimate=cost(items * patches * 40 * width * width, 60 * 2**20),
        name="forward",
    )(tokens, dist, slopes, cross_slopes, gains, norms, cross_gain, present, cotangent, *weights, *cross)


def sum_kernel(plan, results, orders, sizes, *refs):
    n_in, n_out, slots = sizes
    inputs, vector_ref = refs[:n_in], refs[n_in]
    outs, vector_out = refs[n_in + 1 : n_in + 1 + n_out], refs[n_in + 1 + n_out]
    scratch = refs[n_in + 2 + n_out :]
    bits = len(orders[0])
    held, got = scratch[:bits], scratch[bits : 2 * bits]
    vector_held, vector_got = scratch[2 * bits : 3 * bits - 1], scratch[3 * bits - 1 : 4 * bits - 1]
    send_sems, recv_sems = scratch[4 * bits - 1 :]
    me = lax.axis_index("dp")
    mine = ring_bits(me, bits)
    partners = [me + (1 - 2 * mine[bit]) * (1 << bit) for bit in range(bits)]
    barrier = pltpu.get_barrier_semaphore()
    for partner in partners:
        pl.semaphore_signal(barrier, inc=1, device_id={"dp": partner}, device_id_type=pl.DeviceIdType.MESH)
    pl.semaphore_wait(barrier, bits)
    every = list(range(bits))[::-1]
    total = len(plan)
    block = outs[0].shape[0]
    copies = {}

    def left_at(chunk, stage):
        done = orders[chunk][:stage]
        return [bit for bit in every if bit not in done]

    def source(chunk, stage):
        if chunk == total:
            return vector_ref if stage == 0 else vector_held[stage - 1]
        return held[stage].at[chunk % slots]

    def target(chunk, stage):
        return vector_got[stage] if chunk == total else got[stage].at[chunk]

    def send(chunk, stage):
        bit = orders[chunk][stage]
        copy = pltpu.make_async_remote_copy(
            src_ref=side_of(source(chunk, stage), left_at(chunk, stage), bit, 1 - mine[bit]),
            dst_ref=target(chunk, stage),
            send_sem=send_sems.at[stage, chunk],
            recv_sem=recv_sems.at[stage, chunk],
            device_id={"dp": partners[bit]},
            device_id_type=pl.DeviceIdType.MESH,
        )
        copy.start()
        copies[chunk, stage] = copy

    def free(chunk, stage):
        if chunk >= 0:
            copies[chunk, stage].wait_send()

    def make(chunk):
        free(chunk - slots, 0)
        for lefts, rights, cut, place in plan[chunk]:
            product = None
            for one, other in zip(lefts, rights):
                term = dot_first(inputs[one][...], inputs[other][:, cut[0] : cut[1]])
                product = term if product is None else product + term
            product = product.astype(BF16)
            for index in range(1 << bits):
                where = tuple((index >> bit) & 1 for bit in every)
                held[0][(chunk % slots, *where, slice(None), slice(place, place + cut[1] - cut[0]))] = product[
                    index * block : (index + 1) * block
                ]

    def take(chunk, stage):
        bit = orders[chunk][stage]
        copies[chunk, stage].wait_recv()
        kept = side_of(source(chunk, stage), left_at(chunk, stage), bit, mine[bit])
        if chunk == total:
            value = kept[...] + target(chunk, stage)[...]
            (vector_out if stage == bits - 1 else vector_held[stage])[...] = value
        elif stage == bits - 1:
            out, place = results[chunk]
            width = got[stage].shape[-1]
            outs[out][:, place : place + width] = kept[...].astype(F32) + target(chunk, stage)[...].astype(F32)
        else:
            free(chunk - slots, stage + 1)
            held[stage + 1][chunk % slots] = kept[...] + target(chunk, stage)[...]

    for step in range(total + 1 + bits):
        if step < total:
            make(step)
        if step <= total:
            send(step, 0)
        for stage in range(bits):
            chunk = step - 1 - stage
            if 0 <= chunk <= total:
                take(chunk, stage)
                if stage < bits - 1:
                    send(chunk, stage + 1)
    for stage in range(bits):
        for chunk in range(max(0, total - slots), total):
            free(chunk, stage)
        free(total, stage)


def summed_products(inputs, plan, results, widths, vector, count):
    bits = count.bit_length() - 1
    rows = inputs[0].shape[1]
    block, total, slots = rows // count, len(plan), 3
    orders = [tuple(range(bits))] * (total + 1)
    two = (2,) * bits
    return pl.pallas_call(
        functools.partial(sum_kernel, plan, results, orders, (len(inputs), len(widths), slots)),
        out_shape=tuple(shape((block, width), F32) for width in widths) + (shape(vector.shape[bits:], F32),),
        in_specs=[VMEM] * (len(inputs) + 1),
        out_specs=(VMEM,) * (len(widths) + 1),
        scratch_shapes=[pltpu.VMEM((slots, *two[stage:], block, rows), BF16) for stage in range(bits)]
        + [pltpu.VMEM((total, *two[stage + 1 :], block, rows), BF16) for stage in range(bits)]
        + [pltpu.VMEM(vector.shape[stage:], F32) for stage in range(1, bits)]
        + [pltpu.VMEM(vector.shape[stage:], F32) for stage in range(1, bits + 1)]
        + [pltpu.SemaphoreType.DMA((bits, total + 1))] * 2,
        compiler_params=pltpu.CompilerParams(
            collective_id=0, has_side_effects=True, vmem_limit_bytes=62 * 1024 * 1024
        ),
        cost_estimate=cost(total * rows * rows * 512, 48 * 2**20),
        name="sum_products",
    )(*inputs, vector)


def flipped(array, axis, bit):
    return lax.ppermute(array, axis, [(i, i ^ (1 << bit)) for i in range(lax.axis_size(axis))])


def block_order(width, count):
    bits = count.bit_length() - 1
    block = width // count
    rows = jnp.arange(width)
    place = rows // block
    partner = jnp.zeros_like(place)
    for bit in range(bits):
        partner = partner | (((place >> (bits - 1 - bit)) & 1) << bit)
    source = (lax.axis_index("dp") ^ partner) * block + rows % block
    return (source[:, None] == jnp.arange(width)[None, :]).astype(BF16)


def ordered(order, values):
    flat = jnp.concatenate(values, axis=0)
    return jnp.einsum("jd,rd->jr", order, flat, preferred_element_type=F32).astype(BF16)


def summed(left_rows, grad_rows):
    count = lax.axis_size("dp")
    flat = jnp.concatenate(grad_rows, axis=0)
    half = left_rows.shape[0] // 2
    send = jnp.dot(left_rows[half:], flat, preferred_element_type=F32).astype(BF16)
    keep = jnp.dot(left_rows[:half], flat, preferred_element_type=F32).astype(BF16)
    bits = count.bit_length() - 1
    for bit in range(bits):
        got = flipped(send, "dp", bit)
        if bit == bits - 1:
            return keep.astype(F32) + got.astype(F32)
        half = half // 2
        send = (keep[half:].astype(F32) + got[half:].astype(F32)).astype(BF16)
        keep = (keep[:half].astype(F32) + got[:half].astype(F32)).astype(BF16)


def summed_blocks(blocks):
    bits = lax.axis_size("dp").bit_length() - 1
    for bit in range(bits):
        half = blocks.shape[0] // 2
        blocks = blocks[:half] + flipped(blocks[half:], "dp", bit)
    return blocks[0]


def all_summed(products, blocks):
    count = blocks.shape[0]
    rows = products[0][0][0].shape[1]
    if count != 16 or (rows // count) % 16:
        order = block_order(rows, count)
        sums = [summed(ordered(order, lefts), rights) for lefts, rights in products]
        wanted = jnp.dot(order[:: rows // count, :: rows // count].astype(F32), blocks.reshape(count, -1),
                         precision=lax.Precision.HIGHEST)
        return (*sums, summed_blocks(wanted.reshape(blocks.shape)))
    inputs, plan, results, widths, fill = [], [], [], [], 0
    for lefts, rights in products:
        first = len(inputs)
        inputs.extend([*lefts, *rights])
        left = tuple(range(first, first + len(lefts)))
        right = tuple(range(first + len(lefts), len(inputs)))
        width = rights[0].shape[1]
        if width < rows:
            if not fill:
                plan.append([])
                results.append((len(widths), 0))
                widths.append(rows)
            plan[-1].append((left, right, (0, width), fill))
            fill = (fill + width) % rows
            continue
        for start in range(0, width, rows):
            plan.append([(left, right, (start, start + rows), 0)])
            results.append((len(widths), start))
        widths.append(width)
    vector = jnp.pad(blocks, ((0, 0), (0, 8 - blocks.shape[1]), (0, 128 - blocks.shape[2])))
    vector = vector.reshape((2,) * (count.bit_length() - 1) + vector.shape[1:])
    *sums, vector_sum = summed_products(inputs, plan, results, widths, vector, count)
    both = sums.pop(2)
    sums[2:2] = [both[:, : rows // 2], both[:, rows // 2 :]]
    return (*sums, vector_sum[: blocks.shape[1], : blocks.shape[2]])


def shards(
    patch_tokens,
    grid_coords,
    has_radar,
    enc_gains,
    enc_project,
    enc_mixer,
    enc_expand,
    enc_reduce,
    cross_norms,
    cross_gain,
    cross_query,
    cross_keyval,
    cross_mixer,
    cross_expand,
    cross_reduce,
    enc_cotangent,
    joined_cotangent,
):
    item_count, patches, model_width = patch_tokens.shape[1:]
    images = range(item_count)
    half_index = lax.axis_index("mod")
    dp_size = lax.axis_size("dp")
    weights = (enc_project[0], enc_mixer[0], enc_expand[0], enc_reduce[0])
    cross_weights = (cross_query, cross_keyval, cross_mixer, cross_expand, cross_reduce)

    grid = grid_coords.astype(F32)
    across = grid[:, 0, :, None] - grid[:, 0, None, :]
    upward = grid[:, 1, :, None] - grid[:, 1, None, :]
    distance = jnp.sqrt(across * across + upward * upward)
    heads = jnp.arange(HEADS)
    slopes = jnp.exp2(-8.0 * (heads + 1).astype(F32) / HEADS)
    cross_heads = (heads + half_index * (HEADS // 2)) % HEADS
    cross_slopes = jnp.exp2(-8.0 * (cross_heads + 1).astype(F32) / HEADS)

    (encoded, joined_tokens, normed, rows, probs, mixed, resid, normed_two, hidden, slope,
     part, query_in, keyval_in, cnormed, cmixed, chidden, branch, cgexp, cgattn, gq, gkv,
     cross_gains, loss, pool_grad) = forward(
        patch_tokens[0], distance, slopes, cross_slopes, enc_gains[0], cross_norms, cross_gain[None], has_radar,
        joined_cotangent, weights, cross_weights, dp_size,
    )

    def each(values):
        return [values[n] for n in images]

    backward = [
        encode_back(
            enc_cotangent[0, n], part[n], pool_grad[n : n + 1], enc_gains[0], patch_tokens[0, n],
            resid[n], slope[n], rows[n], probs[n], *weights,
        )
        for n in images
    ]
    own_gain = cross_gains[1:2]
    own_gain = own_gain + flipped(own_gain, "mod", 0)
    vectors = jnp.concatenate([backward[0][5] + backward[1][5], cross_gains[:1], own_gain])
    block = model_width // dp_size
    blocks = jnp.moveaxis(vectors.reshape(4, dp_size, block), 1, 0)

    def back(place):
        return [backward[n][place] for n in images]

    products = (
        (each(branch), each(chidden)),
        (each(cnormed), each(cgexp)),
        (each(query_in), each(gq)),
        (each(cgattn), each(cmixed)),
        (each(keyval_in), each(gkv)),
        (back(1), each(hidden)),
        (each(normed_two), back(2)),
        (each(mixed), back(3)),
        (each(normed), back(4)),
    )
    (creduce_sum, cexpand_sum, query_sum, cmixer_sum, keyval_sum, reduce_sum, expand_sum, mixer_sum, project_sum,
     vector_sum) = all_summed(products, blocks)
    width = model_width // 2
    return (
        encoded[None],
        joined_tokens,
        loss[0, 0],
        jnp.stack(back(0))[None],
        vector_sum[None, :2],
        project_sum[None],
        mixer_sum[None],
        expand_sum[None],
        reduce_sum.T[None],
        vector_sum[2:3],
        vector_sum[3],
        query_sum,
        jnp.stack([keyval_sum[:, :width], keyval_sum[:, width:]]),
        cmixer_sum.T,
        cexpand_sum,
        creduce_sum.T,
    )


def solution(mesh):
    placed = (
        P("mod", "dp", None, None),
        P("dp", None, None),
        P("dp"),
        P("mod", None, None),
        P("mod", None, None),
        P("mod", None, None),
        P("mod", None, None),
        P("mod", None, None),
        P(),
        P(),
        P(None, "mod"),
        P(None, None, "mod"),
        P("mod", None),
        P(None, "mod"),
        P("mod", None),
        P("mod", "dp", None, None),
        P("dp", None, None),
    )
    return jax.shard_map(
        shards,
        mesh=mesh,
        in_specs=placed,
        out_specs=(
            P("mod", "dp", None, None),
            P("dp", None, None),
            P(),
            P("mod", "dp", None, None),
            P("mod", None, "dp"),
            P("mod", "dp", None),
            P("mod", "dp", None),
            P("mod", "dp", None),
            P("mod", None, "dp"),
            P("mod", "dp"),
            P("dp"),
            P("dp", "mod"),
            P(None, "dp", "mod"),
            P("mod", "dp"),
            P("dp", "mod"),
            P("mod", "dp"),
        ),
        check_vma=False,
    )
```

```python
import functools

import jax
import jax.numpy as jnp
from jax import lax
from jax.experimental import pallas as pl
from jax.experimental.pallas import tpu as pltpu
from jax.sharding import PartitionSpec as P

HEADS = 12
HEAD_DIM = 64
LOGIT_SCALE = 50.0
F32 = jnp.float32
BF16 = jnp.bfloat16
PAIR = 2 * HEAD_DIM
LAST = (((1,), (1,)), ((), ()))
FIRST = (((0,), (0,)), ((), ()))
VMEM = pl.BlockSpec(memory_space=pltpu.VMEM)
SMEM = pl.BlockSpec(memory_space=pltpu.SMEM)
ANY = pl.BlockSpec(memory_space=pl.ANY)


def dot(left, right):
    return jnp.dot(left, right, preferred_element_type=F32)


def dot_last(left, right):
    return lax.dot_general(left, right, LAST, preferred_element_type=F32)


def dot_first(left, right):
    return lax.dot_general(left, right, FIRST, preferred_element_type=F32)


def norm_rows(values):
    centre = values - jnp.mean(values, axis=-1, keepdims=True)
    inverse = lax.rsqrt(jnp.mean(centre * centre, axis=-1, keepdims=True) + 1e-06)
    return centre * inverse, inverse


def norm_back(grad_out, unit, inverse, gain):
    weighted = grad_out * gain
    return inverse * (
        weighted
        - jnp.mean(weighted, axis=-1, keepdims=True)
        - unit * jnp.mean(weighted * unit, axis=-1, keepdims=True)
    )


def column_sum(values):
    return jnp.sum(values, axis=0, keepdims=True)


def gelu_pair(values):
    root = 0.7978845608028654
    square = values * values
    tanh = jnp.tanh(values * (root + (root * 0.044715) * square))
    half = 0.5 + 0.5 * tanh
    slope = half + (0.5 * values) * (1.0 - tanh * tanh) * (root + (3.0 * root * 0.044715) * square)
    return values * half, slope


def stacked(pair, low):
    zero = jnp.zeros_like(pair)
    return jnp.concatenate([jnp.where(low, pair, zero), jnp.where(low, zero, pair)], axis=0)


def side_by_side(values):
    rows = values.shape[0] // 2
    return jnp.concatenate([values[:rows], values[rows:]], axis=1)


def lanes(first, index):
    return pl.ds(pl.multiple_of(first + index * PAIR, PAIR), PAIR)


def attend(q_ref, k_ref, v_ref, starts, dist_ref, first_head, probs_ref, mixed_ref):
    patches = dist_ref.shape[0]
    low = lax.broadcasted_iota(jnp.int32, (patches, PAIR), 1) < HEAD_DIM
    scale = jnp.asarray(HEAD_DIM**-0.5, BF16)

    def one(index, carry):
        queries = stacked(q_ref[:, lanes(starts[0], index)] * scale, low)
        keys = k_ref[:, lanes(starts[1], index)]
        values = stacked(v_ref[:, lanes(starts[2], index)], low)
        scores = dot_last(queries, keys)
        distance = dist_ref[...]
        halves = []
        for side in range(2):
            head = lax.rem(2 * index + side + first_head, HEADS)
            power = jnp.full((1, patches), head + 1, jnp.int32).astype(F32) * (-8.0 / HEADS)
            part = scores[side * patches : (side + 1) * patches] - jnp.exp2(power) * distance
            part = jnp.exp(part - jnp.max(part, axis=-1, keepdims=True))
            part = part * (1.0 / jnp.sum(part, axis=-1, keepdims=True))
            halves.append(part.astype(BF16))
        probs = jnp.concatenate(halves, axis=1)
        probs_ref[index] = probs
        mixed_ref[:, lanes(0, index)] = dot(probs, values).astype(BF16)
        return carry

    lax.fori_loop(0, HEADS // 2, one, 0)


def attend_back(q_ref, k_ref, v_ref, starts, probs_ref, grad_ref, out_refs, out_starts):
    patches = q_ref.shape[0]
    low = lax.broadcasted_iota(jnp.int32, (patches, PAIR), 1) < HEAD_DIM
    scale = jnp.asarray(HEAD_DIM**-0.5, BF16)

    def one(index, carry):
        queries = stacked(q_ref[:, lanes(starts[0], index)] * scale, low)
        keys = stacked(k_ref[:, lanes(starts[1], index)] * scale, low)
        values = v_ref[:, lanes(starts[2], index)]
        grads = stacked(grad_ref[:, lanes(0, index)], low)
        both = probs_ref[index]
        probs = jnp.concatenate([both[:, :patches], both[:, patches:]], axis=0)
        grad_probs = dot_last(grads, values)
        wide = probs.astype(F32)
        inner = jnp.sum(grad_probs * wide, axis=-1, keepdims=True)
        grad_scores = (wide * (grad_probs - inner)).astype(BF16)
        out_refs[0][:, lanes(out_starts[0], index)] = dot(side_by_side(grad_scores), keys).astype(BF16)
        out_refs[1][:, lanes(out_starts[1], index)] = dot_first(grad_scores, queries).astype(BF16)
        out_refs[2][:, lanes(out_starts[2], index)] = dot_first(probs, grads).astype(BF16)
        return carry

    lax.fori_loop(0, HEADS // 2, one, 0)


def begin(copies):
    for copy in copies:
        copy.start()


def finish(copies):
    for copy in copies:
        copy.wait()


def limits():
    return pltpu.CompilerParams(vmem_limit_bytes=60 * 1024 * 1024)


def shape(dims, dtype):
    return jax.ShapeDtypeStruct(dims, dtype)


def cost(macs, size):
    return pl.CostEstimate(flops=2 * macs, bytes_accessed=size, transcendentals=0)


def encode_back_kernel(
    cotangent_ref, part_ref, pool_ref, gain_ref, tokens_ref, resid_ref, slope_ref, rows_ref, probs_ref,
    project_hbm, mixer_hbm, expand_hbm, reduce_hbm,
    patch_ref, branch_ref, gexp_ref, gattn_ref, grows_ref, gains_ref,
    project_ref, mixer_ref, expand_ref, reduce_ref, gmix_ref, sems,
):
    copies = [
        pltpu.make_async_copy(source, target, sems.at[i])
        for i, (source, target) in enumerate(
            (
                (reduce_hbm, reduce_ref),
                (expand_hbm, expand_ref),
                (mixer_hbm, mixer_ref),
                (project_hbm, project_ref),
            )
        )
    ]
    begin(copies)
    patches, width = tokens_ref.shape
    grad = cotangent_ref[...].astype(F32) + pool_ref[...] * (1.0 / patches) + part_ref[...]
    patch_ref[...] = grad
    branch_ref[...] = grad.astype(BF16)
    copies[0].wait()
    for part in range(expand_ref.shape[1] // width):
        cut = slice(part * width, (part + 1) * width)
        upstream = dot_last(branch_ref[...], reduce_ref[cut, :])
        gexp_ref[:, cut] = (upstream * slope_ref[:, cut].astype(F32)).astype(BF16)
    copies[1].wait()
    grad_normed = dot_last(gexp_ref[...], expand_ref[...])
    unit, inverse = norm_rows(resid_ref[...])
    gains_ref[1:2, :] = column_sum(grad_normed * unit)
    grad = patch_ref[...] + norm_back(grad_normed, unit, inverse, gain_ref[1:2, :])
    patch_ref[...] = grad
    gattn_ref[...] = grad.astype(BF16)
    copies[2].wait()
    gmix_ref[...] = dot_last(gattn_ref[...], mixer_ref[...]).astype(BF16)
    starts = (0, width, 2 * width)
    attend_back(rows_ref, rows_ref, rows_ref, starts, probs_ref, gmix_ref, (grows_ref,) * 3, starts)
    copies[3].wait()
    grad_normed = dot_last(grows_ref[...], project_ref[...])
    unit, inverse = norm_rows(tokens_ref[...].astype(F32))
    gains_ref[0:1, :] = column_sum(grad_normed * unit)
    patch_ref[...] = patch_ref[...] + norm_back(grad_normed, unit, inverse, gain_ref[0:1, :])


def encode_back(cotangent, part, pool, gains, tokens, resid, slope, rows, probs, project, mixer, expand, reduce):
    patches, width = tokens.shape
    wide = expand.shape[1]
    weights = (project, mixer, expand, reduce)
    return pl.pallas_call(
        encode_back_kernel,
        out_shape=(
            shape((patches, width), F32),
            shape((patches, width), BF16),
            shape((patches, wide), BF16),
            shape((patches, width), BF16),
            shape((patches, 3 * width), BF16),
            shape((2, width), F32),
        ),
        in_specs=[VMEM] * 9 + [ANY] * 4,
        out_specs=(VMEM,) * 6,
        scratch_shapes=[pltpu.VMEM(w.shape, BF16) for w in weights]
        + [pltpu.VMEM((patches, width), BF16), pltpu.SemaphoreType.DMA((4,))],
        compiler_params=limits(),
        cost_estimate=cost(patches * sum(w.size for w in weights), 24 * 2**20),
        name="encode_back",
    )(cotangent, part, pool, gains, tokens, resid, slope, rows, probs, *weights)


def ring_bits(index, count):
    return [lax.rem(index // (1 << bit), 2) for bit in range(count)]


class Outputs:
    def __init__(self, sems):
        self.sems, self.used, self.open = sems, 0, {}

    def emit(self, key, source, target):
        copy = pltpu.make_async_copy(source, target, self.sems.at[self.used])
        self.used += 1
        copy.start()
        self.open.setdefault(key, []).append(copy)

    def ready(self, *keys):
        for key in keys:
            for copy in self.open.pop(key, []):
                copy.wait()

    def finish(self):
        self.ready(*list(self.open))


def remote(source, target, send_sem, recv_sem, device):
    return pltpu.make_async_remote_copy(
        src_ref=source,
        dst_ref=target,
        send_sem=send_sem,
        recv_sem=recv_sem,
        device_id=device,
        device_id_type=pl.DeviceIdType.MESH,
    )


class Weights:
    def __init__(self, refs, me, mod, sems):
        self.refs, self.sems, self.mod = refs, sems, mod
        low = ring_bits(me, 3)
        self.flip = [1 - 2 * bit for bit in low]
        self.partner = [{"dp": me + flip * (1 << bit)} for bit, flip in enumerate(self.flip)]
        self.eighth = lax.rem(me, 8)
        self.copies = {}

    def view(self, weight, eighth, own=False):
        query, mixer, expand, reduce = self.refs
        width = mixer.shape[0]
        half, wide = width // 2, 2 * width

        def rows(first, size):
            return pl.ds(pl.multiple_of(first + eighth * size, 16), size)

        if weight == 0:
            return query.at[:, rows(0, width // 8), slice(0, half) if own else slice(half, width)]
        if weight == 1:
            return mixer.at[rows(0 if own else half, half // 8)]
        if weight == 2:
            return expand.at[rows(0, width // 8), slice(0, wide) if own else slice(wide, 2 * wide)]
        return reduce.at[rows(0 if own else wide, wide // 8)]

    def send(self, weight, place, eighth, device, own=False):
        send_sems, recv_sems = self.sems
        copy = remote(
            self.view(weight, eighth, own), self.view(weight, eighth),
            send_sems.at[weight, place], recv_sems.at[weight, place], device,
        )
        copy.start()
        self.copies[weight, place] = copy

    def eighths(self, weight):
        first, second = (2, 1) if weight == 2 else (1, 2)
        at_first = self.eighth + self.flip[first] * (1 << first)
        at_second = self.eighth + self.flip[second] * (1 << second)
        both = at_first + self.flip[second] * (1 << second)
        return first, second, (self.eighth, at_first, at_second, both)

    def advance(self, weight, event):
        first, second, pieces = self.eighths(weight)
        if event == 0:
            self.send(weight, 0, pieces[0], {"mod": 1 - self.mod}, own=True)
        elif event == 1:
            self.copies[weight, 0].wait_recv()
            self.send(weight, 1, pieces[0], self.partner[first])
            self.send(weight, 2, pieces[0], self.partner[second])
            self.send(weight, 4, pieces[0], self.partner[0])
        elif event == 2:
            self.copies[weight, 1].wait_recv()
            self.send(weight, 3, pieces[1], self.partner[second])
            self.send(weight, 5, pieces[1], self.partner[0])
        elif event == 3:
            self.copies[weight, 2].wait_recv()
            self.send(weight, 6, pieces[2], self.partner[0])
            self.copies[weight, 3].wait_recv()
            self.send(weight, 7, pieces[3], self.partner[0])
        else:
            for place in range(4, 8):
                self.copies[weight, place].wait_recv()

    def finish(self):
        for copy in self.copies.values():
            copy.wait_send()


class Gather:
    def __init__(self, ref, me, mod, bits, sems):
        self.ref, self.sems, self.copies, self.done = ref, sems, [], False
        self.me, self.mod, self.flip = me, mod, [1 - 2 * bit for bit in ring_bits(me, bits)]

    def advance(self):
        stage = len(self.copies)
        if self.done:
            return
        if stage:
            self.copies[-1].wait_recv()
        if stage > len(self.flip):
            self.done = True
            return
        if stage == 0:
            view, device = self.ref.at[self.me, self.mod], {"mod": 1 - self.mod}
        else:
            size = 1 << (stage - 1)
            view = self.ref.at[pl.ds(self.me // size * size, size)]
            device = {"dp": self.me + self.flip[stage - 1] * size}
        copy = remote(view, view, self.sems[0].at[stage], self.sems[1].at[stage], device)
        copy.start()
        self.copies.append(copy)

    def finish(self):
        for copy in self.copies:
            copy.wait_send()


def contrast_into(gathered_ref, pooled_ref, grad_ref, loss_ref, pool_ref, me, mod, items):
    count = gathered_ref.shape[0]
    width = pooled_ref.shape[2]
    total = items * count
    for half in range(2):
        for n in range(items):
            for part in range(width // 128):
                pooled_ref[half, n * count : (n + 1) * count, part * 128 : (part + 1) * 128] = gathered_ref[
                    :, half, n * (width // 128) + part, :
                ]
    flags = [gathered_ref[:, 0, items * (width // 128) + n, :][:, 0:1] for n in range(items)]
    present = jnp.concatenate(flags, axis=0)
    same = lax.broadcasted_iota(jnp.int32, (total, total), 0) == lax.broadcasted_iota(jnp.int32, (total, total), 1)
    same = jnp.where(same, 1.0, 0.0)
    present_row = column_sum(present * same)
    scale = LOGIT_SCALE / width
    units, inverses = [], []
    for half in range(2):
        pooled = pooled_ref[half]
        inverses.append(lax.rsqrt(jnp.mean(pooled * pooled, axis=-1, keepdims=True) + 1e-06))
        units.append(pooled * inverses[-1])
    exact = lax.Precision.HIGHEST
    logits = lax.dot_general(units[0], units[1], LAST, precision=exact, preferred_element_type=F32) * scale
    by_row = logits - 10000.0 * (1.0 - present_row)
    by_column = logits - 10000.0 * (1.0 - present)
    row_top = jnp.max(by_row, axis=1, keepdims=True)
    column_top = jnp.max(by_column, axis=0, keepdims=True)
    by_row = jnp.exp(by_row - row_top)
    by_column = jnp.exp(by_column - column_top)
    row_sum = jnp.sum(by_row, axis=1, keepdims=True)
    column_total = column_sum(by_column)
    row_part = present * (row_top + jnp.log(row_sum) - 2.0 * jnp.sum(logits * same, axis=1, keepdims=True))
    column_part = present_row * (column_top + jnp.log(column_total))
    loss = (jnp.sum(row_part) + jnp.sum(column_part)) / (2.0 * total)
    loss_ref[0, 0] = loss
    grad_logits = (
        present * by_row / row_sum + present_row * by_column / column_total - 2.0 * same * present
    ) * (scale / (2.0 * total))

    def own(half, grad_unit):
        unit = units[half]
        grad_ref[...] = inverses[half] * (grad_unit - unit * jnp.mean(grad_unit * unit, axis=-1, keepdims=True))

    @pl.when(mod == 0)
    def _():
        own(0, jnp.dot(grad_logits, units[1], precision=exact, preferred_element_type=F32))

    @pl.when(mod == 1)
    def _():
        own(1, lax.dot_general(grad_logits, units[0], FIRST, precision=exact, preferred_element_type=F32))

    for n in range(items):
        pool_ref[n : n + 1, :] = grad_ref[pl.ds(n * count + me, 1), :]


def forward_kernel(
    tokens_ref, grid_ref, gain_ref, norms_ref, cross_gain_hbm, present_ref, cotangent_ref,
    project_hbm, mixer_hbm, expand_hbm, reduce_hbm,
    query_hbm, keyval_hbm, cmixer_hbm, cexpand_hbm, creduce_hbm,
    encoded_out, joined_out, normed_out, rows_out, probs_out, mixed_out, resid_out, normed_two_out, hidden_out, slope_out,
    part_out, query_in_out, keyval_in_out, cnormed_out, cmixed_out, chidden_out, branch_out, cgexp_out, cgattn_out,
    gq_out, gkv_out,
    gains_ref, loss_ref, pool_ref,
    project_ref, mixer_ref, expand_ref, reduce_ref,
    cquery_ref, cmixer_ref, cexpand_ref, creduce_ref,
    encoded_ref, partner_ref, normed_ref, rows_ref, probs_ref, mixed_ref, resid_ref, normed_two_ref, hidden_ref,
    slope_keep_ref,
    q_ref, kv_ref, cprobs_ref, cmixed_ref, cresid_ref, chidden_ref, cgexp_ref, query_in_ref, keyval_in_ref, cnormed_ref,
    branch_ref, cgattn_ref, gq_ref, gkv_ref, gmix_ref, gin_ref, part_ref, joined_ref,
    gathered_ref, pooled_ref, grad_ref, cgain_ref, dist_ref, cross_gain_ref,
    load_sems, out_sems, weight_sends, weight_recvs, gather_sends, gather_recvs, swap_sends, swap_recvs,
):
    items, patches, width = tokens_ref.shape
    half, wide = width // 2, 2 * width
    count = gathered_ref.shape[0]
    bits = count.bit_length() - 1
    me, mod = lax.axis_index("dp"), lax.axis_index("mod")
    is_radar = mod == 1
    across = {"mod": 1 - mod}
    loads = [
        pltpu.make_async_copy(source, target, load_sems.at[i])
        for i, (source, target) in enumerate(
            (
                (project_hbm, project_ref),
                (query_hbm, cquery_ref.at[0, :, 0:half]),
                (keyval_hbm, cquery_ref.at[1:3, :, 0:half]),
                (cmixer_hbm, cmixer_ref.at[0:half]),
                (cexpand_hbm, cexpand_ref.at[:, 0:wide]),
                (creduce_hbm, creduce_ref.at[0:wide]),
                (mixer_hbm, mixer_ref),
                (expand_hbm, expand_ref),
                (reduce_hbm, reduce_ref),
            )
        )
    ]
    begin(loads)
    weights = Weights((cquery_ref, cmixer_ref, cexpand_ref, creduce_ref), me, mod, (weight_sends, weight_recvs))
    gather = Gather(gathered_ref, me, mod, bits, (gather_sends, gather_recvs))
    outputs = Outputs(out_sems)
    swaps = {}

    def swap(key, source, target):
        place = len(swaps)
        swaps[key] = remote(source, target, swap_sends.at[place], swap_recvs.at[place], across)
        swaps[key].start()

    barrier = pltpu.get_barrier_semaphore()
    others = [across] + [{"dp": me + flip * (1 << bit)} for bit, flip in enumerate(gather.flip)]
    for device in others:
        pl.semaphore_signal(barrier, inc=1, device_id=device, device_id_type=pl.DeviceIdType.MESH)
    pl.semaphore_wait(barrier, len(others))

    def pump(*events):
        for event in events:
            weights.advance(*event)

    cross_gain_ref[...] = cross_gain_hbm[...].reshape(1, width)
    for n in range(items):
        spans = []
        for axis in range(2):
            along = jnp.broadcast_to(grid_ref[n, axis : axis + 1, :].astype(F32), (8, patches))
            spans.append(along.T[:, 0:1] - along[0:1, :])
        dist_ref[n] = jnp.sqrt(spans[0] * spans[0] + spans[1] * spans[1])

    def encode_image(n, pumps):
        def put(key, source, target):
            outputs.emit(key, source, target.at[n])

        tokens = tokens_ref[n].astype(F32)
        unit, _ = norm_rows(tokens)
        outputs.ready("normed", "rows")
        normed_ref[...] = (unit * gain_ref[0:1, :]).astype(BF16)
        put("normed", normed_ref, normed_out)
        if n == 0:
            loads[0].wait()
        for part in range(3):
            cut = slice(part * width, (part + 1) * width)
            rows_ref[:, cut] = dot(normed_ref[...], project_ref[:, cut]).astype(BF16)
        put("rows", rows_ref, rows_out)
        if n == 0:
            finish(loads[1:6])
        pump(*pumps[0])
        outputs.ready("probs", "mixed")
        attend(
            rows_ref, rows_ref, rows_ref, (0, width, 2 * width), dist_ref.at[n], 0, probs_ref, mixed_ref
        )
        put("probs", probs_ref, probs_out)
        put("mixed", mixed_ref, mixed_out)
        pump(*pumps[1])
        if n == 0:
            loads[6].wait()
        outputs.ready("resid", "normed_two")
        resid = tokens_ref[n].astype(F32) + dot(mixed_ref[...], mixer_ref[...])
        resid_ref[...] = resid
        unit, _ = norm_rows(resid)
        normed_two_ref[...] = (unit * gain_ref[1:2, :]).astype(BF16)
        put("resid", resid_ref, resid_out)
        put("normed_two", normed_two_ref, normed_two_out)
        if n == 0:
            finish(loads[7:9])
        outputs.ready("hidden", "slope")
        for part in range(expand_ref.shape[1] // width):
            cut = slice(part * width, (part + 1) * width)
            value, slope = gelu_pair(dot(normed_two_ref[...], expand_ref[:, cut]))
            hidden_ref[:, cut] = value.astype(BF16)
            slope_keep_ref[:, cut] = slope.astype(BF16)
        put("hidden", hidden_ref, hidden_out)
        put("slope", slope_keep_ref, slope_out)
        pump(*pumps[2])
        encoded = (resid_ref[...] + dot(hidden_ref[...], reduce_ref[...])).astype(BF16)
        encoded_ref[n] = encoded
        put(("encoded", n), encoded_ref.at[n], encoded_out)
        swap(n, encoded_ref.at[n], partner_ref.at[n])
        pooled = jnp.mean(encoded.astype(F32), axis=0, keepdims=True)
        if n == 0:
            gathered_ref[me, mod] = jnp.zeros(gathered_ref.shape[2:], F32)
        for part in range(width // 128):
            place = n * (width // 128) + part
            gathered_ref[me, mod, place : place + 1, :] = pooled[:, part * 128 : (part + 1) * 128]
        place = items * (width // 128) + n
        gathered_ref[me, mod, place : place + 1, :] = jnp.full((1, 128), present_ref[n], jnp.int32).astype(F32)
        pump(*pumps[3])

    encode_image(0, (((0, 0), (1, 0), (2, 0), (3, 0)), ((0, 1), (1, 1)), ((0, 2), (1, 2)), ()))
    encode_image(1, (((2, 1),), ((3, 1), (0, 3), (1, 3)), ((2, 2),), ((3, 2),)))
    gather.advance()

    def join_image(n, pumps):
        def put(key, source, target):
            outputs.emit(key, source, target.at[n])

        swaps[n].wait_recv()
        own, other = encoded_ref[n], partner_ref[n]
        unit, _ = norm_rows(jnp.where(is_radar, own, other).astype(F32))
        outputs.ready("query_in", "keyval_in")
        query_in_ref[...] = (unit * norms_ref[1:2, :]).astype(BF16)
        unit, _ = norm_rows(jnp.where(is_radar, other, own).astype(F32))
        keyval_in_ref[...] = (unit * norms_ref[0:1, :]).astype(BF16)
        put("query_in", query_in_ref, query_in_out)
        put("keyval_in", keyval_in_ref, keyval_in_out)
        pump(*pumps[0])
        q_ref[...] = dot(query_in_ref[...], cquery_ref[0]).astype(BF16)
        for part in range(2):
            kv_ref[:, part * width : (part + 1) * width] = dot(keyval_in_ref[...], cquery_ref[1 + part]).astype(BF16)
        gather.advance()
        starts = (0, 0, width)
        outputs.ready("cmixed")
        attend(q_ref, kv_ref, kv_ref, starts, dist_ref.at[n], mod * (HEADS // 2), cprobs_ref, cmixed_ref)
        put("cmixed", cmixed_ref.at[:, 0:half], cmixed_out)
        gather.advance()
        radar = jnp.where(is_radar, encoded_ref[n], partner_ref[n]).astype(F32)
        resid = radar + dot(cmixed_ref[...], cmixer_ref[...])
        cresid_ref[...] = resid
        unit, _ = norm_rows(resid)
        outputs.ready("cnormed", "branch")
        cnormed_ref[...] = (unit * cross_gain_ref[...]).astype(BF16)
        put("cnormed", cnormed_ref, cnormed_out)
        present = present_ref[n].astype(F32)
        branch_ref[...] = (present * cotangent_ref[n].astype(F32)).astype(BF16)
        put("branch", branch_ref, branch_out)
        pump(*pumps[1])
        outputs.ready("chidden", "cgexp")
        for part in range(cexpand_ref.shape[1] // width):
            cut = slice(part * width, (part + 1) * width)
            value, slope = gelu_pair(dot(cnormed_ref[...], cexpand_ref[:, cut]))
            chidden_ref[:, cut] = value.astype(BF16)
            upstream = dot_last(branch_ref[...], creduce_ref[cut, :])
            cgexp_ref[:, cut] = (upstream * slope).astype(BF16)
        put("chidden", chidden_ref.at[:, 0:wide], chidden_out)
        put("cgexp", cgexp_ref.at[:, 0:wide], cgexp_out)

        @pl.when(mod == n)
        def _():
            joined_ref[...] = (present * (cresid_ref[...] + dot(chidden_ref[...], creduce_ref[...]))).astype(BF16)

        if n == items - 1:
            swap("joined", joined_ref, joined_out.at[mod])
            outputs.emit("joined", joined_ref, joined_out.at[mod])
        gather.advance()
        grad_normed = dot_last(cgexp_ref[...], cexpand_ref[...])
        unit, inverse = norm_rows(cresid_ref[...])
        own_gain = jnp.where(mod == n, 1.0, 0.0) * column_sum(grad_normed * unit)
        gains_ref[1:2, :] = own_gain if n == 0 else gains_ref[1:2, :] + own_gain
        if n == items - 1:
            cgain_ref[0] = jnp.broadcast_to(gains_ref[1:2, :], cgain_ref.shape[1:])
            swap("cgain", cgain_ref.at[0], cgain_ref.at[1])
        grad = present * cotangent_ref[n].astype(F32) + norm_back(grad_normed, unit, inverse, cross_gain_ref[...])
        outputs.ready("part", "cgattn")
        part_ref[...] = grad
        cgattn_ref[...] = grad.astype(BF16)
        put("cgattn", cgattn_ref, cgattn_out)
        gmix_ref[...] = dot_last(cgattn_ref[...], cmixer_ref[...]).astype(BF16)
        gather.advance()
        outputs.ready("gq", "gkv")
        attend_back(q_ref, kv_ref, kv_ref, starts, cprobs_ref, gmix_ref, (gq_ref, gkv_ref, gkv_ref), (0, 0, width))
        put("gq", gq_ref.at[:, 0:half], gq_out)
        outputs.emit("gkv", gkv_ref.at[:, 0:half], gkv_out.at[n, :, 0:half])
        outputs.emit("gkv", gkv_ref.at[:, width : width + half], gkv_out.at[n, :, half:width])
        gather.advance()

        @pl.when(is_radar)
        def _():
            gin_ref[...] = dot_last(gq_ref[...], cquery_ref[0])

        @pl.when(mod == 0)
        def _():
            gin_ref[...] = dot_last(gkv_ref[:, 0:width], cquery_ref[1]) + dot_last(gkv_ref[:, width:], cquery_ref[2])

        gain = jnp.where(is_radar, norms_ref[1:2, :], norms_ref[0:1, :])
        unit, inverse = norm_rows(encoded_ref[n].astype(F32))
        grad_in = gin_ref[...]
        sums = column_sum(grad_in * unit)
        gains_ref[0:1, :] = sums if n == 0 else gains_ref[0:1, :] + sums
        part_ref[...] = jnp.where(is_radar, part_ref[...], 0.0) + norm_back(grad_in, unit, inverse, gain)
        put("part", part_ref, part_out)

    join_image(0, (((0, 4), (1, 4)), ((2, 3), (3, 3), (2, 4), (3, 4))))
    join_image(1, ((), ()))
    while not gather.done:
        gather.advance()
    contrast_into(gathered_ref, pooled_ref, grad_ref, loss_ref, pool_ref, me, mod, items)
    swaps["cgain"].wait_recv()
    gains_ref[1:2, :] = gains_ref[1:2, :] + cgain_ref[1, 0:1, :]
    swaps["joined"].wait_recv()
    for copy in swaps.values():
        copy.wait_send()
    weights.finish()
    gather.finish()
    outputs.finish()


def forward(tokens, grid, gains, norms, cross_gain, present, cotangent, weights, cross, count):
    items, patches, width = tokens.shape
    half, wide, full = width // 2, 2 * width, 4 * width
    bits = count.bit_length() - 1
    pairs = HEADS // 2

    def out(*dims, dtype=BF16):
        return shape((items, patches, *dims), dtype)

    outs = (
        out(width), out(width), out(width), out(3 * width), shape((items, pairs, patches, 2 * patches), BF16), out(width),
        out(width, dtype=F32), out(width), out(full), out(full),
        out(width, dtype=F32), out(width), out(width), out(width), out(half), out(wide), out(width), out(wide), out(width),
        out(half), out(width),
    )
    row = (patches, width)
    narrow = [row, (patches, 3 * width), (pairs, patches, 2 * patches), row]
    scratch = [pltpu.VMEM(w.shape, BF16) for w in weights]
    scratch += [pltpu.VMEM(d, BF16) for d in ((3, width, width), (width, width), (width, full), (full, width))]
    scratch += [pltpu.VMEM((items, *row), BF16)] * 2
    scratch += [pltpu.VMEM(d, BF16) for d in narrow]
    scratch += [pltpu.VMEM(row, F32), pltpu.VMEM(row, BF16), pltpu.VMEM((patches, full), BF16), pltpu.VMEM((patches, full), BF16)]
    scratch += [pltpu.VMEM(d, BF16) for d in (row, (patches, wide), (pairs, patches, 2 * patches), row)]
    scratch += [pltpu.VMEM(row, F32), pltpu.VMEM((patches, full), BF16), pltpu.VMEM((patches, full), BF16)]
    scratch += [pltpu.VMEM(row, BF16)] * 5
    scratch += [pltpu.VMEM(row, BF16), pltpu.VMEM((patches, wide), BF16), pltpu.VMEM(row, BF16)]
    scratch += [pltpu.VMEM(row, F32), pltpu.VMEM(row, F32), pltpu.VMEM(row, BF16)]
    scratch += [
        pltpu.VMEM((count, 2, 16, 128), F32),
        pltpu.VMEM((2, items * count, width), F32),
        pltpu.VMEM((items * count, width), F32),
        pltpu.VMEM((2, 8, width), F32),
        pltpu.VMEM((items, patches, patches), F32),
        pltpu.VMEM((1, width), F32),
    ]
    dma = pltpu.SemaphoreType.DMA
    scratch += [dma((9,)), dma((2 * 24 + 4,)), dma((4, 8)), dma((4, 8)), dma((bits + 1,)), dma((bits + 1,)), dma((4,)), dma((4,))]
    return pl.pallas_call(
        forward_kernel,
        out_shape=outs + (shape((2, width), F32), shape((1, 1), F32), shape((items, width), F32)),
        in_specs=[VMEM, VMEM, VMEM, VMEM, VMEM, SMEM, VMEM] + [ANY] * 9,
        out_specs=(ANY,) * len(outs) + (VMEM, SMEM, VMEM),
        scratch_shapes=scratch,
        compiler_params=pltpu.CompilerParams(
            collective_id=1, has_side_effects=True, vmem_limit_bytes=62 * 1024 * 1024
        ),
        cost_estimate=cost(items * patches * 40 * width * width, 60 * 2**20),
        name="forward",
    )(tokens, grid, gains, norms, cross_gain, present, cotangent, *weights, *cross)


class Halvings:
    def __init__(self, orders, held, got, sems, me, make, result):
        self.orders, self.held, self.got, self.sems = orders, held, got, sems
        self.make_chunk, self.result = make, result
        self.bits = len(orders[0])
        self.every = list(range(self.bits))[::-1]
        self.mine = ring_bits(me, self.bits)
        self.partners = [{"dp": me + (1 - 2 * bit) * (1 << place)} for place, bit in enumerate(self.mine)]
        self.copies, self.waited, self.done = {}, set(), set()
        self.total = len(orders)

    def held_at(self, chunk, stage):
        return self.held[stage].at[chunk % self.held[stage].shape[0]]

    def got_at(self, chunk, stage):
        return self.got[stage].at[chunk % self.got[stage].shape[0]]

    def part(self, chunk, stage, kept):
        bit = self.orders[chunk][stage]
        left = [other for other in self.every if other not in self.orders[chunk][:stage]]
        side = self.mine[bit] if kept else 1 - self.mine[bit]
        return self.held_at(chunk, stage).at[tuple(side if other == bit else slice(None) for other in left)]

    def send(self, chunk, stage):
        copy = remote(
            self.part(chunk, stage, False), self.got_at(chunk, stage),
            self.sems[0].at[stage, chunk], self.sems[1].at[stage, chunk],
            self.partners[self.orders[chunk][stage]],
        )
        copy.start()
        self.copies[chunk, stage] = copy

    def free(self, chunk, stage):
        last = chunk - self.held[stage].shape[0]
        if last >= 0 and (last, stage) not in self.waited:
            self.copies[last, stage].wait_send()
            self.waited.add((last, stage))

    def make(self, chunk):
        if not 0 <= chunk < self.total or (chunk, "made") in self.done:
            return
        self.done.add((chunk, "made"))
        self.free(chunk, 0)
        self.make_chunk(chunk, self.held_at(chunk, 0))
        self.send(chunk, 0)

    def take(self, chunk, stage):
        if not 0 <= chunk < self.total or (chunk, stage) in self.done:
            return
        self.done.add((chunk, stage))
        self.copies[chunk, stage].wait_recv()
        kept, arrived = self.part(chunk, stage, True), self.got_at(chunk, stage)
        if stage == self.bits - 1:
            self.result(chunk, kept[...].astype(F32) + arrived[...].astype(F32))
            return
        self.free(chunk, stage + 1)
        target = self.held_at(chunk, stage + 1)
        target[...] = kept[...] + arrived[...]
        self.send(chunk, stage + 1)

    def step(self, chunk):
        self.make(chunk)
        self.take(chunk - 1, 0)
        for stage in range(1, self.bits):
            self.take(chunk - LAG - stage, stage)

    def finish(self):
        for key, copy in self.copies.items():
            if key not in self.waited:
                copy.wait_send()


LAG = 3


def backward_kernel(
    plan, results, orders, sizes,
    pool_ref, gain_ref, cross_gains_ref, part_hbm, cotangent_hbm, tokens_hbm, resid_hbm, slope_hbm, rows_hbm, probs_hbm,
    project_hbm, mixer_hbm, expand_hbm, reduce_hbm, *rest,
):
    n_in, n_out, bits, early = sizes
    operands, rest = rest[:n_in], rest[n_in:]
    patch_out, outs, vector_out, scratch = rest[0], rest[1 : 1 + n_out], rest[1 + n_out], rest[2 + n_out :]
    (
        project_ref, mixer_ref, expand_ref, reduce_ref,
        patch_ref, cotangent_ref, tokens_ref, resid_ref, slope_ref, rows_ref, probs_ref,
        branch_ref, gexp_ref, gattn_ref, grows_ref, gmix_ref, left_ref, right_ref,
    ) = scratch[:18]
    scratch = scratch[18:]
    held, got = scratch[:bits], scratch[bits : 2 * bits]
    vector_held, vector_got = scratch[2 * bits : 3 * bits], scratch[3 * bits : 4 * bits]
    load_sems, left_sems, right_sems, out_sems, send_sems, recv_sems, vector_sends, vector_recvs = scratch[4 * bits :]
    items, patches = pool_ref.shape[0], resid_ref.shape[0] // pool_ref.shape[0]
    width = patch_ref.shape[1]
    me = lax.axis_index("dp")
    resident = {"branch": branch_ref, "gexp": gexp_ref, "gattn": gattn_ref, "grows": grows_ref}
    fetched, loaded, slots = {}, {}, [0, 0]

    def fetch(kind, key, source, target_of, sems):
        if loaded.get(kind, [None])[-1] == key:
            return fetched[key]
        buffers = target_of.shape[0]
        slot = slots[kind] % buffers
        slots[kind] += 1
        copy = pltpu.make_async_copy(source, target_of.at[slot, :, 0 : source.shape[1]], sems.at[slots[kind] - 1])
        copy.start()
        fetched[key] = [slot, copy]
        loaded.setdefault(kind, []).append(key)
        return fetched[key]

    def fetch_chunk(chunk):
        if chunk >= len(plan):
            return
        for left, right, start, size, _ in plan[chunk]:
            if not isinstance(left, str):
                fetch(0, ("left", left), operands[left], left_ref, left_sems)
            if not isinstance(right, str):
                fetch(1, ("right", right, start), operands[right].at[:, start : start + size], right_ref, right_sems)

    def arrived(key):
        entry = fetched[key]
        if entry[1] is not None:
            entry[1].wait()
            entry[1] = None
        return entry[0]

    def make_chunk(chunk, target):
        fetch_chunk(chunk + 1)
        block = target.shape[-2]
        for left, right, start, size, place in plan[chunk]:
            one = resident[left][...] if isinstance(left, str) else left_ref[arrived(("left", left))]
            if isinstance(right, str):
                other = resident[right][:, start : start + size]
            else:
                other = right_ref[arrived(("right", right, start)), :, 0:size]
            product = dot_first(one, other).astype(BF16)
            for index in range(1 << bits):
                where = tuple((index >> bit) & 1 for bit in range(bits)[::-1])
                target[(*where, slice(None), slice(place, place + size))] = product[index * block : (index + 1) * block]

    def result(chunk, value):
        for out, column, first, size in results[chunk]:
            if len(outs[out].shape) == 3:
                outs[out][column] = value[:, first : first + size]
            else:
                outs[out][:, column : column + size] = value[:, first : first + size]

    fetch_chunk(0)
    loads = [
        pltpu.make_async_copy(source, target, load_sems.at[i])
        for i, (source, target) in enumerate(
            (
                (part_hbm, patch_ref), (cotangent_hbm, cotangent_ref), (reduce_hbm, reduce_ref), (slope_hbm, slope_ref),
                (expand_hbm, expand_ref), (resid_hbm, resid_ref), (mixer_hbm, mixer_ref), (rows_hbm, rows_ref),
                (probs_hbm, probs_ref), (project_hbm, project_ref), (tokens_hbm, tokens_ref),
            )
        )
    ]
    begin(loads)
    sums = Halvings(orders, held, got, (send_sems, recv_sems), me, make_chunk, result)
    barrier = pltpu.get_barrier_semaphore()
    for device in sums.partners:
        pl.semaphore_signal(barrier, inc=1, device_id=device, device_id_type=pl.DeviceIdType.MESH)
    pl.semaphore_wait(barrier, bits)
    for chunk in range(early + 1):
        if chunk < early:
            sums.make(chunk)
        sums.take(chunk - 1, 0)

    images = [slice(n * patches, (n + 1) * patches) for n in range(items)]
    finish(loads[0:4])
    for n, own in enumerate(images):
        grad = cotangent_ref[own].astype(F32) + pool_ref[n : n + 1, :] * (1.0 / patches) + patch_ref[own]
        patch_ref[own] = grad
        branch_ref[own] = grad.astype(BF16)
    for part in range(expand_ref.shape[1] // width):
        cut = slice(part * width, (part + 1) * width)
        upstream = dot_last(branch_ref[...], reduce_ref[cut, :])
        gexp_ref[:, cut] = (upstream * slope_ref[:, cut].astype(F32)).astype(BF16)
    sums.take(0, 1)
    finish(loads[4:6])
    gains = []
    for own in images:
        grad_normed = dot_last(gexp_ref[own], expand_ref[...])
        unit, inverse = norm_rows(resid_ref[own])
        gains.append(column_sum(grad_normed * unit))
        grad = patch_ref[own] + norm_back(grad_normed, unit, inverse, gain_ref[1:2, :])
        patch_ref[own] = grad
        gattn_ref[own] = grad.astype(BF16)
    second_gain = sum(gains)
    sums.take(1, 1)
    sums.take(0, 2)
    finish(loads[6:9])
    gmix_ref[...] = dot_last(gattn_ref[...], mixer_ref[...]).astype(BF16)
    starts = (0, width, 2 * width)
    for n, own in enumerate(images):
        rows, grows = rows_ref.at[own], grows_ref.at[own]
        attend_back(rows, rows, rows, starts, probs_ref.at[n], gmix_ref.at[own], (grows,) * 3, starts)
        sums.step(early + n)
    finish(loads[9:11])
    gains = []
    for n, own in enumerate(images):
        grad_normed = dot_last(grows_ref[own], project_ref[...])
        unit, inverse = norm_rows(tokens_ref[own].astype(F32))
        gains.append(column_sum(grad_normed * unit))
        patch_ref[own] = patch_ref[own] + norm_back(grad_normed, unit, inverse, gain_ref[0:1, :])
    patch_copy = pltpu.make_async_copy(patch_ref, patch_out, out_sems.at[0])
    patch_copy.start()
    rows = jnp.concatenate([sum(gains), second_gain, cross_gains_ref[...], jnp.zeros((4, width), F32)], axis=0)
    block = width >> bits
    for index in range(1 << bits):
        where = tuple((index >> bit) & 1 for bit in range(bits)[::-1])
        piece = rows[:, index * block : (index + 1) * block]
        vector_held[0][where] = jnp.concatenate([piece, jnp.zeros((8, 128 - block), F32)], axis=1)
    vector_copies = []

    def vector_step():
        stage = len(vector_copies)
        if stage > bits:
            return
        if stage:
            bit = stage - 1
            vector_copies[-1].wait_recv()
            left = list(range(bit, bits))[::-1]
            kept = vector_held[bit].at[tuple(sums.mine[bit] if other == bit else slice(None) for other in left)]
            value = kept[...] + vector_got[bit][...]
            if stage == bits:
                vector_out[...] = value
                vector_copies.append(None)
                return
            vector_held[stage][...] = value
        left = list(range(stage, bits))[::-1]
        view = vector_held[stage].at[tuple(1 - sums.mine[stage] if other == stage else slice(None) for other in left)]
        copy = remote(view, vector_got[stage], vector_sends.at[stage], vector_recvs.at[stage], sums.partners[stage])
        copy.start()
        vector_copies.append(copy)

    vector_step()
    chunk = early + items
    while len([key for key in sums.done if key[1] == bits - 1]) < len(plan):
        sums.step(chunk)
        vector_step()
        chunk += 1
    while len(vector_copies) <= bits:
        vector_step()
    for copy in vector_copies[:bits]:
        copy.wait_send()
    sums.finish()
    patch_copy.wait()


def backward(pool, gains, cross_gains, activations, weights, operands, plan, results, outs, orders, early, count):
    part, cotangent, tokens, resid, slope, rows, probs = activations
    total_rows, width = tokens.shape
    bits = count.bit_length() - 1
    block, chunks = width // count, len(plan)
    two = (2,) * bits
    full, pairs = slope.shape[1], probs.shape[1:]
    held = (2, 7, 3, 3) + (3,) * (bits - 4)
    got = (4, 10, 5, 5) + (5,) * (bits - 4)
    flat = (total_rows, width)
    lefts = [key for chunk in plan for key in chunk]
    dma = pltpu.SemaphoreType.DMA
    scratch = [pltpu.VMEM(w.shape, BF16) for w in weights]
    scratch += [pltpu.VMEM(flat, F32), pltpu.VMEM(flat, BF16), pltpu.VMEM(flat, BF16), pltpu.VMEM(flat, F32)]
    scratch += [pltpu.VMEM((total_rows, full), BF16), pltpu.VMEM((total_rows, 3 * width), BF16), pltpu.VMEM(probs.shape, BF16)]
    scratch += [pltpu.VMEM(flat, BF16), pltpu.VMEM((total_rows, full), BF16), pltpu.VMEM(flat, BF16)]
    scratch += [pltpu.VMEM((total_rows, 3 * width), BF16), pltpu.VMEM(flat, BF16)]
    scratch += [pltpu.VMEM((3, *flat), BF16), pltpu.VMEM((3, *flat), BF16)]
    scratch += [pltpu.VMEM((held[stage], *two[stage:], block, width), BF16) for stage in range(bits)]
    scratch += [pltpu.VMEM((got[stage], *two[stage + 1 :], block, width), BF16) for stage in range(bits)]
    scratch += [pltpu.VMEM((*two[stage:], 8, 128), F32) for stage in range(bits)]
    scratch += [pltpu.VMEM((*two[stage + 1 :], 8, 128), F32) for stage in range(bits)]
    scratch += [dma((11,)), dma((len(lefts),)), dma((len(lefts),)), dma((1,)), dma((bits, chunks)), dma((bits, chunks))]
    scratch += [dma((bits,)), dma((bits,))]
    return pl.pallas_call(
        functools.partial(backward_kernel, plan, results, orders, (len(operands), len(outs), bits, early)),
        out_shape=(shape(flat, F32), *(shape(dims, F32) for dims in outs), shape((8, 128), F32)),
        in_specs=[VMEM] * 3 + [ANY] * (7 + 4 + len(operands)),
        out_specs=(ANY,) + (VMEM,) * (len(outs) + 1),
        scratch_shapes=scratch,
        compiler_params=pltpu.CompilerParams(
            collective_id=0, has_side_effects=True, vmem_limit_bytes=63 * 1024 * 1024
        ),
        cost_estimate=cost(total_rows * (chunks + 12) * width * width, 60 * 2**20),
        name="backward",
    )(pool, gains, cross_gains, *activations, *weights, *operands)


def flipped(array, axis, bit):
    return lax.ppermute(array, axis, [(i, i ^ (1 << bit)) for i in range(lax.axis_size(axis))])


def block_order(width, count):
    bits = count.bit_length() - 1
    block = width // count
    rows = jnp.arange(width)
    place = rows // block
    partner = jnp.zeros_like(place)
    for bit in range(bits):
        partner = partner | (((place >> (bits - 1 - bit)) & 1) << bit)
    source = (lax.axis_index("dp") ^ partner) * block + rows % block
    return (source[:, None] == jnp.arange(width)[None, :]).astype(BF16)


def ordered(order, values):
    return jnp.einsum("jd,rd->jr", order, values, preferred_element_type=F32).astype(BF16)


def summed(left_rows, grad_rows):
    count = lax.axis_size("dp")
    half = left_rows.shape[0] // 2
    send = jnp.dot(left_rows[half:], grad_rows, preferred_element_type=F32).astype(BF16)
    keep = jnp.dot(left_rows[:half], grad_rows, preferred_element_type=F32).astype(BF16)
    bits = count.bit_length() - 1
    for bit in range(bits):
        got = flipped(send, "dp", bit)
        if bit == bits - 1:
            return keep.astype(F32) + got.astype(F32)
        half = half // 2
        send = (keep[half:].astype(F32) + got[half:].astype(F32)).astype(BF16)
        keep = (keep[:half].astype(F32) + got[:half].astype(F32)).astype(BF16)


def summed_blocks(blocks):
    bits = lax.axis_size("dp").bit_length() - 1
    for bit in range(bits):
        half = blocks.shape[0] // 2
        blocks = blocks[:half] + flipped(blocks[half:], "dp", bit)
    return blocks[0]


def backward_plan(rows, half):
    wide = 2 * rows
    plan, results, outs = [], [], []

    def add(left, right, columns):
        outs.append(columns)
        for start in range(0, columns, rows):
            plan.append([(left, right, start, rows, 0)])
            results.append([(len(outs) - 1, start, 0, rows)])

    add(0, 1, wide)
    add(2, 3, wide)
    outs.extend([half, half])
    plan.append([(4, 5, 0, half, 0), (6, 7, 0, half, half)])
    results.append([(2, 0, 0, half), (3, 0, half, half)])
    outs.append(None)
    plan.append([(8, 9, 0, rows, 0)])
    results.append([(4, 0, 0, half), (4, 1, half, half)])
    early = len(plan)
    add("branch", 10, 4 * rows)
    add(11, "gexp", 4 * rows)
    add(12, "gattn", rows)
    add(13, "grows", 3 * rows)
    return plan, results, outs, early


def finish_kernel(count, *refs):
    sources, loss_ref, vector_ref = refs[:count], refs[count], refs[count + 1]
    targets = refs[count + 2 : 2 * count + 2]
    loss_out, gains_ref, norms_ref, cross_gain_ref = refs[2 * count + 2 : 2 * count + 6]
    kept, (in_sems, out_sems) = refs[2 * count + 6 : 3 * count + 6], refs[3 * count + 6 :]
    arrivals = [pltpu.make_async_copy(a, b, in_sems.at[i]) for i, (a, b) in enumerate(zip(sources, kept))]
    departures = [pltpu.make_async_copy(a, b, out_sems.at[i]) for i, (a, b) in enumerate(zip(kept, targets))]
    begin(arrivals)
    block = gains_ref.shape[1]
    loss_out[0, 0] = loss_ref[0, 0]
    gains_ref[...] = vector_ref[0:2, 0:block]
    norms_ref[...] = vector_ref[2:3, 0:block]
    cross_gain_ref[...] = vector_ref[3:4, 0:block]
    for arrival, departure in zip(arrivals, departures):
        arrival.wait()
        departure.start()
    finish(departures)


def finished(arrays, loss, vector, block):
    small = [shape((1, 1), F32), shape((2, block), F32), shape((1, block), F32), shape((1, block), F32)]
    count = len(arrays)
    return pl.pallas_call(
        functools.partial(finish_kernel, count),
        out_shape=tuple(shape(a.shape, a.dtype) for a in arrays) + tuple(small),
        in_specs=[ANY] * count + [SMEM, VMEM],
        out_specs=(ANY,) * count + (SMEM, VMEM, VMEM, VMEM),
        scratch_shapes=[pltpu.VMEM(a.shape, a.dtype) for a in arrays] + [pltpu.SemaphoreType.DMA((count,))] * 2,
        compiler_params=limits(),
        name="finish",
    )(*arrays, loss, vector)


def shards(
    patch_tokens,
    grid_coords,
    has_radar,
    enc_gains,
    enc_project,
    enc_mixer,
    enc_expand,
    enc_reduce,
    cross_norms,
    cross_gain,
    cross_query,
    cross_keyval,
    cross_mixer,
    cross_expand,
    cross_reduce,
    enc_cotangent,
    joined_cotangent,
):
    item_count, patches, model_width = patch_tokens.shape[1:]
    images = range(item_count)
    dp_size = lax.axis_size("dp")
    weights = (enc_project[0], enc_mixer[0], enc_expand[0], enc_reduce[0])
    cross_weights = (cross_query, cross_keyval, cross_mixer, cross_expand, cross_reduce)

    (encoded, joined_tokens, normed, rows, probs, mixed, resid, normed_two, hidden, slope,
     part, query_in, keyval_in, cnormed, cmixed, chidden, branch, cgexp, cgattn, gq, gkv,
     cross_gains, loss, pool_grad) = forward(
        patch_tokens[0], grid_coords, enc_gains[0], cross_norms, cross_gain, has_radar,
        joined_cotangent, weights, cross_weights, dp_size,
    )

    block = model_width // dp_size

    def flat(values):
        return values.reshape(item_count * patches, *values.shape[2:])

    weight_operands = [
        flat(v)
        for v in (
            branch, chidden, cnormed, cgexp, query_in, gq, cgattn, cmixed, keyval_in, gkv, hidden, normed_two, mixed, normed
        )
    ]
    if dp_size == 16 and block % 16 == 0:
        plan, places, outs, early = backward_plan(model_width, model_width // 2)
        dims = [(2, block, model_width // 2) if columns is None else (block, columns) for columns in outs]
        orders = [(0, 2, 3, 1) if n in (3, 8, 13) else (0, 1, 2, 3) for n in range(len(plan))]
        activations = [flat(v) for v in (part, enc_cotangent[0], patch_tokens[0], resid, slope, rows)] + [probs]
        results = backward(
            pool_grad, enc_gains[0], cross_gains, activations, weights, weight_operands, plan, places, dims, orders, early,
            dp_size,
        )
        vector_sum = results[-1]
        results = results[:-1]
    else:
        back = [
            encode_back(
                enc_cotangent[0, n], part[n], pool_grad[n : n + 1], enc_gains[0], patch_tokens[0, n],
                resid[n], slope[n], rows[n], probs[n], *weights,
            )
            for n in images
        ]
        patch_grad = jnp.concatenate([one[0] for one in back])
        grads = [jnp.concatenate([one[place] for one in back]) for place in range(1, 5)]
        order = block_order(model_width, dp_size)
        pairs = [(weight_operands[2 * n], weight_operands[2 * n + 1]) for n in range(5)]
        pairs += [(grads[0], weight_operands[10])]
        pairs += [(weight_operands[11 + n], grads[1 + n]) for n in range(3)]
        results = [patch_grad] + [summed(ordered(order, left), right) for left, right in pairs]
        results[5] = jnp.stack([results[5][:, : model_width // 2], results[5][:, model_width // 2 :]])
        vectors = jnp.concatenate([back[0][5] + back[1][5], cross_gains])
        blocks = jnp.moveaxis(vectors.reshape(4, dp_size, block), 1, 0)
        wanted = jnp.dot(order[::block, ::block].astype(F32), blocks.reshape(dp_size, -1), precision=lax.Precision.HIGHEST)
        vector_sum = summed_blocks(wanted.reshape(blocks.shape))
        vector_sum = jnp.pad(vector_sum, ((0, 4), (0, 128 - block)))
    (encoded, joined_tokens, patch_grad, creduce_sum, cexpand_sum, query_sum, cmixer_sum, keyval_sum, reduce_sum, expand_sum,
     mixer_sum, project_sum, loss, gains_sum, norms_sum, cross_gain_sum) = finished(
        [encoded, joined_tokens, *results], loss, vector_sum, block
    )
    return (
        encoded[None],
        joined_tokens,
        loss.reshape(()),
        patch_grad.reshape(patch_tokens.shape),
        gains_sum[None],
        project_sum[None],
        mixer_sum[None],
        expand_sum[None],
        reduce_sum.T[None],
        norms_sum,
        cross_gain_sum.reshape(block),
        query_sum,
        keyval_sum,
        cmixer_sum.T,
        cexpand_sum,
        creduce_sum.T,
    )


def solution(mesh):
    placed = (
        P("mod", "dp", None, None),
        P("dp", None, None),
        P("dp"),
        P("mod", None, None),
        P("mod", None, None),
        P("mod", None, None),
        P("mod", None, None),
        P("mod", None, None),
        P(),
        P(),
        P(None, "mod"),
        P(None, None, "mod"),
        P("mod", None),
        P(None, "mod"),
        P("mod", None),
        P("mod", "dp", None, None),
        P("dp", None, None),
    )
    return jax.shard_map(
        shards,
        mesh=mesh,
        in_specs=placed,
        out_specs=(
            P("mod", "dp", None, None),
            P("dp", None, None),
            P(),
            P("mod", "dp", None, None),
            P("mod", None, "dp"),
            P("mod", "dp", None),
            P("mod", "dp", None),
            P("mod", "dp", None),
            P("mod", None, "dp"),
            P("mod", "dp"),
            P("dp"),
            P("dp", "mod"),
            P(None, "dp", "mod"),
            P("mod", "dp"),
            P("dp", "mod"),
            P("mod", "dp"),
        ),
        check_vma=False,
    )
```

```python
import functools

import jax
import jax.numpy as jnp
from jax import lax
from jax.experimental import pallas as pl
from jax.experimental.pallas import tpu as pltpu
from jax.sharding import PartitionSpec as P

HEADS = 12
HEAD_DIM = 64
LOGIT_SCALE = 50.0
F32 = jnp.float32
BF16 = jnp.bfloat16
PAIR = 2 * HEAD_DIM
LAST = (((1,), (1,)), ((), ()))
FIRST = (((0,), (0,)), ((), ()))
VMEM = pl.BlockSpec(memory_space=pltpu.VMEM)
SMEM = pl.BlockSpec(memory_space=pltpu.SMEM)
ANY = pl.BlockSpec(memory_space=pl.ANY)


def dot(left, right):
    return jnp.dot(left, right, preferred_element_type=F32)


def dot_last(left, right):
    return lax.dot_general(left, right, LAST, preferred_element_type=F32)


def dot_first(left, right):
    return lax.dot_general(left, right, FIRST, preferred_element_type=F32)


def norm_rows(values):
    centre = values - jnp.mean(values, axis=-1, keepdims=True)
    inverse = lax.rsqrt(jnp.mean(centre * centre, axis=-1, keepdims=True) + 1e-06)
    return centre * inverse, inverse


def norm_back(grad_out, unit, inverse, gain):
    weighted = grad_out * gain
    return inverse * (
        weighted
        - jnp.mean(weighted, axis=-1, keepdims=True)
        - unit * jnp.mean(weighted * unit, axis=-1, keepdims=True)
    )


def column_sum(values):
    return jnp.sum(values, axis=0, keepdims=True)


def gelu_pair(values):
    root = 0.7978845608028654
    square = values * values
    tanh = jnp.tanh(values * (root + (root * 0.044715) * square))
    half = 0.5 + 0.5 * tanh
    slope = half + (0.5 * values) * (1.0 - tanh * tanh) * (root + (3.0 * root * 0.044715) * square)
    return values * half, slope


def stacked(pair, low):
    zero = jnp.zeros_like(pair)
    return jnp.concatenate([jnp.where(low, pair, zero), jnp.where(low, zero, pair)], axis=0)


def side_by_side(values):
    rows = values.shape[0] // 2
    return jnp.concatenate([values[:rows], values[rows:]], axis=1)


def lanes(first, index):
    return pl.ds(pl.multiple_of(first + index * PAIR, PAIR), PAIR)


def attend(q_ref, k_ref, v_ref, starts, dist_ref, probs_ref, mixed_ref):
    patches = dist_ref.shape[0]
    low = lax.broadcasted_iota(jnp.int32, (patches, PAIR), 1) < HEAD_DIM
    scale = jnp.asarray(HEAD_DIM**-0.5, BF16)

    def one(index, carry):
        queries = stacked(q_ref[:, lanes(starts[0], index)] * scale, low)
        keys = k_ref[:, lanes(starts[1], index)]
        values = stacked(v_ref[:, lanes(starts[2], index)], low)
        scores = dot_last(queries, keys)
        distance = dist_ref[...]
        halves = []
        for side in range(2):
            power = jnp.full((1, patches), 2 * index + side + 1, jnp.int32).astype(F32) * (-8.0 / HEADS)
            part = scores[side * patches : (side + 1) * patches] - jnp.exp2(power) * distance
            part = jnp.exp(part - jnp.max(part, axis=-1, keepdims=True))
            part = part * (1.0 / jnp.sum(part, axis=-1, keepdims=True))
            halves.append(part.astype(BF16))
        probs = jnp.concatenate(halves, axis=1)
        probs_ref[index] = probs
        mixed_ref[:, lanes(0, index)] = dot(probs, values).astype(BF16)
        return carry

    lax.fori_loop(0, HEADS // 2, one, 0, unroll=True)


def attend_back(q_ref, k_ref, v_ref, starts, probs_ref, grad_ref, out_refs, out_starts):
    patches = q_ref.shape[0]
    low = lax.broadcasted_iota(jnp.int32, (patches, PAIR), 1) < HEAD_DIM
    scale = jnp.asarray(HEAD_DIM**-0.5, BF16)

    def one(index, carry):
        queries = stacked(q_ref[:, lanes(starts[0], index)] * scale, low)
        keys = stacked(k_ref[:, lanes(starts[1], index)] * scale, low)
        values = v_ref[:, lanes(starts[2], index)]
        grads = stacked(grad_ref[:, lanes(0, index)], low)
        both = probs_ref[index]
        probs = jnp.concatenate([both[:, :patches], both[:, patches:]], axis=0)
        grad_probs = dot_last(grads, values)
        wide = probs.astype(F32)
        inner = jnp.sum(grad_probs * wide, axis=-1, keepdims=True)
        grad_scores = (wide * (grad_probs - inner)).astype(BF16)
        out_refs[0][:, lanes(out_starts[0], index)] = dot(side_by_side(grad_scores), keys).astype(BF16)
        out_refs[1][:, lanes(out_starts[1], index)] = dot_first(grad_scores, queries).astype(BF16)
        out_refs[2][:, lanes(out_starts[2], index)] = dot_first(probs, grads).astype(BF16)
        return carry

    lax.fori_loop(0, HEADS // 2, one, 0, unroll=True)


def begin(copies):
    for copy in copies:
        copy.start()


def finish(copies):
    for copy in copies:
        copy.wait()


def limits():
    return pltpu.CompilerParams(vmem_limit_bytes=60 * 1024 * 1024)


def shape(dims, dtype):
    return jax.ShapeDtypeStruct(dims, dtype)


def cost(macs, size):
    return pl.CostEstimate(flops=2 * macs, bytes_accessed=size, transcendentals=0)


def encode_back_kernel(
    cotangent_ref, part_ref, pool_ref, gain_ref, tokens_ref, resid_ref, slope_ref, rows_ref, probs_ref,
    project_hbm, mixer_hbm, expand_hbm, reduce_hbm,
    patch_ref, branch_ref, gexp_ref, gattn_ref, grows_ref, gains_ref,
    project_ref, mixer_ref, expand_ref, reduce_ref, gmix_ref, sems,
):
    copies = [
        pltpu.make_async_copy(source, target, sems.at[i])
        for i, (source, target) in enumerate(
            (
                (reduce_hbm, reduce_ref),
                (expand_hbm, expand_ref),
                (mixer_hbm, mixer_ref),
                (project_hbm, project_ref),
            )
        )
    ]
    begin(copies)
    patches, width = tokens_ref.shape
    grad = cotangent_ref[...].astype(F32) + pool_ref[...] * (1.0 / patches) + part_ref[...]
    patch_ref[...] = grad
    branch_ref[...] = grad.astype(BF16)
    copies[0].wait()
    for part in range(expand_ref.shape[1] // width):
        cut = slice(part * width, (part + 1) * width)
        upstream = dot_last(branch_ref[...], reduce_ref[cut, :])
        gexp_ref[:, cut] = (upstream * slope_ref[:, cut].astype(F32)).astype(BF16)
    copies[1].wait()
    grad_normed = dot_last(gexp_ref[...], expand_ref[...])
    unit, inverse = norm_rows(resid_ref[...])
    gains_ref[1:2, :] = column_sum(grad_normed * unit)
    grad = patch_ref[...] + norm_back(grad_normed, unit, inverse, gain_ref[1:2, :])
    patch_ref[...] = grad
    gattn_ref[...] = grad.astype(BF16)
    copies[2].wait()
    gmix_ref[...] = dot_last(gattn_ref[...], mixer_ref[...]).astype(BF16)
    starts = (0, width, 2 * width)
    attend_back(rows_ref, rows_ref, rows_ref, starts, probs_ref, gmix_ref, (grows_ref,) * 3, starts)
    copies[3].wait()
    grad_normed = dot_last(grows_ref[...], project_ref[...])
    unit, inverse = norm_rows(tokens_ref[...].astype(F32))
    gains_ref[0:1, :] = column_sum(grad_normed * unit)
    patch_ref[...] = patch_ref[...] + norm_back(grad_normed, unit, inverse, gain_ref[0:1, :])


def encode_back(cotangent, part, pool, gains, tokens, resid, slope, rows, probs, project, mixer, expand, reduce):
    patches, width = tokens.shape
    wide = expand.shape[1]
    weights = (project, mixer, expand, reduce)
    return pl.pallas_call(
        encode_back_kernel,
        out_shape=(
            shape((patches, width), F32),
            shape((patches, width), BF16),
            shape((patches, wide), BF16),
            shape((patches, width), BF16),
            shape((patches, 3 * width), BF16),
            shape((2, width), F32),
        ),
        in_specs=[VMEM] * 9 + [ANY] * 4,
        out_specs=(VMEM,) * 6,
        scratch_shapes=[pltpu.VMEM(w.shape, BF16) for w in weights]
        + [pltpu.VMEM((patches, width), BF16), pltpu.SemaphoreType.DMA((4,))],
        compiler_params=limits(),
        cost_estimate=cost(patches * sum(w.size for w in weights), 24 * 2**20),
        name="encode_back",
    )(cotangent, part, pool, gains, tokens, resid, slope, rows, probs, *weights)


def ring_bits(index, count):
    return [lax.rem(index // (1 << bit), 2) for bit in range(count)]


class Outputs:
    def __init__(self, sems):
        self.sems, self.used, self.open = sems, 0, {}

    def emit(self, key, source, target):
        copy = pltpu.make_async_copy(source, target, self.sems.at[self.used])
        self.used += 1
        copy.start()
        self.open.setdefault(key, []).append(copy)

    def ready(self, *keys):
        for key in keys:
            for copy in self.open.pop(key, []):
                copy.wait()

    def finish(self):
        self.ready(*list(self.open))


def remote(source, target, send_sem, recv_sem, device):
    return pltpu.make_async_remote_copy(
        src_ref=source,
        dst_ref=target,
        send_sem=send_sem,
        recv_sem=recv_sem,
        device_id=device,
        device_id_type=pl.DeviceIdType.MESH,
    )


class Weights:
    def __init__(self, refs, me, mod, sems):
        self.refs, self.sems, self.mod = refs, sems, mod
        low = ring_bits(me, 3)
        self.flip = [1 - 2 * bit for bit in low]
        self.partner = [{"dp": me + flip * (1 << bit)} for bit, flip in enumerate(self.flip)]
        self.eighth = lax.rem(me, 8)
        self.copies = {}

    def view(self, weight, eighth, own=False):
        query, mixer = self.refs
        width = mixer.shape[0]
        half = width // 2
        side = self.mod if own else 1 - self.mod

        def rows(first, size):
            return pl.ds(pl.multiple_of(first + eighth * size, 16), size)

        if weight < 3:
            return query.at[weight, rows(0, width // 8), pl.ds(pl.multiple_of(side * half, 128), half)]
        return mixer.at[rows(side * half, half // 8)]

    def send(self, weight, place, eighth, device, own=False):
        send_sems, recv_sems = self.sems
        view = self.view(weight, eighth, own)
        copy = remote(
            view, view,
            send_sems.at[weight, place], recv_sems.at[weight, place], device,
        )
        copy.start()
        self.copies[weight, place] = copy

    def eighths(self, weight):
        first, second = (2, 1) if weight % 2 else (1, 2)
        at_first = self.eighth + self.flip[first] * (1 << first)
        at_second = self.eighth + self.flip[second] * (1 << second)
        both = at_first + self.flip[second] * (1 << second)
        return first, second, (self.eighth, at_first, at_second, both)

    def advance(self, weight, event):
        first, second, pieces = self.eighths(weight)
        if event == 0:
            self.send(weight, 0, pieces[0], {"mod": 1 - self.mod}, own=True)
        elif event == 1:
            self.copies[weight, 0].wait_recv()
            self.send(weight, 1, pieces[0], self.partner[first])
            self.send(weight, 2, pieces[0], self.partner[second])
            self.send(weight, 4, pieces[0], self.partner[0])
        elif event == 2:
            self.copies[weight, 1].wait_recv()
            self.send(weight, 3, pieces[1], self.partner[second])
            self.send(weight, 5, pieces[1], self.partner[0])
        elif event == 3:
            self.copies[weight, 2].wait_recv()
            self.send(weight, 6, pieces[2], self.partner[0])
            self.copies[weight, 3].wait_recv()
            self.send(weight, 7, pieces[3], self.partner[0])
        else:
            for place in range(4, 8):
                self.copies[weight, place].wait_recv()

    def finish(self):
        for copy in self.copies.values():
            copy.wait_send()


class Gather:
    def __init__(self, ref, me, mod, bits, sems):
        self.ref, self.sems, self.copies, self.done = ref, sems, [], False
        self.me, self.mod, self.flip = me, mod, [1 - 2 * bit for bit in ring_bits(me, bits)]

    def advance(self):
        stage = len(self.copies)
        if self.done:
            return
        if stage:
            self.copies[-1].wait_recv()
        if stage > len(self.flip):
            self.done = True
            return
        if stage == 0:
            view, device = self.ref.at[self.me, self.mod], {"mod": 1 - self.mod}
        else:
            size = 1 << (stage - 1)
            view = self.ref.at[pl.ds(self.me // size * size, size)]
            device = {"dp": self.me + self.flip[stage - 1] * size}
        copy = remote(view, view, self.sems[0].at[stage], self.sems[1].at[stage], device)
        copy.start()
        self.copies.append(copy)

    def finish(self):
        for copy in self.copies:
            copy.wait_send()


def contrast_into(gathered_ref, pooled_ref, grad_ref, loss_ref, pool_ref, me, mod, items):
    count = gathered_ref.shape[0]
    width = pooled_ref.shape[2]
    total = items * count
    for half in range(2):
        for n in range(items):
            for part in range(width // 128):
                pooled_ref[half, n * count : (n + 1) * count, part * 128 : (part + 1) * 128] = gathered_ref[
                    :, half, n * (width // 128) + part, :
                ]
    flags = [gathered_ref[:, 0, items * (width // 128) + n, :][:, 0:1] for n in range(items)]
    present = jnp.concatenate(flags, axis=0)
    same = lax.broadcasted_iota(jnp.int32, (total, total), 0) == lax.broadcasted_iota(jnp.int32, (total, total), 1)
    same = jnp.where(same, 1.0, 0.0)
    present_row = column_sum(present * same)
    scale = LOGIT_SCALE / width
    units, inverses = [], []
    for half in range(2):
        pooled = pooled_ref[half]
        inverses.append(lax.rsqrt(jnp.mean(pooled * pooled, axis=-1, keepdims=True) + 1e-06))
        units.append(pooled * inverses[-1])
    exact = lax.Precision.HIGHEST
    logits = lax.dot_general(units[0], units[1], LAST, precision=exact, preferred_element_type=F32) * scale
    by_row = logits - 10000.0 * (1.0 - present_row)
    by_column = logits - 10000.0 * (1.0 - present)
    row_top = jnp.max(by_row, axis=1, keepdims=True)
    column_top = jnp.max(by_column, axis=0, keepdims=True)
    by_row = jnp.exp(by_row - row_top)
    by_column = jnp.exp(by_column - column_top)
    row_sum = jnp.sum(by_row, axis=1, keepdims=True)
    column_total = column_sum(by_column)
    row_part = present * (row_top + jnp.log(row_sum) - 2.0 * jnp.sum(logits * same, axis=1, keepdims=True))
    column_part = present_row * (column_top + jnp.log(column_total))
    loss = (jnp.sum(row_part) + jnp.sum(column_part)) / (2.0 * total)
    loss_ref[0, 0] = loss
    grad_logits = (
        present * by_row / row_sum + present_row * by_column / column_total - 2.0 * same * present
    ) * (scale / (2.0 * total))

    def own(half, grad_unit):
        unit = units[half]
        grad_ref[...] = inverses[half] * (grad_unit - unit * jnp.mean(grad_unit * unit, axis=-1, keepdims=True))

    @pl.when(mod == 0)
    def _():
        own(0, jnp.dot(grad_logits, units[1], precision=exact, preferred_element_type=F32))

    @pl.when(mod == 1)
    def _():
        own(1, lax.dot_general(grad_logits, units[0], FIRST, precision=exact, preferred_element_type=F32))

    for n in range(items):
        pool_ref[n : n + 1, :] = grad_ref[pl.ds(n * count + me, 1), :]


def forward_kernel(
    tokens_ref, grid_ref, gain_ref, norms_ref, cross_gain_hbm, present_ref, cotangent_ref,
    project_hbm, mixer_hbm, expand_hbm, reduce_hbm,
    query_hbm, keyval_hbm, cmixer_hbm, cexpand_hbm, creduce_hbm,
    encoded_out, normed_out, rows_out, probs_out, mixed_out, resid_out, normed_two_out, hidden_out, slope_out,
    part_out, query_in_out, keyval_in_out, cnormed_out, cmixed_out, chidden_out, branch_out, cgexp_out, cgattn_out,
    gq_out, gkv_out, cresid_out, joining_out,
    gains_ref, loss_ref, pool_ref,
    project_ref, mixer_ref, expand_ref, reduce_ref,
    cquery_ref, cmixer_ref, cexpand_ref, creduce_ref,
    encoded_ref, partner_ref, normed_ref, rows_ref, probs_ref, mixed_ref, resid_ref, normed_two_ref, hidden_ref,
    slope_keep_ref,
    cprobs_ref, cresid_ref, query_in_ref, keyval_in_ref, cnormed_ref,
    branch_ref, cgattn_ref, gmix_ref, part_ref, half_ref, joining_ref,
    gathered_ref, pooled_ref, grad_ref, dist_ref, cross_gain_ref,
    load_sems, out_sems, weight_sends, weight_recvs, gather_sends, gather_recvs, swap_sends, swap_recvs,
):
    items, patches, width = tokens_ref.shape
    half, wide = width // 2, 2 * width
    count = gathered_ref.shape[0]
    bits = count.bit_length() - 1
    me, mod = lax.axis_index("dp"), lax.axis_index("mod")
    is_radar = mod == 1
    across = {"mod": 1 - mod}
    own_columns = pl.ds(pl.multiple_of(mod * half, 128), half)
    loads = [
        pltpu.make_async_copy(source, target, load_sems.at[i])
        for i, (source, target) in enumerate(
            (
                (project_hbm, project_ref),
                (query_hbm, cquery_ref.at[0, :, own_columns]),
                (keyval_hbm, cquery_ref.at[1:3, :, own_columns]),
                (cmixer_hbm, cmixer_ref.at[own_columns]),
                (mixer_hbm, mixer_ref),
                (expand_hbm, expand_ref),
                (reduce_hbm, reduce_ref),
                (cexpand_hbm, cexpand_ref),
                (creduce_hbm, creduce_ref),
            )
        )
    ]
    begin(loads[0:4])
    weights = Weights((cquery_ref, cmixer_ref), me, mod, (weight_sends, weight_recvs))
    gather = Gather(gathered_ref, me, mod, bits, (gather_sends, gather_recvs))
    outputs = Outputs(out_sems)
    swaps = {}

    def swap(key, source, target):
        place = len(swaps)
        swaps[key] = remote(source, target, swap_sends.at[place], swap_recvs.at[place], across)
        swaps[key].start()

    barrier = pltpu.get_barrier_semaphore()
    others = [across] + [{"dp": me + flip * (1 << bit)} for bit, flip in enumerate(gather.flip)]
    for device in others:
        pl.semaphore_signal(barrier, inc=1, device_id=device, device_id_type=pl.DeviceIdType.MESH)
    cross_gain_ref[...] = cross_gain_hbm[...].reshape(1, width)
    for n in range(items):
        spans = []
        for axis in range(2):
            along = jnp.broadcast_to(grid_ref[n, axis : axis + 1, :].astype(F32), (8, patches))
            spans.append(along.T[:, 0:1] - along[0:1, :])
        dist_ref[n] = jnp.sqrt(spans[0] * spans[0] + spans[1] * spans[1])
    pl.semaphore_wait(barrier, len(others))

    def pump(*events):
        for event in events:
            weights.advance(*event)

    def encode_image(n, pumps):
        def put(key, source, target):
            outputs.emit(key, source, target.at[n])

        unit, _ = norm_rows(tokens_ref[n].astype(F32))
        outputs.ready("normed", "rows")
        normed_ref[...] = (unit * gain_ref[0:1, :]).astype(BF16)
        put("normed", normed_ref, normed_out)
        if n == 0:
            finish(loads[0:4])
            begin(loads[4:])
            pump((0, 0), (1, 0), (2, 0), (3, 0))
        for part in range(3):
            cut = slice(part * width, (part + 1) * width)
            rows_ref[:, cut] = dot(normed_ref[...], project_ref[:, cut]).astype(BF16)
        put("rows", rows_ref, rows_out)
        pump(*pumps[0])
        outputs.ready("probs", "mixed")
        attend(rows_ref, rows_ref, rows_ref, (0, width, 2 * width), dist_ref.at[n], probs_ref, mixed_ref)
        put("probs", probs_ref, probs_out)
        put("mixed", mixed_ref, mixed_out)
        pump(*pumps[1])
        if n == 0:
            loads[4].wait()
        outputs.ready("resid", "normed_two")
        resid = tokens_ref[n].astype(F32) + dot(mixed_ref[...], mixer_ref[...])
        resid_ref[...] = resid
        unit, _ = norm_rows(resid)
        normed_two_ref[...] = (unit * gain_ref[1:2, :]).astype(BF16)
        put("resid", resid_ref, resid_out)
        put("normed_two", normed_two_ref, normed_two_out)
        if n == 0:
            loads[5].wait()
        outputs.ready("hidden", "slope")
        for part in range(expand_ref.shape[1] // width):
            cut = slice(part * width, (part + 1) * width)
            value, slope = gelu_pair(dot(normed_two_ref[...], expand_ref[:, cut]))
            hidden_ref[:, cut] = value.astype(BF16)
            slope_keep_ref[:, cut] = slope.astype(BF16)
        pump(*pumps[2])
        if n == 0:
            loads[6].wait()
        encoded = (resid_ref[...] + dot(hidden_ref[...], reduce_ref[...])).astype(BF16)
        encoded_ref[n] = encoded
        swap(n, encoded_ref.at[n], partner_ref.at[n])
        put("encoded", encoded_ref.at[n], encoded_out)
        put("hidden", hidden_ref, hidden_out)
        put("slope", slope_keep_ref, slope_out)
        pooled = jnp.mean(encoded.astype(F32), axis=0, keepdims=True)
        if n == 0:
            gathered_ref[me, mod] = jnp.zeros(gathered_ref.shape[2:], F32)
        for part in range(width // 128):
            place = n * (width // 128) + part
            gathered_ref[me, mod, place : place + 1, :] = pooled[:, part * 128 : (part + 1) * 128]
        place = items * (width // 128) + n
        gathered_ref[me, mod, place : place + 1, :] = jnp.full((1, 128), present_ref[n], jnp.int32).astype(F32)
        pump(*pumps[3])

    encode_image(0, ((), ((0, 1), (1, 1)), ((2, 1),), ((3, 1), (0, 2))))
    encode_image(1, (((1, 2),), ((2, 2), (3, 2), (0, 3)), ((1, 3), (2, 3)), ((3, 3),)))
    gather.advance()
    starts = (0, 0, width)
    outputs.ready("hidden", "slope")
    images = [slice(n * patches, (n + 1) * patches) for n in range(items)]
    q_refs = [project_ref.at[own, 0:width] for own in images]
    kv_refs = [project_ref.at[own, width : 3 * width] for own in images]
    gq_refs = [expand_ref.at[own, 0:width] for own in images]
    gkv_refs = [expand_ref.at[own, width : 3 * width] for own in images]
    cmixed_refs = [mixer_ref.at[own] for own in images]
    chidden_refs = [hidden_ref.at[:, n * wide : (n + 1) * wide] for n in range(items)]
    cgexp_refs = [slope_keep_ref.at[:, n * wide : (n + 1) * wide] for n in range(items)]

    def join_attend(n):
        def put(key, source, target):
            outputs.emit(key, source.at[n], target.at[n])

        swaps[n].wait_recv()
        own, other = encoded_ref[n], partner_ref[n]
        unit, _ = norm_rows(jnp.where(is_radar, own, other).astype(F32))
        query_in_ref[n] = (unit * norms_ref[1:2, :]).astype(BF16)
        unit, _ = norm_rows(jnp.where(is_radar, other, own).astype(F32))
        keyval_in_ref[n] = (unit * norms_ref[0:1, :]).astype(BF16)
        put("query_in", query_in_ref, query_in_out)
        put("keyval_in", keyval_in_ref, keyval_in_out)
        if n == 0:
            pump((0, 4), (1, 4), (2, 4), (3, 4))
            finish(loads[7:9])
        q_refs[n][...] = dot(query_in_ref[n], cquery_ref[0]).astype(BF16)
        for part in range(2):
            kv_refs[n][:, part * width : (part + 1) * width] = dot(keyval_in_ref[n], cquery_ref[1 + part]).astype(BF16)
        gather.advance()
        kv = kv_refs[n]
        attend(q_refs[n], kv, kv, starts, dist_ref.at[n], cprobs_ref.at[n], cmixed_refs[n])
        outputs.emit("cmixed", cmixed_refs[n].at[:, own_columns], cmixed_out.at[n])
        gather.advance()
        radar = jnp.where(is_radar, encoded_ref[n], partner_ref[n]).astype(F32)
        resid = radar + dot(cmixed_refs[n][...], cmixer_ref[...])
        cresid_ref[n] = resid
        unit, _ = norm_rows(resid)
        cnormed_ref[n] = (unit * cross_gain_ref[...]).astype(BF16)
        put("cresid", cresid_ref, cresid_out)
        put("cnormed", cnormed_ref, cnormed_out)
        branch_ref[n] = (present_ref[n].astype(F32) * cotangent_ref[n].astype(F32)).astype(BF16)
        put("branch", branch_ref, branch_out)

    def join_feed(n):
        for part in range(wide // width):
            cut = slice(part * width, (part + 1) * width)
            value, slope = gelu_pair(dot(cnormed_ref[n], cexpand_ref[:, cut]))
            chidden_refs[n][:, cut] = value.astype(BF16)
            upstream = dot_last(branch_ref[n], creduce_ref[cut, :])
            cgexp_refs[n][:, cut] = (upstream * slope).astype(BF16)
        half_ref[0, n] = dot_last(cgexp_refs[n][...], cexpand_ref[...]).astype(BF16)
        swap(("half", n), half_ref.at[0, n], half_ref.at[1, n])
        outputs.emit("chidden", chidden_refs[n], chidden_out.at[n])
        outputs.emit("cgexp", cgexp_refs[n], cgexp_out.at[n])
        gather.advance()

    def join_back(n):
        def put(key, source, target):
            outputs.emit(key, source.at[n], target.at[n])

        swaps["half", n].wait_recv()
        grad_normed = half_ref[0, n].astype(F32) + half_ref[1, n].astype(F32)
        unit, inverse = norm_rows(cresid_ref[n])
        sums = column_sum(grad_normed * unit)
        gains_ref[1:2, :] = sums if n == 0 else gains_ref[1:2, :] + sums
        present = present_ref[n].astype(F32)
        grad = present * cotangent_ref[n].astype(F32) + norm_back(grad_normed, unit, inverse, cross_gain_ref[...])
        part_ref[n] = grad
        cgattn_ref[n] = grad.astype(BF16)
        put("cgattn", cgattn_ref, cgattn_out)
        gmix_ref[...] = dot_last(cgattn_ref[n], cmixer_ref[...]).astype(BF16)
        gather.advance()
        kv, gq, gkv = kv_refs[n], gq_refs[n], gkv_refs[n]
        attend_back(q_refs[n], kv, kv, starts, cprobs_ref.at[n], gmix_ref, (gq, gkv, gkv), (0, 0, width))
        outputs.emit("gq", gq.at[:, own_columns], gq_out.at[n])
        outputs.emit("gkv", gkv.at[:, own_columns], gkv_out.at[n, :, 0:half])
        second = pl.ds(pl.multiple_of(width + mod * half, 128), half)
        outputs.emit("gkv", gkv.at[:, second], gkv_out.at[n, :, half:width])
        gather.advance()

        def to_own(grad_in, gain, residual):
            unit, inverse = norm_rows(encoded_ref[n].astype(F32))
            sums = column_sum(grad_in * unit)
            gains_ref[0:1, :] = sums if n == 0 else gains_ref[0:1, :] + sums
            grad_in = norm_back(grad_in, unit, inverse, gain)
            part_ref[n] = part_ref[n] + grad_in if residual else grad_in

        @pl.when(is_radar)
        def _():
            to_own(dot_last(gq_refs[n][...], cquery_ref[0]), norms_ref[1:2, :], True)

        @pl.when(mod == 0)
        def _():
            grad_in = dot_last(gkv_refs[n][:, 0:width], cquery_ref[1])
            grad_in = grad_in + dot_last(gkv_refs[n][:, width : 2 * width], cquery_ref[2])
            to_own(grad_in, norms_ref[0:1, :], False)

        put("part", part_ref, part_out)

    for n in range(items):
        join_attend(n)
        join_feed(n)
    for n in range(items):
        joining_ref[n] = dot(chidden_refs[n][...], creduce_ref[...]).astype(BF16)
        outputs.emit("joining", joining_ref.at[n], joining_out.at[n])
    for n in range(items):
        join_back(n)
    while not gather.done:
        gather.advance()
    contrast_into(gathered_ref, pooled_ref, grad_ref, loss_ref, pool_ref, me, mod, items)
    for copy in swaps.values():
        copy.wait_send()
    weights.finish()
    gather.finish()
    outputs.finish()


def forward(tokens, grid, gains, norms, cross_gain, present, cotangent, weights, cross, count):
    items, patches, width = tokens.shape
    half, wide, full = width // 2, 2 * width, 4 * width
    bits = count.bit_length() - 1
    pairs = HEADS // 2

    def out(*dims, dtype=BF16):
        return shape((items, patches, *dims), dtype)

    outs = (
        out(width), out(width), out(3 * width), shape((items, pairs, patches, 2 * patches), BF16), out(width),
        out(width, dtype=F32), out(width), out(full), out(full),
        out(width, dtype=F32), out(width), out(width), out(width), out(half), out(wide), out(width), out(wide), out(width),
        out(half), out(width), out(width, dtype=F32), out(width),
    )
    row, probs = (patches, width), (pairs, patches, 2 * patches)

    def both(*dims, dtype=BF16):
        return pltpu.VMEM((items, *dims), dtype)

    scratch = [pltpu.VMEM(w.shape, BF16) for w in weights]
    scratch += [pltpu.VMEM(d, BF16) for d in ((3, width, width), (width, width), (width, wide), (wide, width))]
    scratch += [both(*row), both(*row)]
    scratch += [pltpu.VMEM(d, BF16) for d in (row, (patches, 3 * width), probs, row)]
    scratch += [pltpu.VMEM(row, F32), pltpu.VMEM(row, BF16), pltpu.VMEM((patches, full), BF16), pltpu.VMEM((patches, full), BF16)]
    scratch += [both(*probs), both(*row, dtype=F32), both(*row), both(*row), both(*row)]
    scratch += [both(*row), both(*row), pltpu.VMEM(row, BF16), both(*row, dtype=F32)]
    scratch += [pltpu.VMEM((2, items, *row), BF16), both(*row)]
    scratch += [
        pltpu.VMEM((count, 2, 16, 128), F32),
        pltpu.VMEM((2, items * count, width), F32),
        pltpu.VMEM((items * count, width), F32),
        pltpu.VMEM((items, patches, patches), F32),
        pltpu.VMEM((1, width), F32),
    ]
    dma = pltpu.SemaphoreType.DMA
    scratch += [dma((9,)), dma((2 * 24,)), dma((4, 8)), dma((4, 8)), dma((bits + 1,)), dma((bits + 1,)), dma((5,)), dma((5,))]
    return pl.pallas_call(
        forward_kernel,
        out_shape=outs + (shape((2, width), F32), shape((1, 1), F32), shape((items, width), F32)),
        in_specs=[VMEM, VMEM, VMEM, VMEM, VMEM, SMEM, VMEM] + [ANY] * 9,
        out_specs=(ANY,) * len(outs) + (VMEM, SMEM, VMEM),
        scratch_shapes=scratch,
        compiler_params=pltpu.CompilerParams(
            collective_id=1, has_side_effects=True, vmem_limit_bytes=63 * 1024 * 1024
        ),
        cost_estimate=cost(items * patches * 40 * width * width, 60 * 2**20),
        name="forward",
    )(tokens, grid, gains, norms, cross_gain, present, cotangent, *weights, *cross)


DEPTH = 2


class Halvings:
    def __init__(self, orders, held, got, sems, me, make, result):
        self.orders, self.held, self.got, self.sems = orders, held, got, sems
        self.make_chunk, self.result = make, result
        self.bits = len(orders[0])
        self.every = list(range(self.bits))[::-1]
        self.mine = ring_bits(me, self.bits)
        self.partners = [{"dp": me + (1 - 2 * bit) * (1 << place)} for place, bit in enumerate(self.mine)]
        self.copies, self.waited, self.done = {}, set(), set()
        self.total = len(orders)

    def held_at(self, chunk, stage):
        return self.held[stage].at[self.place[chunk] % self.held[stage].shape[0]]

    def got_at(self, chunk, stage):
        return self.got[stage].at[self.place[chunk] % self.got[stage].shape[0]]

    def before(self, chunk, stage):
        place = self.place[chunk] - self.held[stage].shape[0]
        return self.order[place] if place >= 0 else None

    def part(self, chunk, stage, kept):
        bit = self.orders[chunk][stage]
        left = [other for other in self.every if other not in self.orders[chunk][:stage]]
        side = self.mine[bit] if kept else 1 - self.mine[bit]
        return self.held_at(chunk, stage).at[tuple(side if other == bit else slice(None) for other in left)]

    def send(self, chunk, stage):
        copy = remote(
            self.part(chunk, stage, False), self.got_at(chunk, stage),
            self.sems[0].at[stage, chunk], self.sems[1].at[stage, chunk],
            self.partners[self.orders[chunk][stage]],
        )
        copy.start()
        self.copies[chunk, stage] = copy

    def free(self, chunk, stage):
        last = self.before(chunk, stage)
        if last is not None and (last, stage) not in self.waited:
            self.copies[last, stage].wait_send()
            self.waited.add((last, stage))

    def make(self, chunk, enter=None):
        if not 0 <= chunk < self.total or (chunk, "made") in self.done:
            return
        self.done.add((chunk, "made"))
        last = self.before(chunk, 0)
        assert last is None or (last, 0) in self.done
        self.free(chunk, 0)
        self.make_chunk(chunk, self.held_at(chunk, 0))
        if enter is not None:
            enter()
        self.send(chunk, 0)

    def take(self, chunk, stage):
        if not 0 <= chunk < self.total or (chunk, stage) in self.done:
            return
        self.done.add((chunk, stage))
        self.copies[chunk, stage].wait_recv()
        kept, arrived = self.part(chunk, stage, True), self.got_at(chunk, stage)
        if stage == self.bits - 1:
            self.result(chunk, kept[...].astype(F32) + arrived[...].astype(F32))
            return
        last = self.before(chunk, stage + 1)
        assert last is None or (last, stage + 1) in self.done
        self.free(chunk, stage + 1)
        target = self.held_at(chunk, stage + 1)
        target[...] = kept[...] + arrived[...]
        if stage:
            self.send(chunk, stage + 1)

    def schedule(self, first, aside, enter):
        self.first, self.aside, self.at = first, aside, 0
        self.needed = [[c] for c in first[DEPTH:]] + [[]] * (DEPTH + 1)
        for chunk, at in aside.items():
            self.needed[at] = self.needed[at] + [chunk]
        order = first[:DEPTH] + [chunk for step in self.needed for chunk in step]
        self.order, self.following = order, dict(zip(order, order[1:]))
        self.place = {chunk: place for place, chunk in enumerate(order)}
        for place, chunk in enumerate(order[: DEPTH + len(self.needed[0])]):
            self.make(chunk, None if place else enter)
            if 0 < place <= DEPTH:
                self.take(first[place - 1], 0)
                self.send(first[place - 1], 1)

    def prepare(self):
        if self.at + 1 < len(self.needed):
            for chunk in self.needed[self.at + 1]:
                self.make(chunk)

    def step(self):
        first, at = self.first, self.at
        self.at += 1
        for chunk in self.needed[at] if at < len(self.needed) else []:
            self.take(chunk, 0)
        if at < len(first):
            self.take(first[at], 1)
        if at + DEPTH < len(first):
            self.send(first[at + DEPTH], 1)
        for chunk, start in self.aside.items():
            if at == start:
                self.send(chunk, 1)
            for stage, delay in ((1, 2), (2, 4), (3, 5)):
                if at == start + delay:
                    self.take(chunk, stage)
        for stage in range(2, self.bits):
            if 0 <= at + 1 - stage < len(first):
                self.take(first[at + 1 - stage], stage)

    def unfinished(self):
        return any((chunk, self.bits - 1) not in self.done for chunk in range(self.total))

    def finish(self):
        for key, copy in self.copies.items():
            if key not in self.waited:
                copy.wait_send()


def backward_kernel(
    plan, results, sizes,
    pool_ref, gain_ref, cross_gains_ref, part_hbm, cotangent_hbm, tokens_hbm, resid_hbm, slope_hbm, rows_hbm, probs_hbm,
    project_hbm, mixer_hbm, expand_hbm, reduce_hbm, *rest,
):
    n_in, n_out, bits, aside = sizes
    present_ref, cresid_hbm, joining_hbm = rest[:3]
    rest = rest[3:]
    operands, rest = rest[:n_in], rest[n_in:]
    joined_out, patch_out, outs, vector_out = rest[0], rest[1], rest[2 : 2 + n_out], rest[2 + n_out]
    scratch = rest[3 + n_out :]
    (
        project_ref, mixer_ref, expand_ref, reduce_ref,
        patch_ref, cotangent_ref, tokens_ref, resid_ref, slope_ref, rows_ref, probs_ref,
        branch_ref, gexp_ref, gattn_ref, grows_ref, gmix_ref, left_ref, right_ref, joining_ref,
    ) = scratch[:19]
    scratch = scratch[19:]
    held, got = scratch[:bits], scratch[bits : 2 * bits]
    vector_held, vector_got = scratch[2 * bits : 3 * bits], scratch[3 * bits : 4 * bits]
    load_sems, left_sems, right_sems, out_sems, send_sems, recv_sems, vector_sends, vector_recvs, swap_sems = scratch[4 * bits :]
    items, patches = pool_ref.shape[0], resid_ref.shape[0] // pool_ref.shape[0]
    width = patch_ref.shape[1]
    me = lax.axis_index("dp")
    resident = {"branch": branch_ref, "gexp": gexp_ref, "gattn": gattn_ref, "grows": grows_ref}
    fetched, loaded, slots = {}, {}, [0, 0]

    def fetch(kind, key, source, target_of, sems):
        if loaded.get(kind, [None])[-1] == key:
            return fetched[key]
        buffers = target_of.shape[0]
        slot = slots[kind] % buffers
        slots[kind] += 1
        copy = pltpu.make_async_copy(source, target_of.at[slot, :, 0 : source.shape[1]], sems.at[slots[kind] - 1])
        copy.start()
        fetched[key] = [slot, copy]
        loaded.setdefault(kind, []).append(key)
        return fetched[key]

    def fetch_chunk(chunk):
        if chunk >= len(plan):
            return
        for left, right, start, size, _ in plan[chunk]:
            if not isinstance(left, str):
                fetch(0, ("left", left), operands[left], left_ref, left_sems)
            if not isinstance(right, str):
                fetch(1, ("right", right, start), operands[right].at[:, start : start + size], right_ref, right_sems)

    def arrived(key):
        entry = fetched[key]
        if entry[1] is not None:
            entry[1].wait()
            entry[1] = None
        return entry[0]

    def make_chunk(chunk, target):
        fetch_chunk(sums.following.get(chunk, len(plan)))
        block = target.shape[-2]
        for left, right, start, size, place in plan[chunk]:
            one = resident[left][...] if isinstance(left, str) else left_ref[arrived(("left", left))]
            if isinstance(right, str):
                other = resident[right][:, start : start + size]
            else:
                other = right_ref[arrived(("right", right, start)), :, 0:size]
            product = dot_first(one, other).astype(BF16)
            for index in range(1 << bits):
                where = tuple((index >> bit) & 1 for bit in range(bits)[::-1])
                target[(*where, slice(None), slice(place, place + size))] = product[index * block : (index + 1) * block]

    def result(chunk, value):
        for out, column, first, size in results[chunk]:
            if len(outs[out].shape) == 3:
                outs[out][column] = value[:, first : first + size]
            else:
                outs[out][:, column : column + size] = value[:, first : first + size]

    fetch_chunk(0)
    loads = [
        pltpu.make_async_copy(source, target, load_sems.at[i])
        for i, (source, target) in enumerate(
            (
                (part_hbm, patch_ref), (cotangent_hbm, cotangent_ref), (reduce_hbm, reduce_ref), (slope_hbm, slope_ref),
                (expand_hbm, expand_ref), (resid_hbm, resid_ref), (mixer_hbm, mixer_ref), (rows_hbm, rows_ref),
                (probs_hbm, probs_ref), (project_hbm, project_ref), (tokens_hbm, tokens_ref),
            )
        )
    ]
    orders = [(0, 2, 3, 1) if chunk in aside else (0, 1, 2, 3) for chunk in range(len(plan))]
    sums = Halvings(orders, held, got, (send_sems, recv_sems), me, make_chunk, result)
    barrier = pltpu.get_barrier_semaphore()
    across = {"mod": 1 - lax.axis_index("mod")}
    for device in [*sums.partners, across]:
        pl.semaphore_signal(barrier, inc=1, device_id=device, device_id_type=pl.DeviceIdType.MESH)
    sums.schedule(
        [chunk for chunk in range(len(plan)) if chunk not in aside], aside,
        lambda: pl.semaphore_wait(barrier, bits + 1),
    )
    begin(loads[0:4])
    joining_swap = remote(joining_hbm, joining_ref, swap_sems.at[0], swap_sems.at[1], across)
    joining_swap.start()
    sums.prepare()

    images = [slice(n * patches, (n + 1) * patches) for n in range(items)]
    finish(loads[0:4])
    begin(loads[4:])
    for n, own in enumerate(images):
        grad = cotangent_ref[own].astype(F32) + pool_ref[n : n + 1, :] * (1.0 / patches) + patch_ref[own]
        patch_ref[own] = grad
        branch_ref[own] = grad.astype(BF16)
    for part in range(expand_ref.shape[1] // width):
        cut = slice(part * width, (part + 1) * width)
        upstream = dot_last(branch_ref[...], reduce_ref[cut, :])
        gexp_ref[:, cut] = (upstream * slope_ref[:, cut].astype(F32)).astype(BF16)
    sums.step()
    sums.prepare()
    finish(loads[4:6])
    gains = []
    for own in images:
        grad_normed = dot_last(gexp_ref[own], expand_ref[...])
        unit, inverse = norm_rows(resid_ref[own])
        gains.append(column_sum(grad_normed * unit))
        grad = patch_ref[own] + norm_back(grad_normed, unit, inverse, gain_ref[1:2, :])
        patch_ref[own] = grad
        gattn_ref[own] = grad.astype(BF16)
    second_gain = sum(gains)
    late = [
        pltpu.make_async_copy(cresid_hbm, resid_ref, load_sems.at[11]),
        pltpu.make_async_copy(joining_hbm, cotangent_ref, load_sems.at[12]),
    ]
    begin(late)
    sums.step()
    sums.prepare()
    finish(loads[6:9])
    gmix_ref[...] = dot_last(gattn_ref[...], mixer_ref[...]).astype(BF16)
    starts = (0, width, 2 * width)
    for n, own in enumerate(images):
        rows, grows = rows_ref.at[own], grows_ref.at[own]
        attend_back(rows, rows, rows, starts, probs_ref.at[n], gmix_ref.at[own], (grows,) * 3, starts)
        sums.step()
        sums.prepare()
    finish(loads[9:11])
    gains = []
    for n, own in enumerate(images):
        grad_normed = dot_last(grows_ref[own], project_ref[...])
        unit, inverse = norm_rows(tokens_ref[own].astype(F32))
        gains.append(column_sum(grad_normed * unit))
        patch_ref[own] = patch_ref[own] + norm_back(grad_normed, unit, inverse, gain_ref[0:1, :])
    patch_copy = pltpu.make_async_copy(patch_ref, patch_out, out_sems.at[0])
    patch_copy.start()
    finish(late)
    joining_swap.wait_recv()
    for n, own in enumerate(images):
        branch = cotangent_ref[own].astype(F32) + joining_ref[own].astype(F32)
        cotangent_ref[own] = (present_ref[n].astype(F32) * (resid_ref[own] + branch)).astype(BF16)
    joined_copy = pltpu.make_async_copy(cotangent_ref, joined_out, out_sems.at[1])
    joined_copy.start()
    rows = jnp.concatenate([sum(gains), second_gain, cross_gains_ref[...], jnp.zeros((4, width), F32)], axis=0)
    block = width >> bits
    for index in range(1 << bits):
        where = tuple((index >> bit) & 1 for bit in range(bits)[::-1])
        piece = rows[:, index * block : (index + 1) * block]
        vector_held[0][where] = jnp.concatenate([piece, jnp.zeros((8, 128 - block), F32)], axis=1)
    vector_copies = []

    def vector_step():
        stage = len(vector_copies)
        if stage > bits:
            return
        if stage:
            bit = stage - 1
            vector_copies[-1].wait_recv()
            left = list(range(bit, bits))[::-1]
            kept = vector_held[bit].at[tuple(sums.mine[bit] if other == bit else slice(None) for other in left)]
            value = kept[...] + vector_got[bit][...]
            if stage == bits:
                vector_out[...] = value
                vector_copies.append(None)
                return
            vector_held[stage][...] = value
        left = list(range(stage, bits))[::-1]
        view = vector_held[stage].at[tuple(1 - sums.mine[stage] if other == stage else slice(None) for other in left)]
        copy = remote(view, vector_got[stage], vector_sends.at[stage], vector_recvs.at[stage], sums.partners[stage])
        copy.start()
        vector_copies.append(copy)

    while sums.unfinished():
        vector_step()
        sums.step()
        sums.prepare()
    while len(vector_copies) <= bits:
        vector_step()
    for copy in vector_copies[:bits]:
        copy.wait_send()
    sums.finish()
    joining_swap.wait_send()
    patch_copy.wait()
    joined_copy.wait()


def backward(pool, gains, cross_gains, activations, weights, joining, operands, plan, results, outs, aside, count):
    part, cotangent, tokens, resid, slope, rows, probs = activations
    total_rows, width = tokens.shape
    bits = count.bit_length() - 1
    block, chunks = width // count, len(plan)
    two = (2,) * bits
    full, pairs = slope.shape[1], probs.shape[1:]
    held, got = (3, 6, 5, 5), (6, 8, 6, 6)
    flat = (total_rows, width)
    lefts = [key for chunk in plan for key in chunk]
    dma = pltpu.SemaphoreType.DMA
    scratch = [pltpu.VMEM(w.shape, BF16) for w in weights]
    scratch += [pltpu.VMEM(flat, F32), pltpu.VMEM(flat, BF16), pltpu.VMEM(flat, BF16), pltpu.VMEM(flat, F32)]
    scratch += [pltpu.VMEM((total_rows, full), BF16), pltpu.VMEM((total_rows, 3 * width), BF16), pltpu.VMEM(probs.shape, BF16)]
    scratch += [pltpu.VMEM(flat, BF16), pltpu.VMEM((total_rows, full), BF16), pltpu.VMEM(flat, BF16)]
    scratch += [pltpu.VMEM((total_rows, 3 * width), BF16), pltpu.VMEM(flat, BF16)]
    scratch += [pltpu.VMEM((3, *flat), BF16), pltpu.VMEM((3, *flat), BF16), pltpu.VMEM(flat, BF16)]
    scratch += [pltpu.VMEM((held[stage], *two[stage:], block, width), BF16) for stage in range(bits)]
    scratch += [pltpu.VMEM((got[stage], *two[stage + 1 :], block, width), BF16) for stage in range(bits)]
    scratch += [pltpu.VMEM((*two[stage:], 8, 128), F32) for stage in range(bits)]
    scratch += [pltpu.VMEM((*two[stage + 1 :], 8, 128), F32) for stage in range(bits)]
    scratch += [dma((13,)), dma((len(lefts),)), dma((len(lefts),)), dma((2,)), dma((bits, chunks)), dma((bits, chunks))]
    scratch += [dma((bits,)), dma((bits,)), dma((2,))]
    return pl.pallas_call(
        functools.partial(backward_kernel, plan, results, (len(operands), len(outs), bits, aside)),
        out_shape=(shape(flat, BF16), shape(flat, F32), *(shape(dims, F32) for dims in outs), shape((8, 128), F32)),
        in_specs=[VMEM] * 3 + [ANY] * (7 + 4) + [SMEM] + [ANY] * (2 + len(operands)),
        out_specs=(ANY, ANY) + (VMEM,) * (len(outs) + 1),
        scratch_shapes=scratch,
        compiler_params=pltpu.CompilerParams(
            collective_id=0, has_side_effects=True, vmem_limit_bytes=63 * 1024 * 1024
        ),
        cost_estimate=cost(total_rows * (chunks + 12) * width * width, 60 * 2**20),
        name="backward",
    )(pool, gains, cross_gains, *activations, *weights, *joining, *operands)


def flipped(array, axis, bit):
    return lax.ppermute(array, axis, [(i, i ^ (1 << bit)) for i in range(lax.axis_size(axis))])


def block_order(width, count):
    bits = count.bit_length() - 1
    block = width // count
    rows = jnp.arange(width)
    place = rows // block
    partner = jnp.zeros_like(place)
    for bit in range(bits):
        partner = partner | (((place >> (bits - 1 - bit)) & 1) << bit)
    source = (lax.axis_index("dp") ^ partner) * block + rows % block
    return (source[:, None] == jnp.arange(width)[None, :]).astype(BF16)


def ordered(order, values):
    return jnp.einsum("jd,rd->jr", order, values, preferred_element_type=F32).astype(BF16)


def summed(left_rows, grad_rows):
    count = lax.axis_size("dp")
    half = left_rows.shape[0] // 2
    send = jnp.dot(left_rows[half:], grad_rows, preferred_element_type=F32).astype(BF16)
    keep = jnp.dot(left_rows[:half], grad_rows, preferred_element_type=F32).astype(BF16)
    bits = count.bit_length() - 1
    for bit in range(bits):
        got = flipped(send, "dp", bit)
        if bit == bits - 1:
            return keep.astype(F32) + got.astype(F32)
        half = half // 2
        send = (keep[half:].astype(F32) + got[half:].astype(F32)).astype(BF16)
        keep = (keep[:half].astype(F32) + got[:half].astype(F32)).astype(BF16)


def summed_blocks(blocks):
    bits = lax.axis_size("dp").bit_length() - 1
    for bit in range(bits):
        half = blocks.shape[0] // 2
        blocks = blocks[:half] + flipped(blocks[half:], "dp", bit)
    return blocks[0]


def backward_plan(rows, half):
    wide = 2 * rows
    plan, results, outs = [], [], []

    def add(left, right, columns):
        outs.append(columns)
        for start in range(0, columns, rows):
            plan.append([(left, right, start, rows, 0)])
            results.append([(len(outs) - 1, start, 0, rows)])

    add(0, 1, wide)
    add(2, 3, wide)
    outs.extend([half, half])
    plan.append([(4, 5, 0, half, 0), (6, 7, 0, half, half)])
    results.append([(2, 0, 0, half), (3, 0, half, half)])
    outs.append(None)
    plan.append([(8, 9, 0, rows, 0)])
    results.append([(4, 0, 0, half), (4, 1, half, half)])
    add("branch", 10, 4 * rows)
    add(11, "gexp", 4 * rows)
    add(12, "gattn", rows)
    add(13, "grows", 3 * rows)
    return plan, results, outs


def finish_kernel(count, *refs):
    sources, loss_ref, vector_ref = refs[:count], refs[count], refs[count + 1]
    targets = refs[count + 2 : 2 * count + 2]
    loss_out, gains_ref, norms_ref, cross_gain_ref = refs[2 * count + 2 : 2 * count + 6]
    kept, (in_sems, out_sems) = refs[2 * count + 6 : 3 * count + 6], refs[3 * count + 6 :]
    arrivals = [pltpu.make_async_copy(a, b, in_sems.at[i]) for i, (a, b) in enumerate(zip(sources, kept))]
    departures = [pltpu.make_async_copy(a, b, out_sems.at[i]) for i, (a, b) in enumerate(zip(kept, targets))]
    begin(arrivals)
    block = gains_ref.shape[1]
    loss_out[0, 0] = loss_ref[0, 0]
    gains_ref[...] = vector_ref[0:2, 0:block]
    norms_ref[...] = vector_ref[2:3, 0:block]
    cross_gain_ref[...] = vector_ref[3:4, 0:block]
    for arrival, departure in zip(arrivals, departures):
        arrival.wait()
        departure.start()
    finish(departures)


def finished(arrays, loss, vector, block):
    small = [shape((1, 1), F32), shape((2, block), F32), shape((1, block), F32), shape((1, block), F32)]
    count = len(arrays)
    return pl.pallas_call(
        functools.partial(finish_kernel, count),
        out_shape=tuple(shape(a.shape, a.dtype) for a in arrays) + tuple(small),
        in_specs=[ANY] * count + [SMEM, VMEM],
        out_specs=(ANY,) * count + (SMEM, VMEM, VMEM, VMEM),
        scratch_shapes=[pltpu.VMEM(a.shape, a.dtype) for a in arrays] + [pltpu.SemaphoreType.DMA((count,))] * 2,
        compiler_params=limits(),
        name="finish",
    )(*arrays, loss, vector)


def shards(
    patch_tokens,
    grid_coords,
    has_radar,
    enc_gains,
    enc_project,
    enc_mixer,
    enc_expand,
    enc_reduce,
    cross_norms,
    cross_gain,
    cross_query,
    cross_keyval,
    cross_mixer,
    cross_expand,
    cross_reduce,
    enc_cotangent,
    joined_cotangent,
):
    item_count, patches, model_width = patch_tokens.shape[1:]
    images = range(item_count)
    dp_size = lax.axis_size("dp")
    weights = (enc_project[0], enc_mixer[0], enc_expand[0], enc_reduce[0])
    cross_weights = (cross_query, cross_keyval, cross_mixer, cross_expand, cross_reduce)

    (encoded, normed, rows, probs, mixed, resid, normed_two, hidden, slope,
     part, query_in, keyval_in, cnormed, cmixed, chidden, branch, cgexp, cgattn, gq, gkv,
     cresid, joining, cross_gains, loss, pool_grad) = forward(
        patch_tokens[0], grid_coords, enc_gains[0], cross_norms, cross_gain, has_radar,
        joined_cotangent, weights, cross_weights, dp_size,
    )

    block = model_width // dp_size

    def flat(values):
        return values.reshape(item_count * patches, *values.shape[2:])

    weight_operands = [
        flat(v)
        for v in (
            branch, chidden, cnormed, cgexp, query_in, gq, cgattn, cmixed, keyval_in, gkv, hidden, normed_two, mixed, normed
        )
    ]
    if dp_size == 16 and block % 16 == 0:
        plan, places, outs = backward_plan(model_width, model_width // 2)
        dims = [(2, block, model_width // 2) if columns is None else (block, columns) for columns in outs]
        activations = [flat(v) for v in (part, enc_cotangent[0], patch_tokens[0], resid, slope, rows)] + [probs]
        results = backward(
            pool_grad, enc_gains[0], cross_gains, activations, weights, (has_radar, flat(cresid), flat(joining)), weight_operands,
            plan, places, dims, {4: 2, 9: 6, 14: 10},
            dp_size,
        )
        joined_tokens, vector_sum = results[0].reshape(encoded.shape), results[-1]
        results = results[1:-1]
    else:
        back = [
            encode_back(
                enc_cotangent[0, n], part[n], pool_grad[n : n + 1], enc_gains[0], patch_tokens[0, n],
                resid[n], slope[n], rows[n], probs[n], *weights,
            )
            for n in images
        ]
        patch_grad = jnp.concatenate([one[0] for one in back])
        both = joining.astype(F32) + flipped(joining, "mod", 0).astype(F32)
        joined_tokens = (has_radar.astype(F32)[:, None, None] * (cresid + both)).astype(BF16)
        grads = [jnp.concatenate([one[place] for one in back]) for place in range(1, 5)]
        order = block_order(model_width, dp_size)
        pairs = [(weight_operands[2 * n], weight_operands[2 * n + 1]) for n in range(5)]
        pairs += [(grads[0], weight_operands[10])]
        pairs += [(weight_operands[11 + n], grads[1 + n]) for n in range(3)]
        results = [patch_grad] + [summed(ordered(order, left), right) for left, right in pairs]
        results[5] = jnp.stack([results[5][:, : model_width // 2], results[5][:, model_width // 2 :]])
        vectors = jnp.concatenate([back[0][5] + back[1][5], cross_gains])
        blocks = jnp.moveaxis(vectors.reshape(4, dp_size, block), 1, 0)
        wanted = jnp.dot(order[::block, ::block].astype(F32), blocks.reshape(dp_size, -1), precision=lax.Precision.HIGHEST)
        vector_sum = summed_blocks(wanted.reshape(blocks.shape))
        vector_sum = jnp.pad(vector_sum, ((0, 4), (0, 128 - block)))
    (encoded, joined_tokens, patch_grad, creduce_sum, cexpand_sum, query_sum, cmixer_sum, keyval_sum, reduce_sum, expand_sum,
     mixer_sum, project_sum, loss, gains_sum, norms_sum, cross_gain_sum) = finished(
        [encoded, joined_tokens, *results], loss, vector_sum, block
    )
    return (
        encoded[None],
        joined_tokens,
        loss.reshape(()),
        patch_grad.reshape(patch_tokens.shape),
        gains_sum[None],
        project_sum[None],
        mixer_sum[None],
        expand_sum[None],
        reduce_sum.T[None],
        norms_sum,
        cross_gain_sum.reshape(block),
        query_sum,
        keyval_sum,
        cmixer_sum.T,
        cexpand_sum,
        creduce_sum.T,
    )


def solution(mesh):
    placed = (
        P("mod", "dp", None, None),
        P("dp", None, None),
        P("dp"),
        P("mod", None, None),
        P("mod", None, None),
        P("mod", None, None),
        P("mod", None, None),
        P("mod", None, None),
        P(),
        P(),
        P(None, "mod"),
        P(None, None, "mod"),
        P("mod", None),
        P(None, "mod"),
        P("mod", None),
        P("mod", "dp", None, None),
        P("dp", None, None),
    )
    return jax.shard_map(
        shards,
        mesh=mesh,
        in_specs=placed,
        out_specs=(
            P("mod", "dp", None, None),
            P("dp", None, None),
            P(),
            P("mod", "dp", None, None),
            P("mod", None, "dp"),
            P("mod", "dp", None),
            P("mod", "dp", None),
            P("mod", "dp", None),
            P("mod", None, "dp"),
            P("mod", "dp"),
            P("dp"),
            P("dp", "mod"),
            P(None, "dp", "mod"),
            P("mod", "dp"),
            P("dp", "mod"),
            P("mod", "dp"),
        ),
        check_vma=False,
    )
```

```python
import functools

import jax
import jax.numpy as jnp
from jax import lax
from jax.experimental import pallas as pl
from jax.experimental.pallas import tpu as pltpu
from jax.sharding import PartitionSpec as P

HEADS = 12
HEAD_DIM = 64
LOGIT_SCALE = 50.0
F32 = jnp.float32
BF16 = jnp.bfloat16
PAIR = 2 * HEAD_DIM
LAST = (((1,), (1,)), ((), ()))
FIRST = (((0,), (0,)), ((), ()))
VMEM = pl.BlockSpec(memory_space=pltpu.VMEM)
SMEM = pl.BlockSpec(memory_space=pltpu.SMEM)
ANY = pl.BlockSpec(memory_space=pl.ANY)


def dot(left, right):
    return jnp.dot(left, right, preferred_element_type=F32)


def dot_last(left, right):
    return lax.dot_general(left, right, LAST, preferred_element_type=F32)


def dot_first(left, right):
    return lax.dot_general(left, right, FIRST, preferred_element_type=F32)


def norm_rows(values):
    centre = values - jnp.mean(values, axis=-1, keepdims=True)
    inverse = lax.rsqrt(jnp.mean(centre * centre, axis=-1, keepdims=True) + 1e-06)
    return centre * inverse, inverse


def norm_back(grad_out, unit, inverse, gain):
    weighted = grad_out * gain
    return inverse * (
        weighted
        - jnp.mean(weighted, axis=-1, keepdims=True)
        - unit * jnp.mean(weighted * unit, axis=-1, keepdims=True)
    )


def column_sum(values):
    return jnp.sum(values, axis=0, keepdims=True)


def gelu_pair(values):
    root = 0.7978845608028654
    square = values * values
    tanh = jnp.tanh(values * (root + (root * 0.044715) * square))
    half = 0.5 + 0.5 * tanh
    slope = half + (0.5 * values) * (1.0 - tanh * tanh) * (root + (3.0 * root * 0.044715) * square)
    return values * half, slope


def stacked(pair, low):
    zero = jnp.zeros_like(pair)
    return jnp.concatenate([jnp.where(low, pair, zero), jnp.where(low, zero, pair)], axis=0)


def side_by_side(values):
    rows = values.shape[0] // 2
    return jnp.concatenate([values[:rows], values[rows:]], axis=1)


def lanes(first, index):
    return pl.ds(pl.multiple_of(first + index * PAIR, PAIR), PAIR)


def attend(q_ref, k_ref, v_ref, starts, dist_ref, probs_ref, mixed_ref):
    patches = dist_ref.shape[0]
    low = lax.broadcasted_iota(jnp.int32, (patches, PAIR), 1) < HEAD_DIM
    scale = jnp.asarray(HEAD_DIM**-0.5, BF16)

    def one(index, carry):
        queries = stacked(q_ref[:, lanes(starts[0], index)] * scale, low)
        keys = k_ref[:, lanes(starts[1], index)]
        values = stacked(v_ref[:, lanes(starts[2], index)], low)
        scores = dot_last(queries, keys)
        distance = dist_ref[...]
        halves = []
        for side in range(2):
            power = jnp.full((1, patches), 2 * index + side + 1, jnp.int32).astype(F32) * (-8.0 / HEADS)
            part = scores[side * patches : (side + 1) * patches] - jnp.exp2(power) * distance
            part = jnp.exp(part - jnp.max(part, axis=-1, keepdims=True))
            part = part * (1.0 / jnp.sum(part, axis=-1, keepdims=True))
            halves.append(part.astype(BF16))
        probs = jnp.concatenate(halves, axis=1)
        probs_ref[index] = probs
        mixed_ref[:, lanes(0, index)] = dot(probs, values).astype(BF16)
        return carry

    lax.fori_loop(0, HEADS // 2, one, 0, unroll=True)


def attend_back(q_ref, k_ref, v_ref, starts, probs_ref, grad_ref, out_refs, out_starts):
    patches = q_ref.shape[0]
    low = lax.broadcasted_iota(jnp.int32, (patches, PAIR), 1) < HEAD_DIM
    scale = jnp.asarray(HEAD_DIM**-0.5, BF16)

    def one(index, carry):
        queries = stacked(q_ref[:, lanes(starts[0], index)] * scale, low)
        keys = stacked(k_ref[:, lanes(starts[1], index)] * scale, low)
        values = v_ref[:, lanes(starts[2], index)]
        grads = stacked(grad_ref[:, lanes(0, index)], low)
        both = probs_ref[index]
        probs = jnp.concatenate([both[:, :patches], both[:, patches:]], axis=0)
        grad_probs = dot_last(grads, values)
        wide = probs.astype(F32)
        inner = jnp.sum(grad_probs * wide, axis=-1, keepdims=True)
        grad_scores = (wide * (grad_probs - inner)).astype(BF16)
        out_refs[0][:, lanes(out_starts[0], index)] = dot(side_by_side(grad_scores), keys).astype(BF16)
        out_refs[1][:, lanes(out_starts[1], index)] = dot_first(grad_scores, queries).astype(BF16)
        out_refs[2][:, lanes(out_starts[2], index)] = dot_first(probs, grads).astype(BF16)
        return carry

    lax.fori_loop(0, HEADS // 2, one, 0, unroll=True)


def begin(copies):
    for copy in copies:
        copy.start()


def finish(copies):
    for copy in copies:
        copy.wait()


def limits():
    return pltpu.CompilerParams(vmem_limit_bytes=60 * 1024 * 1024)


def shape(dims, dtype):
    return jax.ShapeDtypeStruct(dims, dtype)


def cost(macs, size):
    return pl.CostEstimate(flops=2 * macs, bytes_accessed=size, transcendentals=0)


def encode_back_kernel(
    cotangent_ref, part_ref, pool_ref, gain_ref, tokens_ref, resid_ref, slope_ref, rows_ref, probs_ref,
    project_hbm, mixer_hbm, expand_hbm, reduce_hbm,
    patch_ref, branch_ref, gexp_ref, gattn_ref, grows_ref, gains_ref,
    project_ref, mixer_ref, expand_ref, reduce_ref, gmix_ref, sems,
):
    copies = [
        pltpu.make_async_copy(source, target, sems.at[i])
        for i, (source, target) in enumerate(
            (
                (reduce_hbm, reduce_ref),
                (expand_hbm, expand_ref),
                (mixer_hbm, mixer_ref),
                (project_hbm, project_ref),
            )
        )
    ]
    begin(copies)
    patches, width = tokens_ref.shape
    grad = cotangent_ref[...].astype(F32) + pool_ref[...] * (1.0 / patches) + part_ref[...]
    patch_ref[...] = grad
    branch_ref[...] = grad.astype(BF16)
    copies[0].wait()
    for part in range(expand_ref.shape[1] // width):
        cut = slice(part * width, (part + 1) * width)
        upstream = dot_last(branch_ref[...], reduce_ref[cut, :])
        gexp_ref[:, cut] = (upstream * slope_ref[:, cut].astype(F32)).astype(BF16)
    copies[1].wait()
    grad_normed = dot_last(gexp_ref[...], expand_ref[...])
    unit, inverse = norm_rows(resid_ref[...])
    gains_ref[1:2, :] = column_sum(grad_normed * unit)
    grad = patch_ref[...] + norm_back(grad_normed, unit, inverse, gain_ref[1:2, :])
    patch_ref[...] = grad
    gattn_ref[...] = grad.astype(BF16)
    copies[2].wait()
    gmix_ref[...] = dot_last(gattn_ref[...], mixer_ref[...]).astype(BF16)
    starts = (0, width, 2 * width)
    attend_back(rows_ref, rows_ref, rows_ref, starts, probs_ref, gmix_ref, (grows_ref,) * 3, starts)
    copies[3].wait()
    grad_normed = dot_last(grows_ref[...], project_ref[...])
    unit, inverse = norm_rows(tokens_ref[...].astype(F32))
    gains_ref[0:1, :] = column_sum(grad_normed * unit)
    patch_ref[...] = patch_ref[...] + norm_back(grad_normed, unit, inverse, gain_ref[0:1, :])


def encode_back(cotangent, part, pool, gains, tokens, resid, slope, rows, probs, project, mixer, expand, reduce):
    patches, width = tokens.shape
    wide = expand.shape[1]
    weights = (project, mixer, expand, reduce)
    return pl.pallas_call(
        encode_back_kernel,
        out_shape=(
            shape((patches, width), F32),
            shape((patches, width), BF16),
            shape((patches, wide), BF16),
            shape((patches, width), BF16),
            shape((patches, 3 * width), BF16),
            shape((2, width), F32),
        ),
        in_specs=[VMEM] * 9 + [ANY] * 4,
        out_specs=(VMEM,) * 6,
        scratch_shapes=[pltpu.VMEM(w.shape, BF16) for w in weights]
        + [pltpu.VMEM((patches, width), BF16), pltpu.SemaphoreType.DMA((4,))],
        compiler_params=limits(),
        cost_estimate=cost(patches * sum(w.size for w in weights), 24 * 2**20),
        name="encode_back",
    )(cotangent, part, pool, gains, tokens, resid, slope, rows, probs, *weights)


def ring_bits(index, count):
    return [lax.rem(index // (1 << bit), 2) for bit in range(count)]


class Outputs:
    def __init__(self, sems):
        self.sems, self.used, self.open = sems, 0, {}

    def emit(self, key, source, target):
        copy = pltpu.make_async_copy(source, target, self.sems.at[self.used])
        self.used += 1
        copy.start()
        self.open.setdefault(key, []).append(copy)

    def ready(self, *keys):
        for key in keys:
            for copy in self.open.pop(key, []):
                copy.wait()

    def finish(self):
        self.ready(*list(self.open))


def remote(source, target, send_sem, recv_sem, device):
    return pltpu.make_async_remote_copy(
        src_ref=source,
        dst_ref=target,
        send_sem=send_sem,
        recv_sem=recv_sem,
        device_id=device,
        device_id_type=pl.DeviceIdType.MESH,
    )


class Weights:
    def __init__(self, refs, sources, me, mod, sems):
        self.refs, self.sources, self.sems, self.mod = refs, sources, sems, mod
        low = ring_bits(me, 3)
        self.flip = [1 - 2 * bit for bit in low]
        self.partner = [{"dp": me + flip * (1 << bit)} for bit, flip in enumerate(self.flip)]
        self.eighth = lax.rem(me, 8)
        self.copies = {}

    def view(self, weight, eighth, own=False):
        query, mixer = self.refs
        width = mixer.shape[0]
        half = width // 2
        side = self.mod if own else 1 - self.mod

        def rows(first, size):
            return pl.ds(pl.multiple_of(first + eighth * size, 16), size)

        if weight < 3:
            return query.at[weight, rows(0, width // 8), pl.ds(pl.multiple_of(side * half, 128), half)]
        return mixer.at[rows(side * half, half // 8)]

    def send(self, weight, place, eighth, device, own=False):
        send_sems, recv_sems = self.sems
        view = self.view(weight, eighth, own)
        source = view
        if own:
            first, size = self.sources[weight], view.shape[0]
            source = first.at[pl.ds(pl.multiple_of(eighth * size, 16), size)]
        copy = remote(source, view, send_sems.at[weight, place], recv_sems.at[weight, place], device)
        copy.start()
        self.copies[weight, place] = copy

    def eighths(self, weight):
        first, second = (2, 1) if weight % 2 else (1, 2)
        at_first = self.eighth + self.flip[first] * (1 << first)
        at_second = self.eighth + self.flip[second] * (1 << second)
        both = at_first + self.flip[second] * (1 << second)
        return first, second, (self.eighth, at_first, at_second, both)

    def advance(self, weight, event):
        first, second, pieces = self.eighths(weight)
        if event == 0:
            self.send(weight, 0, pieces[0], {"mod": 1 - self.mod}, own=True)
        elif event == 1:
            self.copies[weight, 0].wait_recv()
            self.send(weight, 1, pieces[0], self.partner[first])
            self.send(weight, 2, pieces[0], self.partner[second])
            self.send(weight, 4, pieces[0], self.partner[0])
        elif event == 2:
            self.copies[weight, 1].wait_recv()
            self.send(weight, 3, pieces[1], self.partner[second])
            self.send(weight, 5, pieces[1], self.partner[0])
        elif event == 3:
            self.copies[weight, 2].wait_recv()
            self.send(weight, 6, pieces[2], self.partner[0])
            self.copies[weight, 3].wait_recv()
            self.send(weight, 7, pieces[3], self.partner[0])
        else:
            for place in range(4, 8):
                self.copies[weight, place].wait_recv()

    def finish(self):
        for copy in self.copies.values():
            copy.wait_send()


class Gather:
    def __init__(self, ref, me, mod, bits, sems):
        self.ref, self.sems, self.copies, self.done = ref, sems, [], False
        self.me, self.mod, self.flip = me, mod, [1 - 2 * bit for bit in ring_bits(me, bits)]

    def advance(self):
        stage = len(self.copies)
        if self.done:
            return
        if stage:
            self.copies[-1].wait_recv()
        if stage > len(self.flip):
            self.done = True
            return
        if stage == 0:
            view, device = self.ref.at[self.me, self.mod], {"mod": 1 - self.mod}
        else:
            size = 1 << (stage - 1)
            view = self.ref.at[pl.ds(self.me // size * size, size)]
            device = {"dp": self.me + self.flip[stage - 1] * size}
        copy = remote(view, view, self.sems[0].at[stage], self.sems[1].at[stage], device)
        copy.start()
        self.copies.append(copy)

    def finish(self):
        for copy in self.copies:
            copy.wait_send()


def contrast_into(gathered_ref, pooled_ref, grad_ref, loss_ref, pool_ref, me, mod, items):
    count = gathered_ref.shape[0]
    width = pooled_ref.shape[2]
    total = items * count
    for half in range(2):
        for n in range(items):
            for part in range(width // 128):
                pooled_ref[half, n * count : (n + 1) * count, part * 128 : (part + 1) * 128] = gathered_ref[
                    :, half, n * (width // 128) + part, :
                ]
    flags = [gathered_ref[:, 0, items * (width // 128) + n, :][:, 0:1] for n in range(items)]
    present = jnp.concatenate(flags, axis=0)
    same = lax.broadcasted_iota(jnp.int32, (total, total), 0) == lax.broadcasted_iota(jnp.int32, (total, total), 1)
    same = jnp.where(same, 1.0, 0.0)
    present_row = column_sum(present * same)
    scale = LOGIT_SCALE / width
    units, inverses = [], []
    for half in range(2):
        pooled = pooled_ref[half]
        inverses.append(lax.rsqrt(jnp.mean(pooled * pooled, axis=-1, keepdims=True) + 1e-06))
        units.append(pooled * inverses[-1])
    exact = lax.Precision.HIGHEST
    logits = lax.dot_general(units[0], units[1], LAST, precision=exact, preferred_element_type=F32) * scale
    by_row = logits - 10000.0 * (1.0 - present_row)
    by_column = logits - 10000.0 * (1.0 - present)
    row_top = jnp.max(by_row, axis=1, keepdims=True)
    column_top = jnp.max(by_column, axis=0, keepdims=True)
    by_row = jnp.exp(by_row - row_top)
    by_column = jnp.exp(by_column - column_top)
    row_sum = jnp.sum(by_row, axis=1, keepdims=True)
    column_total = column_sum(by_column)
    row_part = present * (row_top + jnp.log(row_sum) - 2.0 * jnp.sum(logits * same, axis=1, keepdims=True))
    column_part = present_row * (column_top + jnp.log(column_total))
    loss = (jnp.sum(row_part) + jnp.sum(column_part)) / (2.0 * total)
    loss_ref[0, 0] = loss
    grad_logits = (
        present * by_row / row_sum + present_row * by_column / column_total - 2.0 * same * present
    ) * (scale / (2.0 * total))

    def own(half, grad_unit):
        unit = units[half]
        grad_ref[...] = inverses[half] * (grad_unit - unit * jnp.mean(grad_unit * unit, axis=-1, keepdims=True))

    @pl.when(mod == 0)
    def _():
        own(0, jnp.dot(grad_logits, units[1], precision=exact, preferred_element_type=F32))

    @pl.when(mod == 1)
    def _():
        own(1, lax.dot_general(grad_logits, units[0], FIRST, precision=exact, preferred_element_type=F32))

    for n in range(items):
        pool_ref[n : n + 1, :] = grad_ref[pl.ds(n * count + me, 1), :]


def forward_kernel(
    tokens_ref, grid_ref, gain_ref, norms_ref, cross_gain_hbm, present_ref, cotangent_ref,
    project_hbm, mixer_hbm, expand_hbm, reduce_hbm,
    query_hbm, keyval_hbm, cmixer_hbm, cexpand_hbm, creduce_hbm,
    encoded_out, normed_out, rows_out, probs_out, mixed_out, resid_out, normed_two_out, hidden_out, slope_out,
    part_out, query_in_out, keyval_in_out, cnormed_out, cmixed_out, chidden_out, branch_out, cgexp_out, cgattn_out,
    gq_out, gkv_out, cresid_out, joining_out, early_out,
    gains_ref, loss_ref, pool_ref,
    project_ref, mixer_ref, expand_ref, reduce_ref,
    cquery_ref, cmixer_ref, cexpand_ref, creduce_ref,
    encoded_ref, partner_ref, normed_ref, rows_ref, probs_ref, mixed_ref, resid_ref, normed_two_ref, hidden_ref,
    slope_keep_ref,
    cprobs_ref, cresid_ref, query_in_ref, keyval_in_ref, cnormed_ref,
    branch_ref, cgattn_ref, gmix_ref, part_ref, half_ref, joining_ref,
    gathered_ref, pooled_ref, grad_ref, dist_ref, cross_gain_ref,
    early_ref, early_got_ref, early_sems,
    load_sems, out_sems, weight_sends, weight_recvs, gather_sends, gather_recvs, swap_sends, swap_recvs,
):
    items, patches, width = tokens_ref.shape
    half, wide = width // 2, 2 * width
    count = gathered_ref.shape[0]
    bits = count.bit_length() - 1
    me, mod = lax.axis_index("dp"), lax.axis_index("mod")
    is_radar = mod == 1
    across = {"mod": 1 - mod}
    own_columns = pl.ds(pl.multiple_of(mod * half, 128), half)
    loads = [
        pltpu.make_async_copy(source, target, load_sems.at[i])
        for i, (source, target) in enumerate(
            (
                (project_hbm, project_ref),
                (query_hbm, cquery_ref.at[0, :, own_columns]),
                (keyval_hbm, cquery_ref.at[1:3, :, own_columns]),
                (cmixer_hbm, cmixer_ref.at[own_columns]),
                (mixer_hbm, mixer_ref),
                (expand_hbm, expand_ref),
                (reduce_hbm, reduce_ref),
                (cexpand_hbm, cexpand_ref),
                (creduce_hbm, creduce_ref),
            )
        )
    ]
    begin(loads[0:4])
    sources = (query_hbm, keyval_hbm.at[0], keyval_hbm.at[1], cmixer_hbm)
    weights = Weights((cquery_ref, cmixer_ref), sources, me, mod, (weight_sends, weight_recvs))
    gather = Gather(gathered_ref, me, mod, bits, (gather_sends, gather_recvs))
    outputs = Outputs(out_sems)
    swaps = {}

    def swap(key, source, target):
        place = len(swaps)
        swaps[key] = remote(source, target, swap_sends.at[place], swap_recvs.at[place], across)
        swaps[key].start()

    barrier = pltpu.get_barrier_semaphore()
    others = [across] + [{"dp": me + flip * (1 << bit)} for bit, flip in enumerate(gather.flip)]
    for device in others:
        pl.semaphore_signal(barrier, inc=1, device_id=device, device_id_type=pl.DeviceIdType.MESH)
    cross_gain_ref[...] = cross_gain_hbm[...].reshape(1, width)
    for n in range(items):
        spans = []
        for axis in range(2):
            along = jnp.broadcast_to(grid_ref[n, axis : axis + 1, :].astype(F32), (8, patches))
            spans.append(along.T[:, 0:1] - along[0:1, :])
        dist_ref[n] = jnp.sqrt(spans[0] * spans[0] + spans[1] * spans[1])
    pl.semaphore_wait(barrier, len(others))

    def pump(*events):
        for event in events:
            weights.advance(*event)

    pump((0, 0), (1, 0), (2, 0), (3, 0))

    def encode_image(n, pumps):
        def put(key, source, target):
            outputs.emit(key, source, target.at[n])

        unit, _ = norm_rows(tokens_ref[n].astype(F32))
        outputs.ready("normed", "rows")
        normed_ref[...] = (unit * gain_ref[0:1, :]).astype(BF16)
        put("normed", normed_ref, normed_out)
        if n == 0:
            finish(loads[0:4])
            begin(loads[4:])
        for part in range(3):
            cut = slice(part * width, (part + 1) * width)
            rows_ref[:, cut] = dot(normed_ref[...], project_ref[:, cut]).astype(BF16)
        put("rows", rows_ref, rows_out)
        pump(*pumps[0])
        outputs.ready("probs", "mixed")
        attend(rows_ref, rows_ref, rows_ref, (0, width, 2 * width), dist_ref.at[n], probs_ref, mixed_ref)
        put("probs", probs_ref, probs_out)
        put("mixed", mixed_ref, mixed_out)
        pump(*pumps[1])
        if n == 0:
            loads[4].wait()
        outputs.ready("resid", "normed_two")
        resid = tokens_ref[n].astype(F32) + dot(mixed_ref[...], mixer_ref[...])
        resid_ref[...] = resid
        unit, _ = norm_rows(resid)
        normed_two_ref[...] = (unit * gain_ref[1:2, :]).astype(BF16)
        put("resid", resid_ref, resid_out)
        put("normed_two", normed_two_ref, normed_two_out)
        if n == 0:
            loads[5].wait()
        outputs.ready("hidden", "slope")
        for part in range(expand_ref.shape[1] // width):
            cut = slice(part * width, (part + 1) * width)
            value, slope = gelu_pair(dot(normed_two_ref[...], expand_ref[:, cut]))
            hidden_ref[:, cut] = value.astype(BF16)
            slope_keep_ref[:, cut] = slope.astype(BF16)
        pump(*pumps[2])
        if n == 0:
            loads[6].wait()
        encoded = (resid_ref[...] + dot(hidden_ref[...], reduce_ref[...])).astype(BF16)
        encoded_ref[n] = encoded
        swap(n, encoded_ref.at[n], partner_ref.at[n])
        put("encoded", encoded_ref.at[n], encoded_out)
        put("hidden", hidden_ref, hidden_out)
        put("slope", slope_keep_ref, slope_out)
        pooled = jnp.mean(encoded.astype(F32), axis=0, keepdims=True)
        if n == 0:
            gathered_ref[me, mod] = jnp.zeros(gathered_ref.shape[2:], F32)
        for part in range(width // 128):
            place = n * (width // 128) + part
            gathered_ref[me, mod, place : place + 1, :] = pooled[:, part * 128 : (part + 1) * 128]
        place = items * (width // 128) + n
        gathered_ref[me, mod, place : place + 1, :] = jnp.full((1, 128), present_ref[n], jnp.int32).astype(F32)
        pump(*pumps[3])

    encode_image(0, ((), ((0, 1), (1, 1)), ((2, 1),), ((3, 1), (0, 2))))
    encode_image(1, (((1, 2),), ((2, 2), (3, 2), (0, 3)), ((1, 3), (2, 3)), ((3, 3),)))
    gather.advance()
    starts = (0, 0, width)
    outputs.ready("hidden", "slope")
    images = [slice(n * patches, (n + 1) * patches) for n in range(items)]
    q_refs = [project_ref.at[own, 0:width] for own in images]
    kv_refs = [project_ref.at[own, width : 3 * width] for own in images]
    gq_refs = [expand_ref.at[own, 0:width] for own in images]
    gkv_refs = [expand_ref.at[own, width : 3 * width] for own in images]
    cmixed_refs = [mixer_ref.at[own] for own in images]
    chidden_refs = [hidden_ref.at[:, n * wide : (n + 1) * wide] for n in range(items)]
    cgexp_refs = [slope_keep_ref.at[:, n * wide : (n + 1) * wide] for n in range(items)]

    def join_attend(n):
        def put(key, source, target):
            outputs.emit(key, source.at[n], target.at[n])

        swaps[n].wait_recv()
        own, other = encoded_ref[n], partner_ref[n]
        unit, _ = norm_rows(jnp.where(is_radar, own, other).astype(F32))
        query_in_ref[n] = (unit * norms_ref[1:2, :]).astype(BF16)
        unit, _ = norm_rows(jnp.where(is_radar, other, own).astype(F32))
        keyval_in_ref[n] = (unit * norms_ref[0:1, :]).astype(BF16)
        put("query_in", query_in_ref, query_in_out)
        put("keyval_in", keyval_in_ref, keyval_in_out)
        if n == 0:
            pump((0, 4), (1, 4), (2, 4), (3, 4))
            finish(loads[7:9])
        q_refs[n][...] = dot(query_in_ref[n], cquery_ref[0]).astype(BF16)
        for part in range(2):
            kv_refs[n][:, part * width : (part + 1) * width] = dot(keyval_in_ref[n], cquery_ref[1 + part]).astype(BF16)
        gather.advance()
        kv = kv_refs[n]
        attend(q_refs[n], kv, kv, starts, dist_ref.at[n], cprobs_ref.at[n], cmixed_refs[n])
        outputs.emit("cmixed", cmixed_refs[n].at[:, own_columns], cmixed_out.at[n])
        gather.advance()
        radar = jnp.where(is_radar, encoded_ref[n], partner_ref[n]).astype(F32)
        resid = radar + dot(cmixed_refs[n][...], cmixer_ref[...])
        cresid_ref[n] = resid
        unit, _ = norm_rows(resid)
        cnormed_ref[n] = (unit * cross_gain_ref[...]).astype(BF16)
        put("cresid", cresid_ref, cresid_out)
        put("cnormed", cnormed_ref, cnormed_out)
        branch_ref[n] = (present_ref[n].astype(F32) * cotangent_ref[n].astype(F32)).astype(BF16)
        put("branch", branch_ref, branch_out)

    def join_feed(n):
        for part in range(wide // width):
            cut = slice(part * width, (part + 1) * width)
            value, slope = gelu_pair(dot(cnormed_ref[n], cexpand_ref[:, cut]))
            chidden_refs[n][:, cut] = value.astype(BF16)
            upstream = dot_last(branch_ref[n], creduce_ref[cut, :])
            cgexp_refs[n][:, cut] = (upstream * slope).astype(BF16)
        half_ref[0, n] = dot_last(cgexp_refs[n][...], cexpand_ref[...]).astype(BF16)
        swap(("half", n), half_ref.at[0, n], half_ref.at[1, n])
        outputs.emit("chidden", chidden_refs[n], chidden_out.at[n])
        outputs.emit("cgexp", cgexp_refs[n], cgexp_out.at[n])
        gather.advance()

    def join_back(n):
        def put(key, source, target):
            outputs.emit(key, source.at[n], target.at[n])

        swaps["half", n].wait_recv()
        grad_normed = half_ref[0, n].astype(F32) + half_ref[1, n].astype(F32)
        unit, inverse = norm_rows(cresid_ref[n])
        sums = column_sum(grad_normed * unit)
        gains_ref[1:2, :] = sums if n == 0 else gains_ref[1:2, :] + sums
        present = present_ref[n].astype(F32)
        grad = present * cotangent_ref[n].astype(F32) + norm_back(grad_normed, unit, inverse, cross_gain_ref[...])
        part_ref[n] = grad
        cgattn_ref[n] = grad.astype(BF16)
        put("cgattn", cgattn_ref, cgattn_out)
        gmix_ref[...] = dot_last(cgattn_ref[n], cmixer_ref[...]).astype(BF16)
        gather.advance()
        kv, gq, gkv = kv_refs[n], gq_refs[n], gkv_refs[n]
        attend_back(q_refs[n], kv, kv, starts, cprobs_ref.at[n], gmix_ref, (gq, gkv, gkv), (0, 0, width))
        outputs.emit("gq", gq.at[:, own_columns], gq_out.at[n])
        outputs.emit("gkv", gkv.at[:, own_columns], gkv_out.at[n, :, 0:half])
        second = pl.ds(pl.multiple_of(width + mod * half, 128), half)
        outputs.emit("gkv", gkv.at[:, second], gkv_out.at[n, :, half:width])
        gather.advance()

        def to_own(grad_in, gain, residual):
            unit, inverse = norm_rows(encoded_ref[n].astype(F32))
            sums = column_sum(grad_in * unit)
            gains_ref[0:1, :] = sums if n == 0 else gains_ref[0:1, :] + sums
            grad_in = norm_back(grad_in, unit, inverse, gain)
            part_ref[n] = part_ref[n] + grad_in if residual else grad_in

        @pl.when(is_radar)
        def _():
            to_own(dot_last(gq_refs[n][...], cquery_ref[0]), norms_ref[1:2, :], True)

        @pl.when(mod == 0)
        def _():
            grad_in = dot_last(gkv_refs[n][:, 0:width], cquery_ref[1])
            grad_in = grad_in + dot_last(gkv_refs[n][:, width : 2 * width], cquery_ref[2])
            to_own(grad_in, norms_ref[0:1, :], False)

        put("part", part_ref, part_out)

    for n in range(items):
        join_attend(n)
        join_feed(n)
    early_copies = []
    if early_ref.shape[0] == 2:
        core = lax.rem(me, 2)
        beside = {"dp": me + 1 - 2 * core}
        block = early_ref.shape[-2]
        for chunk in range(2):
            cut = slice(chunk * width, (chunk + 1) * width)
            product = dot_first(branch_ref[0], chidden_refs[0][:, cut])
            for n in range(1, items):
                product = product + dot_first(branch_ref[n], chidden_refs[n][:, cut])
            product = product.astype(BF16)
            for index in range(1 << bits):
                place = tuple((index >> bit) & 1 for bit in range(bits)[::-1])
                early_ref[(chunk, *place)] = product[index * block : (index + 1) * block]
            copy = remote(
                early_ref.at[chunk, :, :, :, 1 - core], early_got_ref.at[chunk],
                early_sems.at[0, chunk], early_sems.at[1, chunk], beside,
            )
            copy.start()
            early_copies.append(copy)
    for n in range(items):
        join_back(n)
        if n == 0:
            for chunk, copy in enumerate(early_copies):
                copy.wait_recv()
                early_got_ref[chunk] = early_got_ref[chunk] + early_ref[chunk, :, :, :, core]
                outputs.emit("early", early_got_ref.at[chunk], early_out.at[chunk])
            for m in range(items):
                joining_ref[m] = dot(chidden_refs[m][...], creduce_ref[...]).astype(BF16)
                outputs.emit("joining", joining_ref.at[m], joining_out.at[m])
            while not gather.done:
                gather.advance()
            contrast_into(gathered_ref, pooled_ref, grad_ref, loss_ref, pool_ref, me, mod, items)
    for copy in early_copies:
        copy.wait_send()
    for copy in swaps.values():
        copy.wait_send()
    weights.finish()
    gather.finish()
    outputs.finish()


def sums_here(width, count):
    return count == 16 and width // count % 16 == 0


def forward(tokens, grid, gains, norms, cross_gain, present, cotangent, weights, cross, count):
    items, patches, width = tokens.shape
    half, wide, full = width // 2, 2 * width, 4 * width
    bits = count.bit_length() - 1
    pairs = HEADS // 2

    def out(*dims, dtype=BF16):
        return shape((items, patches, *dims), dtype)

    outs = (
        out(width), out(width), out(3 * width), shape((items, pairs, patches, 2 * patches), BF16), out(width),
        out(width, dtype=F32), out(width), out(full), out(full),
        out(width, dtype=F32), out(width), out(width), out(width), out(half), out(wide), out(width), out(wide), out(width),
        out(half), out(width), out(width, dtype=F32), out(width),
    )
    block = width // count
    early = (2,) * bits + (block, width) if sums_here(width, count) else (8, 128)
    outs = (*outs, shape(early, BF16))
    row, probs = (patches, width), (pairs, patches, 2 * patches)

    def both(*dims, dtype=BF16):
        return pltpu.VMEM((items, *dims), dtype)

    scratch = [pltpu.VMEM(w.shape, BF16) for w in weights]
    scratch += [pltpu.VMEM(d, BF16) for d in ((3, width, width), (width, width), (width, wide), (wide, width))]
    scratch += [both(*row), both(*row)]
    scratch += [pltpu.VMEM(d, BF16) for d in (row, (patches, 3 * width), probs, row)]
    scratch += [pltpu.VMEM(row, F32), pltpu.VMEM(row, BF16), pltpu.VMEM((patches, full), BF16), pltpu.VMEM((patches, full), BF16)]
    scratch += [both(*probs), both(*row, dtype=F32), both(*row), both(*row), both(*row)]
    scratch += [both(*row), both(*row), pltpu.VMEM(row, BF16), both(*row, dtype=F32)]
    scratch += [pltpu.VMEM((2, items, *row), BF16), both(*row)]
    scratch += [
        pltpu.VMEM((count, 2, 16, 128), F32),
        pltpu.VMEM((2, items * count, width), F32),
        pltpu.VMEM((items * count, width), F32),
        pltpu.VMEM((items, patches, patches), F32),
        pltpu.VMEM((1, width), F32),
    ]
    dma = pltpu.SemaphoreType.DMA
    scratch += [pltpu.VMEM((2, *early), BF16) if early[0] == 2 else pltpu.VMEM(early, BF16), pltpu.VMEM(early, BF16), dma((2, 2))]
    scratch += [dma((9,)), dma((2 * 24,)), dma((4, 8)), dma((4, 8)), dma((bits + 1,)), dma((bits + 1,)), dma((5,)), dma((5,))]
    return pl.pallas_call(
        forward_kernel,
        out_shape=outs + (shape((2, width), F32), shape((1, 1), F32), shape((items, width), F32)),
        in_specs=[VMEM, VMEM, VMEM, VMEM, VMEM, SMEM, VMEM] + [ANY] * 9,
        out_specs=(ANY,) * len(outs) + (VMEM, SMEM, VMEM),
        scratch_shapes=scratch,
        compiler_params=pltpu.CompilerParams(
            collective_id=1, has_side_effects=True, vmem_limit_bytes=63 * 1024 * 1024
        ),
        cost_estimate=cost(items * patches * 40 * width * width, 60 * 2**20),
        name="forward",
    )(tokens, grid, gains, norms, cross_gain, present, cotangent, *weights, *cross)


DEPTH = 2


class Halvings:
    def __init__(self, orders, held, got, sems, me, make, result):
        self.orders, self.held, self.got, self.sems = orders, held, got, sems
        self.make_chunk, self.result = make, result
        self.bits = len(orders[0])
        self.every = list(range(self.bits))[::-1]
        self.mine = ring_bits(me, self.bits)
        self.partners = [{"dp": me + (1 - 2 * bit) * (1 << place)} for place, bit in enumerate(self.mine)]
        self.copies, self.waited, self.done = {}, set(), set()
        self.total = len(orders)

    def held_at(self, chunk, stage):
        return self.held[stage].at[self.place[chunk] % self.held[stage].shape[0]]

    def got_at(self, chunk, stage):
        return self.got[stage].at[self.place[chunk] % self.got[stage].shape[0]]

    def before(self, chunk, stage):
        place = self.place[chunk] - self.held[stage].shape[0]
        return self.order[place] if place >= 0 else None

    def part(self, chunk, stage, kept):
        bit = self.orders[chunk][stage]
        left = [other for other in self.every if other not in self.orders[chunk][:stage]]
        side = self.mine[bit] if kept else 1 - self.mine[bit]
        return self.held_at(chunk, stage).at[tuple(side if other == bit else slice(None) for other in left)]

    def send(self, chunk, stage):
        copy = remote(
            self.part(chunk, stage, False), self.got_at(chunk, stage),
            self.sems[0].at[stage, chunk], self.sems[1].at[stage, chunk],
            self.partners[self.orders[chunk][stage]],
        )
        copy.start()
        self.copies[chunk, stage] = copy

    def free(self, chunk, stage):
        last = self.before(chunk, stage)
        if (last, stage) in self.copies and (last, stage) not in self.waited:
            self.copies[last, stage].wait_send()
            self.waited.add((last, stage))

    def make(self, chunk):
        if not 0 <= chunk < self.total or (chunk, "made") in self.done:
            return
        self.done.add((chunk, "made"))
        last = self.before(chunk, 0)
        assert last is None or (last, 0) in self.done
        self.free(chunk, 0)
        self.make_chunk(chunk, self.held_at(chunk, 0))
        self.send(chunk, 0)

    def take(self, chunk, stage):
        if not 0 <= chunk < self.total or (chunk, stage) in self.done:
            return
        self.done.add((chunk, stage))
        self.copies[chunk, stage].wait_recv()
        kept, arrived = self.part(chunk, stage, True), self.got_at(chunk, stage)
        if stage == self.bits - 1:
            self.result(chunk, kept[...].astype(F32) + arrived[...].astype(F32))
            return
        last = self.before(chunk, stage + 1)
        assert last is None or (last, stage + 1) in self.done
        self.free(chunk, stage + 1)
        target = self.held_at(chunk, stage + 1)
        target[...] = kept[...] + arrived[...]
        if stage:
            self.send(chunk, stage + 1)

    def schedule(self, first, aside, enter):
        self.first, self.aside, self.at = first, aside, 0
        self.needed = [[c] for c in first[DEPTH:]] + [[]] * (DEPTH + 1)
        for chunk, at in aside.items():
            self.needed[at] = self.needed[at] + [chunk]
        order = first[:DEPTH] + [chunk for step in self.needed for chunk in step]
        self.order, self.following = order, dict(zip(order, order[1:]))
        self.place = {chunk: place for place, chunk in enumerate(order)}
        enter()
        for chunk in first[:DEPTH]:
            self.done.update({(chunk, "made"), (chunk, 0)})
            self.send(chunk, 1)
        for chunk in self.needed[0]:
            self.make(chunk)

    def prepare(self):
        if self.at + 1 < len(self.needed):
            for chunk in self.needed[self.at + 1]:
                self.make(chunk)

    def step(self):
        first, at = self.first, self.at
        self.at += 1
        for chunk in self.needed[at] if at < len(self.needed) else []:
            self.take(chunk, 0)
        if at < len(first):
            self.take(first[at], 1)
        if at + DEPTH < len(first):
            self.send(first[at + DEPTH], 1)
        for chunk, start in self.aside.items():
            if at == start:
                self.send(chunk, 1)
            for stage, delay in ((1, 2), (2, 4), (3, 5)):
                if at == start + delay:
                    self.take(chunk, stage)
        for stage in range(2, self.bits):
            if 0 <= at + 1 - stage < len(first):
                self.take(first[at + 1 - stage], stage)

    def unfinished(self):
        return any((chunk, self.bits - 1) not in self.done for chunk in range(self.total))

    def finish(self):
        for key, copy in self.copies.items():
            if key not in self.waited:
                copy.wait_send()


def backward_kernel(
    plan, results, sizes,
    pool_ref, gain_ref, cross_gains_ref, part_hbm, cotangent_hbm, tokens_hbm, resid_hbm, slope_hbm, rows_hbm, probs_hbm,
    project_hbm, mixer_hbm, expand_hbm, reduce_hbm, *rest,
):
    n_in, n_out, bits, aside = sizes
    present_ref, cresid_hbm, joining_hbm, early_hbm = rest[:4]
    rest = rest[4:]
    operands, rest = rest[:n_in], rest[n_in:]
    joined_out, patch_out, outs, vector_out = rest[0], rest[1], rest[2 : 2 + n_out], rest[2 + n_out]
    scratch = rest[3 + n_out :]
    (
        project_ref, mixer_ref, expand_ref, reduce_ref,
        patch_ref, cotangent_ref, tokens_ref, resid_ref, slope_ref, rows_ref, probs_ref,
        branch_ref, gexp_ref, gattn_ref, grows_ref, gmix_ref, left_ref, right_ref, joining_ref,
    ) = scratch[:19]
    scratch = scratch[19:]
    held, got = scratch[:bits], scratch[bits : 2 * bits]
    vector_held, vector_got = scratch[2 * bits : 3 * bits], scratch[3 * bits : 4 * bits]
    load_sems, left_sems, right_sems, out_sems, send_sems, recv_sems, vector_sends, vector_recvs, swap_sems = scratch[4 * bits :]
    items, patches = pool_ref.shape[0], resid_ref.shape[0] // pool_ref.shape[0]
    width = patch_ref.shape[1]
    me = lax.axis_index("dp")
    resident = {"branch": branch_ref, "gexp": gexp_ref, "gattn": gattn_ref, "grows": grows_ref}
    fetched, loaded, slots = {}, {}, [0, 0]

    def fetch(kind, key, source, target_of, sems):
        if loaded.get(kind, [None])[-1] == key:
            return fetched[key]
        buffers = target_of.shape[0]
        slot = slots[kind] % buffers
        slots[kind] += 1
        copy = pltpu.make_async_copy(source, target_of.at[slot, :, 0 : source.shape[1]], sems.at[slots[kind] - 1])
        copy.start()
        fetched[key] = [slot, copy]
        loaded.setdefault(kind, []).append(key)
        return fetched[key]

    def fetch_chunk(chunk):
        if chunk >= len(plan):
            return
        for left, right, start, size, _ in plan[chunk]:
            if not isinstance(left, str):
                fetch(0, ("left", left), operands[left], left_ref, left_sems)
            if not isinstance(right, str):
                fetch(1, ("right", right, start), operands[right].at[:, start : start + size], right_ref, right_sems)

    def arrived(key):
        entry = fetched[key]
        if entry[1] is not None:
            entry[1].wait()
            entry[1] = None
        return entry[0]

    def make_chunk(chunk, target):
        fetch_chunk(sums.following.get(chunk, len(plan)))
        block = target.shape[-2]
        for left, right, start, size, place in plan[chunk]:
            one = resident[left][...] if isinstance(left, str) else left_ref[arrived(("left", left))]
            if isinstance(right, str):
                other = resident[right][:, start : start + size]
            else:
                other = right_ref[arrived(("right", right, start)), :, 0:size]
            product = dot_first(one, other).astype(BF16)
            for index in range(1 << bits):
                where = tuple((index >> bit) & 1 for bit in range(bits)[::-1])
                target[(*where, slice(None), slice(place, place + size))] = product[index * block : (index + 1) * block]

    def result(chunk, value):
        for out, column, first, size in results[chunk]:
            if len(outs[out].shape) == 3:
                outs[out][column] = value[:, first : first + size]
            else:
                outs[out][:, column : column + size] = value[:, first : first + size]

    early = pltpu.make_async_copy(early_hbm, held[1].at[0:DEPTH], load_sems.at[13])
    early.start()
    fetch_chunk(DEPTH)
    loads = [
        pltpu.make_async_copy(source, target, load_sems.at[i])
        for i, (source, target) in enumerate(
            (
                (part_hbm, patch_ref), (cotangent_hbm, cotangent_ref), (reduce_hbm, reduce_ref), (slope_hbm, slope_ref),
                (expand_hbm, expand_ref), (resid_hbm, resid_ref), (mixer_hbm, mixer_ref), (rows_hbm, rows_ref),
                (probs_hbm, probs_ref), (project_hbm, project_ref), (tokens_hbm, tokens_ref),
            )
        )
    ]
    orders = [(0, 2, 3, 1) if chunk in aside else (0, 1, 2, 3) for chunk in range(len(plan))]
    sums = Halvings(orders, held, got, (send_sems, recv_sems), me, make_chunk, result)
    barrier = pltpu.get_barrier_semaphore()
    across = {"mod": 1 - lax.axis_index("mod")}
    for device in [*sums.partners, across]:
        pl.semaphore_signal(barrier, inc=1, device_id=device, device_id_type=pl.DeviceIdType.MESH)
    early.wait()
    sums.schedule(
        [chunk for chunk in range(len(plan)) if chunk not in aside], aside,
        lambda: pl.semaphore_wait(barrier, bits + 1),
    )
    begin(loads[0:4])
    joining_swap = remote(joining_hbm, joining_ref, swap_sems.at[0], swap_sems.at[1], across)
    joining_swap.start()
    sums.prepare()

    images = [slice(n * patches, (n + 1) * patches) for n in range(items)]
    finish(loads[0:4])
    begin(loads[4:])
    for n, own in enumerate(images):
        grad = cotangent_ref[own].astype(F32) + pool_ref[n : n + 1, :] * (1.0 / patches) + patch_ref[own]
        patch_ref[own] = grad
        branch_ref[own] = grad.astype(BF16)
    for part in range(expand_ref.shape[1] // width):
        cut = slice(part * width, (part + 1) * width)
        upstream = dot_last(branch_ref[...], reduce_ref[cut, :])
        gexp_ref[:, cut] = (upstream * slope_ref[:, cut].astype(F32)).astype(BF16)
    sums.step()
    sums.prepare()
    finish(loads[4:6])
    gains = []
    for own in images:
        grad_normed = dot_last(gexp_ref[own], expand_ref[...])
        unit, inverse = norm_rows(resid_ref[own])
        gains.append(column_sum(grad_normed * unit))
        grad = patch_ref[own] + norm_back(grad_normed, unit, inverse, gain_ref[1:2, :])
        patch_ref[own] = grad
        gattn_ref[own] = grad.astype(BF16)
    second_gain = sum(gains)
    late = [
        pltpu.make_async_copy(cresid_hbm, resid_ref, load_sems.at[11]),
        pltpu.make_async_copy(joining_hbm, cotangent_ref, load_sems.at[12]),
    ]
    begin(late)
    sums.step()
    sums.prepare()
    finish(loads[6:9])
    gmix_ref[...] = dot_last(gattn_ref[...], mixer_ref[...]).astype(BF16)
    starts = (0, width, 2 * width)
    for n, own in enumerate(images):
        rows, grows = rows_ref.at[own], grows_ref.at[own]
        attend_back(rows, rows, rows, starts, probs_ref.at[n], gmix_ref.at[own], (grows,) * 3, starts)
        sums.step()
        sums.prepare()
    finish(loads[9:11])
    gains = []
    for n, own in enumerate(images):
        grad_normed = dot_last(grows_ref[own], project_ref[...])
        unit, inverse = norm_rows(tokens_ref[own].astype(F32))
        gains.append(column_sum(grad_normed * unit))
        patch_ref[own] = patch_ref[own] + norm_back(grad_normed, unit, inverse, gain_ref[0:1, :])
    patch_copy = pltpu.make_async_copy(patch_ref, patch_out, out_sems.at[0])
    patch_copy.start()
    finish(late)
    joining_swap.wait_recv()
    for n, own in enumerate(images):
        branch = cotangent_ref[own].astype(F32) + joining_ref[own].astype(F32)
        cotangent_ref[own] = (present_ref[n].astype(F32) * (resid_ref[own] + branch)).astype(BF16)
    joined_copy = pltpu.make_async_copy(cotangent_ref, joined_out, out_sems.at[1])
    joined_copy.start()
    rows = jnp.concatenate([sum(gains), second_gain, cross_gains_ref[...], jnp.zeros((4, width), F32)], axis=0)
    block = width >> bits
    for index in range(1 << bits):
        where = tuple((index >> bit) & 1 for bit in range(bits)[::-1])
        piece = rows[:, index * block : (index + 1) * block]
        vector_held[0][where] = jnp.concatenate([piece, jnp.zeros((8, 128 - block), F32)], axis=1)
    vector_copies = []

    def vector_step():
        stage = len(vector_copies)
        if stage > bits:
            return
        if stage:
            bit = stage - 1
            vector_copies[-1].wait_recv()
            left = list(range(bit, bits))[::-1]
            kept = vector_held[bit].at[tuple(sums.mine[bit] if other == bit else slice(None) for other in left)]
            value = kept[...] + vector_got[bit][...]
            if stage == bits:
                vector_out[...] = value
                vector_copies.append(None)
                return
            vector_held[stage][...] = value
        left = list(range(stage, bits))[::-1]
        view = vector_held[stage].at[tuple(1 - sums.mine[stage] if other == stage else slice(None) for other in left)]
        copy = remote(view, vector_got[stage], vector_sends.at[stage], vector_recvs.at[stage], sums.partners[stage])
        copy.start()
        vector_copies.append(copy)

    while sums.unfinished():
        vector_step()
        sums.step()
        sums.prepare()
    while len(vector_copies) <= bits:
        vector_step()
    for copy in vector_copies[:bits]:
        copy.wait_send()
    sums.finish()
    joining_swap.wait_send()
    patch_copy.wait()
    joined_copy.wait()


def backward(pool, gains, cross_gains, activations, weights, joining, operands, plan, results, outs, aside, count):
    part, cotangent, tokens, resid, slope, rows, probs = activations
    total_rows, width = tokens.shape
    bits = count.bit_length() - 1
    block, chunks = width // count, len(plan)
    two = (2,) * bits
    full, pairs = slope.shape[1], probs.shape[1:]
    held, got = (3, 6, 5, 5), (6, 8, 6, 6)
    flat = (total_rows, width)
    lefts = [key for chunk in plan for key in chunk]
    dma = pltpu.SemaphoreType.DMA
    scratch = [pltpu.VMEM(w.shape, BF16) for w in weights]
    scratch += [pltpu.VMEM(flat, F32), pltpu.VMEM(flat, BF16), pltpu.VMEM(flat, BF16), pltpu.VMEM(flat, F32)]
    scratch += [pltpu.VMEM((total_rows, full), BF16), pltpu.VMEM((total_rows, 3 * width), BF16), pltpu.VMEM(probs.shape, BF16)]
    scratch += [pltpu.VMEM(flat, BF16), pltpu.VMEM((total_rows, full), BF16), pltpu.VMEM(flat, BF16)]
    scratch += [pltpu.VMEM((total_rows, 3 * width), BF16), pltpu.VMEM(flat, BF16)]
    scratch += [pltpu.VMEM((3, *flat), BF16), pltpu.VMEM((3, *flat), BF16), pltpu.VMEM(flat, BF16)]
    scratch += [pltpu.VMEM((held[stage], *two[stage:], block, width), BF16) for stage in range(bits)]
    scratch += [pltpu.VMEM((got[stage], *two[stage + 1 :], block, width), BF16) for stage in range(bits)]
    scratch += [pltpu.VMEM((*two[stage:], 8, 128), F32) for stage in range(bits)]
    scratch += [pltpu.VMEM((*two[stage + 1 :], 8, 128), F32) for stage in range(bits)]
    scratch += [dma((14,)), dma((len(lefts),)), dma((len(lefts),)), dma((2,)), dma((bits, chunks)), dma((bits, chunks))]
    scratch += [dma((bits,)), dma((bits,)), dma((2,))]
    return pl.pallas_call(
        functools.partial(backward_kernel, plan, results, (len(operands), len(outs), bits, aside)),
        out_shape=(shape(flat, BF16), shape(flat, F32), *(shape(dims, F32) for dims in outs), shape((8, 128), F32)),
        in_specs=[VMEM] * 3 + [ANY] * (7 + 4) + [SMEM] + [ANY] * (3 + len(operands)),
        out_specs=(ANY, ANY) + (VMEM,) * (len(outs) + 1),
        scratch_shapes=scratch,
        compiler_params=pltpu.CompilerParams(
            collective_id=0, has_side_effects=True, vmem_limit_bytes=63 * 1024 * 1024
        ),
        cost_estimate=cost(total_rows * (chunks + 12) * width * width, 60 * 2**20),
        name="backward",
    )(pool, gains, cross_gains, *activations, *weights, *joining, *operands)


def flipped(array, axis, bit):
    return lax.ppermute(array, axis, [(i, i ^ (1 << bit)) for i in range(lax.axis_size(axis))])


def block_order(width, count):
    bits = count.bit_length() - 1
    block = width // count
    rows = jnp.arange(width)
    place = rows // block
    partner = jnp.zeros_like(place)
    for bit in range(bits):
        partner = partner | (((place >> (bits - 1 - bit)) & 1) << bit)
    source = (lax.axis_index("dp") ^ partner) * block + rows % block
    return (source[:, None] == jnp.arange(width)[None, :]).astype(BF16)


def ordered(order, values):
    return jnp.einsum("jd,rd->jr", order, values, preferred_element_type=F32).astype(BF16)


def summed(left_rows, grad_rows):
    count = lax.axis_size("dp")
    half = left_rows.shape[0] // 2
    send = jnp.dot(left_rows[half:], grad_rows, preferred_element_type=F32).astype(BF16)
    keep = jnp.dot(left_rows[:half], grad_rows, preferred_element_type=F32).astype(BF16)
    bits = count.bit_length() - 1
    for bit in range(bits):
        got = flipped(send, "dp", bit)
        if bit == bits - 1:
            return keep.astype(F32) + got.astype(F32)
        half = half // 2
        send = (keep[half:].astype(F32) + got[half:].astype(F32)).astype(BF16)
        keep = (keep[:half].astype(F32) + got[:half].astype(F32)).astype(BF16)


def summed_blocks(blocks):
    bits = lax.axis_size("dp").bit_length() - 1
    for bit in range(bits):
        half = blocks.shape[0] // 2
        blocks = blocks[:half] + flipped(blocks[half:], "dp", bit)
    return blocks[0]


def backward_plan(rows, half):
    wide = 2 * rows
    plan, results, outs = [], [], []

    def add(left, right, columns):
        outs.append(columns)
        for start in range(0, columns, rows):
            plan.append([(left, right, start, rows, 0)])
            results.append([(len(outs) - 1, start, 0, rows)])

    add(0, 1, wide)
    add(2, 3, wide)
    outs.extend([half, half])
    plan.append([(4, 5, 0, half, 0), (6, 7, 0, half, half)])
    results.append([(2, 0, 0, half), (3, 0, half, half)])
    outs.append(None)
    plan.append([(8, 9, 0, rows, 0)])
    results.append([(4, 0, 0, half), (4, 1, half, half)])
    add("branch", 10, 4 * rows)
    add(11, "gexp", 4 * rows)
    add(12, "gattn", rows)
    add(13, "grows", 3 * rows)
    return plan, results, outs


def finish_kernel(count, *refs):
    sources, loss_ref, vector_ref = refs[:count], refs[count], refs[count + 1]
    targets = refs[count + 2 : 2 * count + 2]
    loss_out, gains_ref, norms_ref, cross_gain_ref = refs[2 * count + 2 : 2 * count + 6]
    kept, (in_sems, out_sems) = refs[2 * count + 6 : 3 * count + 6], refs[3 * count + 6 :]
    arrivals = [pltpu.make_async_copy(a, b, in_sems.at[i]) for i, (a, b) in enumerate(zip(sources, kept))]
    departures = [pltpu.make_async_copy(a, b, out_sems.at[i]) for i, (a, b) in enumerate(zip(kept, targets))]
    begin(arrivals)
    block = gains_ref.shape[1]
    loss_out[0, 0] = loss_ref[0, 0]
    gains_ref[...] = vector_ref[0:2, 0:block]
    norms_ref[...] = vector_ref[2:3, 0:block]
    cross_gain_ref[...] = vector_ref[3:4, 0:block]
    for arrival, departure in zip(arrivals, departures):
        arrival.wait()
        departure.start()
    finish(departures)


def finished(arrays, loss, vector, block):
    small = [shape((1, 1), F32), shape((2, block), F32), shape((1, block), F32), shape((1, block), F32)]
    count = len(arrays)
    return pl.pallas_call(
        functools.partial(finish_kernel, count),
        out_shape=tuple(shape(a.shape, a.dtype) for a in arrays) + tuple(small),
        in_specs=[ANY] * count + [SMEM, VMEM],
        out_specs=(ANY,) * count + (SMEM, VMEM, VMEM, VMEM),
        scratch_shapes=[pltpu.VMEM(a.shape, a.dtype) for a in arrays] + [pltpu.SemaphoreType.DMA((count,))] * 2,
        compiler_params=limits(),
        name="finish",
    )(*arrays, loss, vector)


def shards(
    patch_tokens,
    grid_coords,
    has_radar,
    enc_gains,
    enc_project,
    enc_mixer,
    enc_expand,
    enc_reduce,
    cross_norms,
    cross_gain,
    cross_query,
    cross_keyval,
    cross_mixer,
    cross_expand,
    cross_reduce,
    enc_cotangent,
    joined_cotangent,
):
    item_count, patches, model_width = patch_tokens.shape[1:]
    images = range(item_count)
    dp_size = lax.axis_size("dp")
    weights = (enc_project[0], enc_mixer[0], enc_expand[0], enc_reduce[0])
    cross_weights = (cross_query, cross_keyval, cross_mixer, cross_expand, cross_reduce)

    (encoded, normed, rows, probs, mixed, resid, normed_two, hidden, slope,
     part, query_in, keyval_in, cnormed, cmixed, chidden, branch, cgexp, cgattn, gq, gkv,
     cresid, joining, early, cross_gains, loss, pool_grad) = forward(
        patch_tokens[0], grid_coords, enc_gains[0], cross_norms, cross_gain, has_radar,
        joined_cotangent, weights, cross_weights, dp_size,
    )

    block = model_width // dp_size

    def flat(values):
        return values.reshape(item_count * patches, *values.shape[2:])

    weight_operands = [
        flat(v)
        for v in (
            branch, chidden, cnormed, cgexp, query_in, gq, cgattn, cmixed, keyval_in, gkv, hidden, normed_two, mixed, normed
        )
    ]
    if sums_here(model_width, dp_size):
        plan, places, outs = backward_plan(model_width, model_width // 2)
        dims = [(2, block, model_width // 2) if columns is None else (block, columns) for columns in outs]
        activations = [flat(v) for v in (part, enc_cotangent[0], patch_tokens[0], resid, slope, rows)] + [probs]
        results = backward(
            pool_grad, enc_gains[0], cross_gains, activations, weights, (has_radar, flat(cresid), flat(joining), early), weight_operands,
            plan, places, dims, {4: 2, 9: 6, 14: 10},
            dp_size,
        )
        joined_tokens, vector_sum = results[0].reshape(encoded.shape), results[-1]
        results = results[1:-1]
    else:
        back = [
            encode_back(
                enc_cotangent[0, n], part[n], pool_grad[n : n + 1], enc_gains[0], patch_tokens[0, n],
                resid[n], slope[n], rows[n], probs[n], *weights,
            )
            for n in images
        ]
        patch_grad = jnp.concatenate([one[0] for one in back])
        both = joining.astype(F32) + flipped(joining, "mod", 0).astype(F32)
        joined_tokens = (has_radar.astype(F32)[:, None, None] * (cresid + both)).astype(BF16)
        grads = [jnp.concatenate([one[place] for one in back]) for place in range(1, 5)]
        order = block_order(model_width, dp_size)
        pairs = [(weight_operands[2 * n], weight_operands[2 * n + 1]) for n in range(5)]
        pairs += [(grads[0], weight_operands[10])]
        pairs += [(weight_operands[11 + n], grads[1 + n]) for n in range(3)]
        results = [patch_grad] + [summed(ordered(order, left), right) for left, right in pairs]
        results[5] = jnp.stack([results[5][:, : model_width // 2], results[5][:, model_width // 2 :]])
        vectors = jnp.concatenate([back[0][5] + back[1][5], cross_gains])
        blocks = jnp.moveaxis(vectors.reshape(4, dp_size, block), 1, 0)
        wanted = jnp.dot(order[::block, ::block].astype(F32), blocks.reshape(dp_size, -1), precision=lax.Precision.HIGHEST)
        vector_sum = summed_blocks(wanted.reshape(blocks.shape))
        vector_sum = jnp.pad(vector_sum, ((0, 4), (0, 128 - block)))
    (encoded, joined_tokens, patch_grad, creduce_sum, cexpand_sum, query_sum, cmixer_sum, keyval_sum, reduce_sum, expand_sum,
     mixer_sum, project_sum, loss, gains_sum, norms_sum, cross_gain_sum) = finished(
        [encoded, joined_tokens, *results], loss, vector_sum, block
    )
    return (
        encoded[None],
        joined_tokens,
        loss.reshape(()),
        patch_grad.reshape(patch_tokens.shape),
        gains_sum[None],
        project_sum[None],
        mixer_sum[None],
        expand_sum[None],
        reduce_sum.T[None],
        norms_sum,
        cross_gain_sum.reshape(block),
        query_sum,
        keyval_sum,
        cmixer_sum.T,
        cexpand_sum,
        creduce_sum.T,
    )


def solution(mesh):
    placed = (
        P("mod", "dp", None, None),
        P("dp", None, None),
        P("dp"),
        P("mod", None, None),
        P("mod", None, None),
        P("mod", None, None),
        P("mod", None, None),
        P("mod", None, None),
        P(),
        P(),
        P(None, "mod"),
        P(None, None, "mod"),
        P("mod", None),
        P(None, "mod"),
        P("mod", None),
        P("mod", "dp", None, None),
        P("dp", None, None),
    )
    return jax.shard_map(
        shards,
        mesh=mesh,
        in_specs=placed,
        out_specs=(
            P("mod", "dp", None, None),
            P("dp", None, None),
            P(),
            P("mod", "dp", None, None),
            P("mod", None, "dp"),
            P("mod", "dp", None),
            P("mod", "dp", None),
            P("mod", "dp", None),
            P("mod", None, "dp"),
            P("mod", "dp"),
            P("dp"),
            P("dp", "mod"),
            P(None, "dp", "mod"),
            P("mod", "dp"),
            P("dp", "mod"),
            P("mod", "dp"),
        ),
        check_vma=False,
    )
```
